32 devices in a mesh: ep: 8 (over z, y), tp: 4 (over x, core).
Axes of the slice: x: 2, y: 2, z: 4, core: 2. Of those that a mesh axis runs over, the one named last changes fastest.
Arguments:
- queries: bfloat16 [512, 2048], P('ep', 'tp'), may hold values from -1024 to 1024
- new_keys: bfloat16 [512, 512], P('ep', 'tp'), may hold values from -6 to 6
- new_values: bfloat16 [512, 512], P('ep', 'tp'), may hold values from -5 to 5
- key_cache: bfloat16 [8, 512, 512], P('ep', None, 'tp'), may hold values from -5 to 5
- value_cache: bfloat16 [8, 512, 512], P('ep', None, 'tp'), may hold values from -5 to 5
- cache_lengths: int32 [8], P('ep'), may hold values from 1 to 512, 2048 in all
- request_order: int32 [8], replicated, may hold values from 0 to 7, each once
- residual: bfloat16 [512, 2048], P('ep', 'tp'), may hold values from -6 to 6
- out_weight: bfloat16 [2048, 2048], P('tp'), may hold values from -0.125 to 0.125
- norm_gain: float32 [2048], replicated, may hold values from 0.1 to 1.9
- route_experts: int32 [512, 2], P('ep'), may hold values from 0 to 7, all different within a row; in each aligned block of 64 rows (0 to 63, 64 to 127, ...) at most 32 rows name the same one
- route_weights: float32 [512, 2], P('ep'), may hold values from 0.1 to 1
- expert_gate: bfloat16 [8, 2048, 768], P('ep', None, 'tp'), may hold values from -0.125 to 0.125
- expert_up: bfloat16 [8, 2048, 768], P('ep', None, 'tp'), may hold values from -0.125 to 0.125
- expert_down: bfloat16 [8, 768, 2048], P('ep', None, 'tp'), may hold values from -0.21875 to 0.21875
Outputs:
- output: bfloat16 [512, 2048], P('ep', 'tp')
The draws below stay inside these ranges and needn't reach their ends.
Inputs may be any that keep to these rules, and one draw needn't show every extreme that they name: `cache_lengths`: the longest cache holds exactly 512 rows in every draw. `request_order`: each request block appears once. `route_experts`: each row names 2 different experts; within each request's block of 64 rows no expert is named by more than 32 rows, a bound that some block reaches.
All inputs are finite; a program needn't handle non-finite values. No bound on the sum of `cache_lengths` on one device may be relied on, other than what follows from the above.
Results may differ from the reference program's by a relative error of at most 0.0057.
Values may be sent and summed in bfloat16 or wider, within the bound.
No kernel may reach another device: no remote copies, remote signals or barrier semaphores. Data moves between devices by JAX's collectives and lax.ppermute only.
A program may use at most 64 MiB of HBM per device.

```python
import math
import jax
import jax.numpy as jnp
import numpy as np
from jax import lax

D = 2048
HEAD = 128
QHEADS = 16
KVHEADS = 4
FF = 768
TOK_DEV = 64
CACHE = 512
REQS = 8
TOKENS = 512
EXPERTS = 8
TOP = 2
CAP = 32


def cached_keys_draw(key):
    folded = jax.random.fold_in(key, 7)
    dims_all = (REQS, CACHE, KVHEADS * HEAD)
    values = jnp.clip(jax.random.normal(folded, dims_all, jnp.float32), -5.0, 5.0)
    return values


def draw_key_cache(key, part):
    return cached_keys_draw(key).astype(jnp.bfloat16)


def draw_new_keys(key, part):
    drawn = jnp.clip(jax.random.normal(jax.random.fold_in(key, 11), (TOKENS, KVHEADS * HEAD), jnp.float32), -5.0, 5.0)
    return drawn.astype(jnp.bfloat16)


def draw_queries(key, part):
    drawn = jnp.clip(jax.random.normal(jax.random.fold_in(key, 13), (REQS, TOK_DEV, QHEADS, HEAD), jnp.float32), -5.0, 5.0)
    return drawn.reshape(TOKENS, QHEADS * HEAD).astype(jnp.bfloat16)


def level_of(rng, dims, shards, least, largest):
    def one(dim, parts):
        steps = jax.random.uniform(jax.random.fold_in(jax.random.fold_in(rng, 6), dim), (parts,), jnp.float32, least / len(shards), largest / len(shards))
        return jnp.repeat(jnp.exp(steps), dims[dim] // parts).reshape((-1,) + (1,) * (len(dims) - dim - 1))

    gain = one(*shards[0])
    for cut in shards[1:]:
        gain = gain * one(*cut)
    return gain


def profile(amount, total, limit, slope):
    weights = [(1 << 20) // math.isqrt(grade ** slope) + 1 for grade in range(2, amount + 1)]
    surplus, counts = total - limit - (amount - 1), [1] * (amount - 1)
    while surplus > 0:
        movable = [i for i in range(amount - 1) if counts[i] < limit]
        whole, budget = sum([weights[i] for i in movable]), surplus
        for i in movable:
            addition = min(limit - counts[i], max(1, budget * weights[i] // whole), surplus)
            counts[i] = counts[i] + addition
            surplus = surplus - addition
    return np.array([limit] + counts)


def ragged(stream_key, count, total, limit, skew):
    if count == 2:
        one = jax.random.randint(stream_key, (), max(1, total - limit), min(limit, total - 1) + 1)
        return jnp.stack([one, total - one])
    tallies = jnp.asarray(profile(count, total, limit, skew), jnp.int32)
    couples = (count - 1) // 2
    giver, sink = tallies[1:1 + 2 * couples:2], tallies[2:2 + 2 * couples:2]
    slack = jnp.minimum(giver - 1, limit - sink)
    passed = jax.random.randint(jax.random.fold_in(stream_key, 1), (couples,), 0, 1 << 20) % (slack + 1)
    tallies = tallies.at[1:1 + 2 * couples:2].set(giver - passed).at[2:2 + 2 * couples:2].set(sink + passed)
    return tallies[jax.random.permutation(jax.random.fold_in(stream_key, 2), count)]


def assign_block(rng, own, number, rows, count, top, reach, lean):
    order = jax.random.permutation(rng, count)
    heavy_load, usual = load_shares(count, rows * top, reach, lean, True), load_shares(count, rows * top, reach, lean, False)
    places = jnp.arange(count)

    def named(sizes, turn):
        used = int((sizes > 0).sum())
        fixed = max(1, used // 4)
        shifted = fixed + (places - fixed + turn * (used - fixed)) % max(1, count - fixed)
        return jnp.zeros((count,), jnp.int32).at[order[jnp.where(places < fixed, places, shifted)]].set(jnp.asarray(sizes, jnp.int32))

    sizes = jnp.where(number % 4 == 0, named(heavy_load, number // 4), named(usual, number - number // 4 - 1))
    mixed = jax.random.permutation(jax.random.fold_in(own, 3), count)
    giver, taker = mixed[0:count // 2 * 2:2], mixed[1:count // 2 * 2:2]
    room = jnp.minimum(sizes[giver] - 1, reach - sizes[taker]) // 2
    room = jnp.where((giver == order[0]) | (taker == order[0]) | (sizes[taker] == 0), 0, jnp.maximum(room, 0))
    shifted = jax.random.randint(jax.random.fold_in(own, 4), (count // 2,), 0, 1 << 20) % (room + 1)
    sizes = sizes.at[giver].add(-shifted).at[taker].add(shifted)
    members = jnp.searchsorted(jnp.cumsum(sizes), jnp.arange(rows * top), side="right").astype(jnp.int32)
    listing = members.reshape(top, rows).T
    listing = listing[jax.random.permutation(jax.random.fold_in(own, 1), rows)]
    turn = jax.random.randint(jax.random.fold_in(own, 2), (rows, 1), 0, top)
    return jnp.take_along_axis(listing, (jnp.arange(top)[None, :] + turn) % top, axis=1)


def load_shares(count, total, bound, slope, full):
    weights = [(1 << 20) // math.isqrt(grade ** slope) + 1 for grade in range(1, count + 1)]
    largest = bound if full else min(bound, max(-(-total // count), total * weights[0] // sum(weights)))
    least = 1 if total - largest >= count - 1 else 0
    holding, spare = [largest] + [least] * (count - 1), total - largest - least * (count - 1)
    while spare > 0:
        free = [i for i in range(1, count) if holding[i] < largest] or [i for i in range(1, count) if holding[i] < bound]
        mass, left = sum([weights[i] for i in free]), spare
        for i in free:
            extra = min(bound - holding[i], max(1, left * weights[i] // mass), spare)
            holding[i] = holding[i] + extra
            spare = spare - extra
    return np.array(holding)


def bell_draw(rng, extent, width, reach, shards=(), held_as=jnp.bfloat16):
    level = level_of(rng, extent, shards, -0.22, 0.18) if shards else 1.0
    values = jax.random.normal(rng, extent, jnp.float32) * width * level
    return jnp.minimum(jnp.maximum(values, -reach), reach).astype(held_as)


def setup_inputs(seed: int = 0) -> dict:
    splits = jax.random.split(jax.random.key(seed), 16)
    queries = draw_queries(jax.random.fold_in(splits[15], 71), 0)
    new_keys = draw_new_keys(jax.random.fold_in(splits[15], 71), 0)
    new_values = bell_draw(splits[2], (TOKENS, KVHEADS * HEAD), 1.0, 5.0, ((0, 8), (1, 4)))
    key_cache = draw_key_cache(jax.random.fold_in(splits[15], 71), 0)
    value_cache = bell_draw(splits[4], (REQS, CACHE, KVHEADS * HEAD), 1.0, 5.0, ((0, 8), (2, 4)))
    cache_lengths = ragged(splits[5], REQS, REQS * CACHE // 2, CACHE, 2).astype(jnp.int32)
    request_order = jax.random.permutation(splits[6], REQS).astype(jnp.int32)
    residual = bell_draw(splits[7], (TOKENS, D), 1.0, 6.0, ((0, 8), (1, 4)))
    out_weight = bell_draw(splits[8], (QHEADS * HEAD, D), (QHEADS * HEAD) ** -0.5, 0.125, ((0, 4),))
    norm_gain = jnp.clip(1.0 + 0.18 * jax.random.normal(splits[9], (D,), jnp.float32), 0.1, 1.9)
    route_experts_keys = jax.random.split(jax.random.fold_in(splits[10], 1), TOKENS // TOK_DEV)
    route_experts_turns = jax.random.permutation(jax.random.fold_in(splits[10], 3), TOKENS // TOK_DEV)
    route_experts = jax.vmap(lambda own, number: assign_block(jax.random.fold_in(splits[10], 2), own, number, TOK_DEV, EXPERTS, TOP, CAP, 2))(route_experts_keys, route_experts_turns).reshape((TOKENS, TOP))
    route_weights = jnp.clip(jnp.exp(math.log(1.0) - 2.3025851 * jax.random.uniform(splits[11], (TOKENS, TOP), jnp.float32) ** level_of(splits[11], (TOKENS, TOP), ((0, 8),), -0.2, 0.2)), 0.1, 1.0)
    expert_gate = bell_draw(splits[12], (EXPERTS, D, FF), D ** -0.5, 0.125, ((0, 8), (2, 4)))
    expert_up = bell_draw(splits[13], (EXPERTS, D, FF), D ** -0.5, 0.125, ((0, 8), (2, 4)))
    expert_down = bell_draw(splits[14], (EXPERTS, FF, D), FF ** -0.5, 0.21875, ((0, 8), (2, 4)))
    return {"queries": queries, "new_keys": new_keys, "new_values": new_values, "key_cache": key_cache, "value_cache": value_cache, "cache_lengths": cache_lengths, "request_order": request_order, "residual": residual, "out_weight": out_weight, "norm_gain": norm_gain, "route_experts": route_experts, "route_weights": route_weights, "expert_gate": expert_gate, "expert_up": expert_up, "expert_down": expert_down}


def attend_request(operands):
    query_rows, key_rows, value_rows, cached_keys, cached_values, length = operands
    group_size = QHEADS // KVHEADS
    query_view = query_rows.astype(jnp.float32).reshape(TOK_DEV, KVHEADS, group_size, HEAD)
    all_keys = jnp.concatenate([cached_keys, key_rows], axis=0).astype(jnp.float32).reshape(CACHE + TOK_DEV, KVHEADS, HEAD)
    all_values = jnp.concatenate([cached_values, value_rows], axis=0).astype(jnp.float32).reshape(CACHE + TOK_DEV, KVHEADS, HEAD)
    scores = jnp.einsum('tghd,kgd->tghk', query_view, all_keys) / math.sqrt(HEAD)
    position = jnp.arange(CACHE + TOK_DEV, dtype=jnp.int32)
    current = jnp.arange(TOK_DEV, dtype=jnp.int32)
    visible = jnp.where(position[None, :] < CACHE, position[None, :] < length, position[None, :] - CACHE <= current[:, None])
    visible = visible[:, None, None, :]
    highest = lax.optimization_barrier(jnp.max(jnp.where(visible, scores, -1e+30), axis=-1, keepdims=True))
    raised = jnp.exp(jnp.where(visible, scores - highest, -1e+30))
    totals = lax.optimization_barrier(jnp.sum(raised, axis=-1, keepdims=True))
    rounded = lax.optimization_barrier(raised.astype(jnp.bfloat16)).astype(jnp.float32)
    context = jnp.einsum('tghk,kgd->tghd', rounded, all_values) / totals
    return context.astype(jnp.bfloat16).reshape(TOK_DEV, QHEADS * HEAD)

def reference(queries, new_keys, new_values, key_cache, value_cache, cache_lengths, request_order, residual, out_weight, norm_gain, route_experts, route_weights, expert_gate, expert_up, expert_down):
    contexts = lax.map(attend_request, (queries.reshape(REQS, TOK_DEV, -1), new_keys.reshape(REQS, TOK_DEV, -1), new_values.reshape(REQS, TOK_DEV, -1), key_cache, value_cache, cache_lengths))
    context = contexts.reshape(TOKENS, QHEADS * HEAD)
    attended = jnp.dot(context, out_weight, preferred_element_type=jnp.float32)
    hidden_state = (residual.astype(jnp.float32) + attended).astype(jnp.bfloat16)
    widened = hidden_state.astype(jnp.float32)
    mean_square = lax.optimization_barrier(jnp.mean(widened * widened, axis=-1, keepdims=True))
    normed = (widened * lax.rsqrt(mean_square + 1e-06) * norm_gain).astype(jnp.bfloat16)
    mixing = (route_weights / lax.optimization_barrier(jnp.sum(route_weights, axis=-1, keepdims=True))).astype(jnp.bfloat16)
    flat_routes = route_experts.reshape(REQS, TOK_DEV * TOP)
    onehot = (flat_routes[:, :, None] == jnp.arange(EXPERTS, dtype=jnp.int32)[None, None, :]).astype(jnp.int32)
    ranking = lax.optimization_barrier(jnp.sum(jnp.cumsum(onehot, axis=1) * onehot, axis=2)) - 1
    request_ids = jnp.broadcast_to(jnp.arange(REQS, dtype=jnp.int32)[:, None], flat_routes.shape)
    token_ids = request_ids * TOK_DEV + jnp.arange(TOK_DEV * TOP, dtype=jnp.int32)[None, :] // TOP
    table_tokens = jnp.full((EXPERTS, REQS, CAP), -1, jnp.int32).at[flat_routes, request_ids, ranking].set(token_ids)
    table_mix = jnp.zeros((EXPERTS, REQS, CAP), jnp.bfloat16).at[flat_routes, request_ids, ranking].set(mixing.reshape(REQS, TOK_DEV * TOP))

    def expert_step(running, operands):
        weights_gate, weights_up, weights_down, token_list, mix_list = operands
        present = token_list >= 0
        safe_ids = jnp.where(present, token_list, 0)
        inputs = normed[safe_ids]
        gate_value = jnp.dot(inputs, weights_gate, preferred_element_type=jnp.float32)
        up_value = jnp.dot(inputs, weights_up, preferred_element_type=jnp.float32)
        activation = (jax.nn.silu(gate_value) * up_value).astype(jnp.bfloat16)
        expert_out = jnp.dot(activation, weights_down, preferred_element_type=jnp.float32)
        contribution = (mix_list.astype(jnp.float32)[:, None] * (widened[safe_ids] + expert_out)).astype(jnp.bfloat16)
        contribution = lax.optimization_barrier(contribution).astype(jnp.float32)
        contribution = jnp.where(present[:, None], contribution, 0.0)
        return (running.at[safe_ids].add(contribution), None)
    initial = jnp.zeros((TOKENS, D), jnp.float32)
    summed, _ = lax.scan(expert_step, initial, (expert_gate, expert_up, expert_down, table_tokens.reshape(EXPERTS, REQS * CAP), table_mix.reshape(EXPERTS, REQS * CAP)))
    placed = jnp.zeros((REQS, TOK_DEV, D), jnp.float32).at[request_order].set(summed.reshape(REQS, TOK_DEV, D))
    return placed.reshape(TOKENS, D).astype(jnp.bfloat16)
```

```python
import math

import jax
import jax.numpy as jnp
from jax import lax
from jax.sharding import PartitionSpec as P

HEAD = 128
QHEADS = 16
KVHEADS = 4
META = 128


def attention_block(queries, new_keys, new_values, key_cache, value_cache, cache_lengths, kv_local):
    tokens_here = queries.shape[0]
    cached = key_cache.shape[1]
    group_size = QHEADS // KVHEADS
    query_view = queries.reshape(tokens_here, kv_local, group_size, HEAD)
    all_keys = jnp.concatenate([key_cache[0], new_keys], axis=0).reshape(
        cached + tokens_here, kv_local, HEAD
    )
    all_values = jnp.concatenate([value_cache[0], new_values], axis=0).reshape(
        cached + tokens_here, kv_local, HEAD
    )
    scores = jnp.einsum(
        "tghd,kgd->tghk", query_view, all_keys, preferred_element_type=jnp.float32
    ) / math.sqrt(HEAD)
    position = jnp.arange(cached + tokens_here, dtype=jnp.int32)
    current = jnp.arange(tokens_here, dtype=jnp.int32)
    visible = jnp.where(
        position[None, :] < cached,
        position[None, :] < cache_lengths[0],
        position[None, :] - cached <= current[:, None],
    )
    visible = visible[:, None, None, :]
    highest = jnp.max(jnp.where(visible, scores, -1e30), axis=-1, keepdims=True)
    raised = jnp.exp(jnp.where(visible, scores - highest, -1e30))
    totals = jnp.sum(raised, axis=-1, keepdims=True)
    weights = raised.astype(jnp.bfloat16)
    context = (
        jnp.einsum("tghk,kgd->tghd", weights, all_values, preferred_element_type=jnp.float32)
        / totals
    )
    return context.astype(jnp.bfloat16).reshape(tokens_here, -1)


def shards(
    queries,
    new_keys,
    new_values,
    key_cache,
    value_cache,
    cache_lengths,
    request_order,
    residual,
    out_weight,
    norm_gain,
    route_experts,
    route_weights,
    expert_gate,
    expert_up,
    expert_down,
):
    tp_count = lax.axis_size("tp")
    ep_count = lax.axis_size("ep")
    kv_local = KVHEADS // tp_count
    me_ep = lax.axis_index("ep")
    me_tp = lax.axis_index("tp")
    half, core = me_tp // 2, me_tp % 2
    bf = jnp.bfloat16

    def swap_core(x):
        return lax.ppermute(x, "tp", [(i, i ^ 1) for i in range(tp_count)])

    def swap_half(x):
        return lax.ppermute(x, "tp", [(i, i ^ 2) for i in range(tp_count)])

    tokens_here, top_count = route_experts.shape
    experts_local = expert_gate.shape[0]
    expert_count = experts_local * ep_count
    capacity = 2 * tokens_here * top_count // expert_count
    rows_each = experts_local * capacity
    peers = ep_count // 2
    width = residual.shape[1]
    full = width * tp_count

    context = attention_block(
        queries, new_keys, new_values, key_cache, value_cache, cache_lengths, kv_local
    )
    terms = jnp.dot(context, out_weight, preferred_element_type=jnp.float32)
    terms = terms.reshape(tokens_here, 2, 2, width)
    first, second = terms[:, :, 0], terms[:, :, 1]
    keep = jnp.where(core == 0, first, second)
    give = jnp.where(core == 0, second, first).astype(bf)
    keep = keep + swap_core(give).astype(jnp.float32)
    mine = (jnp.arange(2) == half)[None, :, None]
    keep = keep + jnp.where(mine, residual.astype(jnp.float32)[:, None, :], 0.0)
    hidden_part = (keep + swap_half(keep.astype(bf)).astype(jnp.float32)).astype(bf)
    hidden_other = swap_core(hidden_part)
    hidden = jnp.stack(
        [
            jnp.where(core == 0, hidden_part, hidden_other),
            jnp.where(core == 0, hidden_other, hidden_part),
        ],
        axis=2,
    ).reshape(tokens_here, full)

    offsets = 2 * jnp.arange(peers, dtype=jnp.int32) + core
    peer = jnp.bitwise_xor(me_ep, offsets)
    wanted = (
        peer[:, None] * experts_local + jnp.arange(experts_local, dtype=jnp.int32)[None, :]
    ).reshape(-1)
    named = jnp.any(route_experts[None] == wanted[:, None, None], axis=2)
    token_range = jnp.arange(tokens_here, dtype=jnp.int32)
    before = (token_range[:, None] < token_range[None, :]).astype(bf)
    rank = jnp.dot(named.astype(bf), before, preferred_element_type=jnp.float32).astype(jnp.int32)
    slot_range = jnp.arange(capacity, dtype=jnp.int32)
    pick = (
        (rank[:, None, :] == slot_range[None, :, None]) & named[:, None, :]
    ).astype(bf).reshape(peers * rows_each, tokens_here)
    mixing = (route_weights / jnp.sum(route_weights, axis=1, keepdims=True)).astype(bf)
    meta = jnp.concatenate(
        [(token_range + 1).astype(bf)[:, None], mixing, route_experts.astype(bf)], axis=1
    )
    meta = jnp.pad(meta, ((0, 0), (0, META - meta.shape[1])))
    source = jnp.concatenate([hidden, meta], axis=1)
    send = jnp.dot(pick, source, preferred_element_type=jnp.float32).astype(bf)
    send = send.reshape(peers, rows_each, full + META)

    def route(k):
        return [
            (e * tp_count + t, (e ^ (2 * k + t % 2)) * tp_count + t)
            for e in range(ep_count)
            for t in range(tp_count)
        ]

    got = [lax.ppermute(send[k], ("ep", "tp"), route(k)) for k in range(peers)]
    own = jnp.stack(got)
    other = jnp.stack([swap_core(g) for g in got])
    rows = jnp.concatenate(
        [jnp.where(core == 0, own, other), jnp.where(core == 0, other, own)], axis=0
    )
    rows = rows.reshape(ep_count, experts_local, capacity, full + META)
    tags = rows[..., full:].astype(jnp.float32)
    token = tags[..., 0]
    expert_ids = (me_ep * experts_local + jnp.arange(experts_local)).astype(jnp.float32)
    mix = jnp.sum(
        jnp.where(
            tags[..., 1 + top_count : 1 + 2 * top_count] == expert_ids[None, :, None, None],
            tags[..., 1 : 1 + top_count],
            0.0,
        ),
        axis=-1,
    )
    rows = rows[..., :full].astype(jnp.float32)
    factor = lax.rsqrt(jnp.mean(rows * rows, axis=-1, keepdims=True) + 1e-06)
    normed = (rows * factor * norm_gain).astype(bf)
    gate = jnp.einsum("secd,edf->secf", normed, expert_gate, preferred_element_type=jnp.float32)
    up = jnp.einsum("secd,edf->secf", normed, expert_up, preferred_element_type=jnp.float32)
    activation = (jax.nn.silu(gate) * up).astype(bf)
    activation = lax.all_gather(activation, "tp", axis=3, tiled=True)
    expert_out = jnp.einsum(
        "secf,efd->secd", activation, expert_down, preferred_element_type=jnp.float32
    )
    own_rows = lax.dynamic_slice_in_dim(rows, me_tp * width, width, axis=3)
    contribution = (mix[..., None] * (own_rows + expert_out)).astype(bf)
    result = jnp.concatenate(
        [contribution, jnp.broadcast_to(token[..., None].astype(bf), token.shape + (META,))],
        axis=-1,
    ).reshape(ep_count, rows_each, width + META)

    requests = jnp.arange(ep_count, dtype=jnp.int32)
    offset = jnp.bitwise_xor(requests, me_ep)
    place = offset // 2 + (offset % 2) * peers
    back = jnp.zeros((ep_count,), jnp.int32)
    back = jnp.sum(
        jnp.where(request_order[None, :] == requests[:, None], place[None, :], 0), axis=1
    )
    came = lax.all_to_all(
        jnp.take(result, back, axis=0), "ep", split_axis=0, concat_axis=0, tiled=True
    ).reshape(ep_count * rows_each, width + META)
    selector = (came[:, width].astype(jnp.int32)[None, :] == token_range[:, None] + 1).astype(bf)
    return jnp.dot(selector, came[:, :width], preferred_element_type=jnp.float32).astype(bf)


def solution(mesh):
    return jax.shard_map(
        shards,
        mesh=mesh,
        in_specs=(
            P("ep", "tp"),
            P("ep", "tp"),
            P("ep", "tp"),
            P("ep", None, "tp"),
            P("ep", None, "tp"),
            P("ep"),
            P(),
            P("ep", "tp"),
            P("tp", None),
            P(),
            P("ep", None),
            P("ep", None),
            P("ep", None, "tp"),
            P("ep", None, "tp"),
            P("ep", None, "tp"),
        ),
        out_specs=P("ep", "tp"),
        check_vma=False,
    )
```

```python
import functools
import math

import jax
import jax.numpy as jnp
from jax import lax
from jax.experimental import pallas as pl
from jax.experimental.pallas import tpu as pltpu
from jax.sharding import PartitionSpec as P

HEAD = 128
QHEADS = 16
KVHEADS = 4
LANES = 128
TAGS = 16
VMEM_LIMIT = 24 * 1024 * 1024

BF16 = jnp.bfloat16
F32 = jnp.float32


def vmem():
    return pl.BlockSpec(memory_space=pltpu.VMEM)


def params():
    return pltpu.CompilerParams(vmem_limit_bytes=VMEM_LIMIT)


def dot(a, b):
    return jnp.dot(a, b, preferred_element_type=F32)


def dot_t(a, b):
    return lax.dot_general(a, b, (((1,), (1,)), ((), ())), preferred_element_type=F32)


def attend_kernel(
    kv_local,
    length_ref,
    query_ref,
    new_key_ref,
    new_value_ref,
    key_ref,
    value_ref,
    weight_hbm,
    keep_ref,
    give_ref,
    weight_ref,
    sems,
):
    core = lax.axis_index("tp") % 2
    width = weight_ref.shape[2]
    copies = []
    for i, block in enumerate((1 - core, 3 - core, core, core + 2)):
        start = pl.multiple_of(block * width, width)
        copy = pltpu.make_async_copy(
            weight_hbm.at[:, pl.ds(start, width)], weight_ref.at[i], sems.at[i]
        )
        copy.start()
        copies.append(copy)
    tokens = query_ref.shape[0]
    cached = key_ref.shape[0]
    group = QHEADS // KVHEADS
    length = length_ref[0]
    scale = 1.0 / math.sqrt(HEAD)
    pieces = []
    for g in range(kv_local):
        columns = slice(g * HEAD, (g + 1) * HEAD)
        rows = jnp.concatenate(
            [
                query_ref[:, (g * group + i) * HEAD : (g * group + i + 1) * HEAD]
                for i in range(group)
            ],
            axis=0,
        )
        old = dot_t(rows, key_ref[:, columns]) * scale
        new = dot_t(rows, new_key_ref[:, columns]) * scale
        position = lax.broadcasted_iota(jnp.int32, old.shape, 1)
        old = jnp.where(position < length, old, -1e30)
        current = lax.broadcasted_iota(jnp.int32, new.shape, 0) % tokens
        position = lax.broadcasted_iota(jnp.int32, new.shape, 1)
        new = jnp.where(position <= current, new, -1e30)
        highest = jnp.maximum(
            jnp.max(old, axis=1, keepdims=True), jnp.max(new, axis=1, keepdims=True)
        )
        old = jnp.exp(old - highest)
        new = jnp.exp(new - highest)
        totals = jnp.sum(old, axis=1, keepdims=True) + jnp.sum(new, axis=1, keepdims=True)
        mixed = dot(old.astype(BF16), value_ref[:, columns]) + dot(
            new.astype(BF16), new_value_ref[:, columns]
        )
        mixed = (mixed / totals).astype(BF16)
        pieces += [mixed[i * tokens : (i + 1) * tokens] for i in range(group)]
    context = jnp.concatenate(pieces, axis=1)
    for i in range(4):
        copies[i].wait()
        part = dot(context, weight_ref[i])
        columns = slice((i % 2) * width, (i % 2 + 1) * width)
        if i < 2:
            give_ref[:, columns] = part.astype(BF16)
        else:
            keep_ref[:, columns] = part


def gather_kernel(peers, part_ref, other_ref, pick_ref, tags_ref, *send_refs):
    core = lax.axis_index("tp") % 2
    rows_each = pick_ref.shape[0] // peers
    pick = pick_ref[...]
    width = part_ref.shape[1] // 2
    blocks = width // LANES
    for source, parity in ((part_ref, core), (other_ref, 1 - core)):
        for half in range(2):
            rows = dot(pick, source[:, half * width : (half + 1) * width]).astype(BF16)
            base = (2 * half + parity) * (blocks * rows_each)
            for k in range(peers):
                for j in range(blocks):
                    start = pl.multiple_of(base + j * rows_each, rows_each)
                    send_refs[k][pl.ds(start, rows_each), :] = rows[
                        k * rows_each : (k + 1) * rows_each, j * LANES : (j + 1) * LANES
                    ]
    for k in range(peers):
        send_refs[k][4 * blocks * rows_each :, :] = tags_ref[k]


def hidden_units_kernel(
    peers, rows_each, gain_ref, gate_ref, gate_pair_ref, up_ref, up_pair_ref, *refs
):
    got = refs[:peers]
    act_ref, side_ref = refs[peers:]
    tp = lax.axis_index("tp")
    core = tp % 2
    blocks = gain_ref.shape[0]
    per_device = blocks // 4
    parts = [
        jnp.concatenate(
            [ref[j * rows_each : (j + 1) * rows_each, :] for ref in got], axis=0
        ).astype(F32)
        for j in range(blocks)
    ]
    squares = parts[0] * parts[0]
    for part in parts[1:]:
        squares = squares + part * part
    mean = jnp.sum(squares, axis=1, keepdims=True) * (1.0 / (blocks * LANES))
    factor = lax.rsqrt(mean + 1e-06)
    normed = jnp.concatenate(
        [(parts[j] * factor * gain_ref[j : j + 1, :]).astype(BF16) for j in range(blocks)], axis=1
    )

    def units(gate, up):
        value = dot(normed, gate[...])
        return value / (1.0 + jnp.exp(-value)) * dot(normed, up[...])

    own = units(gate_ref, up_ref)
    pair = units(gate_pair_ref, up_pair_ref)
    low = jnp.where(core == 0, own, pair)
    high = jnp.where(core == 0, pair, own)
    act_ref[...] = jnp.concatenate([low, high], axis=1).astype(BF16)
    tall = per_device * rows_each
    start = pl.multiple_of((tp + 1 - 2 * core) * tall, tall)
    for k in range(peers):
        side_ref[k, :tall, :] = got[k][pl.ds(start, tall), :]
        side_ref[k, tall:, :] = got[k][blocks * rows_each :, :]


def down_kernel(
    peers,
    rows_each,
    order_ref,
    act_ref,
    act_half_ref,
    act_core_ref,
    act_both_ref,
    down_ref,
    side_ref,
    *refs,
):
    got = refs[:peers]
    out_ref = refs[peers]
    tp = lax.axis_index("tp")
    me = lax.axis_index("ep")
    half, core = tp // 2, tp % 2
    units = act_ref.shape[1]
    blocks = down_ref.shape[1] // LANES
    tall = blocks * rows_each
    here = down_ref[pl.ds(pl.multiple_of(half * units, units), units), :]
    there = down_ref[pl.ds(pl.multiple_of((1 - half) * units, units), units), :]
    diagonal = lax.broadcasted_iota(jnp.int32, (rows_each, LANES), 0) == lax.broadcasted_iota(
        jnp.int32, (rows_each, LANES), 1
    )
    start = pl.multiple_of(tp * tall, tall)
    for group in range(2):
        near, far = ((act_ref, act_half_ref), (act_core_ref, act_both_ref))[group]
        result = dot(near[...], here) + dot(far[...], there)
        for k in range(peers):
            request = jnp.bitwise_xor(me, 2 * k + (core if group == 0 else 1 - core))
            place = order_ref[request]
            if group == 0:
                rows = got[k][pl.ds(start, tall), :]
                tags = got[k][4 * tall :, :]
            else:
                rows = side_ref[k, :tall, :]
                tags = side_ref[k, tall:, :]
            mix = jnp.sum(
                jnp.where(diagonal, tags.astype(F32)[1:2, :], 0.0), axis=1, keepdims=True
            )
            for j in range(blocks):
                piece = slice(j * rows_each, (j + 1) * rows_each)
                value = rows[piece].astype(F32) + result[
                    k * rows_each : (k + 1) * rows_each, j * LANES : (j + 1) * LANES
                ]
                out_ref[place, piece, :] = (mix * value).astype(BF16)
            out_ref[place, tall:, :] = tags


def combine_kernel(rows_each, came_ref, out_ref):
    tokens, width = out_ref.shape
    blocks = width // LANES
    tall = blocks * rows_each
    number = lax.broadcasted_iota(jnp.int32, (tokens, rows_each), 0).astype(F32) + 1.0
    total = jnp.zeros((tokens, width), F32)
    for e in range(came_ref.shape[0]):
        tags = came_ref[e, tall:, :].astype(F32)
        chosen = (number == tags[0:1, :rows_each]).astype(BF16)
        rows = jnp.concatenate(
            [came_ref[e, j * rows_each : (j + 1) * rows_each, :] for j in range(blocks)], axis=1
        )
        total = total + dot(chosen, rows)
    out_ref[...] = total.astype(BF16)


def shards(
    queries,
    new_keys,
    new_values,
    key_cache,
    value_cache,
    cache_lengths,
    request_order,
    residual,
    out_weight,
    norm_gain,
    route_experts,
    route_weights,
    expert_gate,
    expert_up,
    expert_down,
):
    tp_count = lax.axis_size("tp")
    ep_count = lax.axis_size("ep")
    kv_local = KVHEADS // tp_count
    me_ep = lax.axis_index("ep")
    me_tp = lax.axis_index("tp")
    half, core = me_tp // 2, me_tp % 2

    def swap_core(x):
        return lax.ppermute(x, "tp", [(i, i ^ 1) for i in range(tp_count)])

    def swap_half(x):
        return lax.ppermute(x, "tp", [(i, i ^ 2) for i in range(tp_count)])

    gate, up, down = expert_gate[0], expert_up[0], expert_down[0]
    gate_pair, up_pair = swap_core(gate), swap_core(up)

    tokens, top = route_experts.shape
    capacity = 2 * tokens * top // ep_count
    rows_each = -(-capacity // 16) * 16
    peers = ep_count // 2
    width = residual.shape[1]
    blocks = width // LANES
    tall = blocks * rows_each
    units = 2 * gate.shape[1]
    shape = jax.ShapeDtypeStruct

    keep, give = pl.pallas_call(
        functools.partial(attend_kernel, kv_local),
        out_shape=(shape((tokens, 2 * width), F32), shape((tokens, 2 * width), BF16)),
        in_specs=[pl.BlockSpec(memory_space=pltpu.SMEM)]
        + [vmem()] * 5
        + [pl.BlockSpec(memory_space=pl.ANY)],
        out_specs=(vmem(), vmem()),
        scratch_shapes=[
            pltpu.VMEM((4, out_weight.shape[0], width), BF16),
            pltpu.SemaphoreType.DMA((4,)),
        ],
        compiler_params=params(),
        name="attend",
    )(
        cache_lengths,
        queries,
        new_keys,
        new_values,
        key_cache[0],
        value_cache[0],
        out_weight,
    )

    peer = jnp.bitwise_xor(me_ep, 2 * jnp.arange(peers, dtype=jnp.int32) + core)
    matches = route_experts[None] == peer[:, None, None]
    named = jnp.any(matches, axis=2)
    token_range = jnp.arange(tokens, dtype=jnp.int32)
    before = (token_range[:, None] < token_range[None, :]).astype(BF16)
    rank = dot(named.astype(BF16), before).astype(jnp.int32)
    slots = jnp.arange(rows_each, dtype=jnp.int32)
    pick = (rank[:, None, :] == slots[None, :, None]) & named[:, None, :]
    mixing = (route_weights / jnp.sum(route_weights, axis=1, keepdims=True)).astype(BF16)
    mix_of = jnp.sum(jnp.where(matches, mixing[None].astype(F32), 0.0), axis=2)
    token_tag = jnp.sum(jnp.where(pick, (token_range + 1).astype(F32), 0.0), axis=2)
    mix_tag = jnp.sum(jnp.where(pick, mix_of[:, None, :], 0.0), axis=2)
    tags = jnp.pad(
        jnp.stack([token_tag, mix_tag], axis=1).astype(BF16),
        ((0, 0), (0, TAGS - 2), (0, LANES - rows_each)),
    )
    pick = pick.astype(BF16).reshape(peers * rows_each, tokens)

    keep = keep + swap_core(give).astype(F32)
    keep = keep.reshape(tokens, 2, width)
    mine = (jnp.arange(2) == half)[None, :, None]
    keep = keep + jnp.where(mine, residual.astype(F32)[:, None, :], 0.0)
    keep = keep.reshape(tokens, 2 * width)
    part = (keep + swap_half(keep.astype(BF16)).astype(F32)).astype(BF16)
    other = swap_core(part)

    block_shape = shape((tp_count * tall + TAGS, LANES), BF16)
    send = pl.pallas_call(
        functools.partial(gather_kernel, peers),
        out_shape=[block_shape] * peers,
        in_specs=[vmem()] * 4,
        out_specs=[vmem()] * peers,
        compiler_params=params(),
        name="gather_rows",
    )(part, other, pick, tags)

    def route(k):
        return [
            (e * tp_count + t, (e ^ (2 * k + t % 2)) * tp_count + t)
            for e in range(ep_count)
            for t in range(tp_count)
        ]

    got = [lax.ppermute(send[k], ("ep", "tp"), route(k)) for k in range(peers)]

    act, side = pl.pallas_call(
        functools.partial(hidden_units_kernel, peers, rows_each),
        out_shape=(
            shape((peers * rows_each, units), BF16),
            shape((peers, tall + TAGS, LANES), BF16),
        ),
        in_specs=[vmem()] * (5 + peers),
        out_specs=(vmem(), vmem()),
        compiler_params=params(),
        name="hidden_units",
    )(norm_gain.reshape(-1, LANES), gate, gate_pair, up, up_pair, *got)

    act_half = swap_half(act)
    act_core = swap_core(act)
    side = swap_core(side)
    act_both = swap_core(act_half)

    result = pl.pallas_call(
        functools.partial(down_kernel, peers, rows_each),
        out_shape=shape((ep_count, tall + TAGS, LANES), BF16),
        in_specs=[pl.BlockSpec(memory_space=pltpu.SMEM)] + [vmem()] * (6 + peers),
        out_specs=vmem(),
        compiler_params=params(),
        name="down",
    )(request_order, act, act_half, act_core, act_both, down, side, *got)

    came = lax.all_to_all(result, "ep", split_axis=0, concat_axis=0, tiled=True)
    return pl.pallas_call(
        functools.partial(combine_kernel, rows_each),
        out_shape=shape((tokens, width), BF16),
        in_specs=[vmem()],
        out_specs=vmem(),
        compiler_params=params(),
        name="combine",
    )(came)


def solution(mesh):
    return jax.shard_map(
        shards,
        mesh=mesh,
        in_specs=(
            P("ep", "tp"),
            P("ep", "tp"),
            P("ep", "tp"),
            P("ep", None, "tp"),
            P("ep", None, "tp"),
            P("ep"),
            P(),
            P("ep", "tp"),
            P("tp", None),
            P(),
            P("ep", None),
            P("ep", None),
            P("ep", None, "tp"),
            P("ep", None, "tp"),
            P("ep", None, "tp"),
        ),
        out_specs=P("ep", "tp"),
        check_vma=False,
    )
```

```python
import functools
import math

import jax
import jax.numpy as jnp
from jax import lax
from jax.experimental import pallas as pl
from jax.experimental.pallas import tpu as pltpu
from jax.sharding import PartitionSpec as P

HEAD = 128
QHEADS = 16
KVHEADS = 4
LANES = 128
TAGS = 16
MIB = 1024 * 1024
ATTEND_MIB = 61

BF16 = jnp.bfloat16
F32 = jnp.float32


def vmem():
    return pl.BlockSpec(memory_space=pltpu.VMEM)


def hbm():
    return pl.BlockSpec(memory_space=pltpu.HBM)


def params(mib):
    return pltpu.CompilerParams(vmem_limit_bytes=int(mib * MIB))


def dot(a, b):
    return jnp.dot(a, b, preferred_element_type=F32)


def dot_t(a, b):
    return lax.dot_general(a, b, (((1,), (1,)), ((), ())), preferred_element_type=F32)


def attend_kernel(
    kv_local,
    length_hbm,
    query_hbm,
    new_key_hbm,
    new_value_hbm,
    key_hbm,
    value_hbm,
    residual_hbm,
    weight_hbm,
    keep_hbm,
    give_hbm,
    length_ref,
    query_ref,
    new_key_ref,
    new_value_ref,
    key_ref,
    value_ref,
    residual_ref,
    weight_ref,
    keep_ref,
    give_ref,
    sems,
):
    tp = lax.axis_index("tp")
    half, core = tp // 2, tp % 2
    width = weight_ref.shape[2]
    copies = []
    for source, target in (
        (query_hbm, query_ref),
        (key_hbm, key_ref),
        (new_key_hbm, new_key_ref),
        (length_hbm, length_ref),
        (value_hbm, value_ref),
        (new_value_hbm, new_value_ref),
        (residual_hbm, residual_ref),
    ):
        copies.append(pltpu.make_async_copy(source, target, sems.at[len(copies)]))
    for i, block in enumerate((1 - core, 3 - core, core, core + 2)):
        start = pl.multiple_of(block * width, width)
        copies.append(
            pltpu.make_async_copy(
                weight_hbm.at[:, pl.ds(start, width)], weight_ref.at[i], sems.at[len(copies)]
            )
        )
    for copy in copies:
        copy.start()
    tokens = query_ref.shape[0]
    group = QHEADS // KVHEADS
    scale = 1.0 / math.sqrt(HEAD)
    for copy in copies[:4]:
        copy.wait()
    length = length_ref[0]
    pieces = []
    for g in range(kv_local):
        columns = slice(g * HEAD, (g + 1) * HEAD)
        rows = jnp.concatenate(
            [
                query_ref[:, (g * group + i) * HEAD : (g * group + i + 1) * HEAD]
                for i in range(group)
            ],
            axis=0,
        )
        old = dot_t(rows, key_ref[:, columns]) * scale
        new = dot_t(rows, new_key_ref[:, columns]) * scale
        position = lax.broadcasted_iota(jnp.int32, old.shape, 1)
        old = jnp.where(position < length, old, -1e30)
        current = lax.broadcasted_iota(jnp.int32, new.shape, 0) % tokens
        position = lax.broadcasted_iota(jnp.int32, new.shape, 1)
        new = jnp.where(position <= current, new, -1e30)
        highest = jnp.maximum(
            jnp.max(old, axis=1, keepdims=True), jnp.max(new, axis=1, keepdims=True)
        )
        old = jnp.exp(old - highest)
        new = jnp.exp(new - highest)
        totals = jnp.sum(old, axis=1, keepdims=True) + jnp.sum(new, axis=1, keepdims=True)
        if g == 0:
            for copy in copies[4:6]:
                copy.wait()
        mixed = dot(old.astype(BF16), value_ref[:, columns]) + dot(
            new.astype(BF16), new_value_ref[:, columns]
        )
        mixed = (mixed / totals).astype(BF16)
        pieces += [mixed[i * tokens : (i + 1) * tokens] for i in range(group)]
    context = jnp.concatenate(pieces, axis=1)
    copies[6].wait()
    given = pltpu.make_async_copy(give_ref, give_hbm, sems.at[len(copies)])
    kept = pltpu.make_async_copy(keep_ref, keep_hbm, sems.at[len(copies) + 1])
    for i in range(4):
        copies[7 + i].wait()
        part = dot(context, weight_ref[i])
        columns = slice((i % 2) * width, (i % 2 + 1) * width)
        if i < 2:
            give_ref[:, columns] = part.astype(BF16)
        else:
            keep_ref[:, columns] = part + jnp.where(
                half == i - 2, residual_ref[...].astype(F32), 0.0
            )
        if i == 1:
            given.start()
    kept.start()
    given.wait()
    kept.wait()


def load_kernel(from_ref, to_ref):
    to_ref[...] = from_ref[...]


def route_kernel(peers, after_ref, expert_ref, weight_ref, pick_ref, tags_ref):
    del after_ref
    me = lax.axis_index("ep")
    core = lax.axis_index("tp") % 2
    top, tokens = expert_ref.shape
    rows_each = pick_ref.shape[0] // peers
    peer = jnp.bitwise_xor(
        2 * lax.broadcasted_iota(jnp.int32, (peers, tokens), 0) + core, me
    )
    weights = weight_ref[...]
    mixing = (weights / jnp.sum(weights, axis=0, keepdims=True)).astype(BF16).astype(F32)
    mix_of = jnp.zeros((peers, tokens), F32)
    named = jnp.zeros((peers, tokens), F32)
    for j in range(top):
        match = expert_ref[j : j + 1, :] == peer
        mix_of = mix_of + jnp.where(match, mixing[j : j + 1, :], 0.0)
        named = named + jnp.where(match, 1.0, 0.0)
    earlier = lax.broadcasted_iota(jnp.int32, (tokens, tokens), 0) < lax.broadcasted_iota(
        jnp.int32, (tokens, tokens), 1
    )
    rank = dot(named.astype(BF16), jnp.where(earlier, 1.0, 0.0).astype(BF16))
    rank = jnp.where(named > 0.0, rank, -1.0)
    slot = lax.broadcasted_iota(jnp.int32, (rows_each, tokens), 0).astype(F32)
    line = lax.broadcasted_iota(jnp.int32, (TAGS, tokens), 0)
    number = lax.broadcasted_iota(jnp.int32, (TAGS, tokens), 1).astype(F32) + 1.0
    tags_ref[...] = jnp.zeros(tags_ref.shape, BF16)
    for k in range(peers):
        pick = jnp.where(rank[k : k + 1, :] == slot, 1.0, 0.0).astype(BF16)
        pick_ref[k * rows_each : (k + 1) * rows_each, :] = pick
        known = jnp.where(line == 0, number, jnp.where(line == 1, mix_of[k : k + 1, :], 0.0))
        tags_ref[k, :, :rows_each] = dot_t(known.astype(BF16), pick).astype(BF16)


def add_core_kernel(keep_ref, came_ref, sum_ref, send_ref):
    value = keep_ref[...] + came_ref[...].astype(F32)
    sum_ref[...] = value
    send_ref[...] = value.astype(BF16)


def add_half_kernel(sum_ref, came_ref, out_ref):
    out_ref[...] = (sum_ref[...] + came_ref[...].astype(F32)).astype(BF16)


def gather_kernel(peers, part_ref, other_ref, pick_ref, tags_ref, *send_refs):
    core = lax.axis_index("tp") % 2
    rows_each = pick_ref.shape[0] // peers
    pick = pick_ref[...]
    width = part_ref.shape[1] // 2
    blocks = width // LANES
    for source, parity in ((part_ref, core), (other_ref, 1 - core)):
        for half in range(2):
            rows = dot(pick, source[:, half * width : (half + 1) * width]).astype(BF16)
            base = (2 * half + parity) * (blocks * rows_each)
            for k in range(peers):
                for j in range(blocks):
                    start = pl.multiple_of(base + j * rows_each, rows_each)
                    send_refs[k][pl.ds(start, rows_each), :] = rows[
                        k * rows_each : (k + 1) * rows_each, j * LANES : (j + 1) * LANES
                    ]
    for k in range(peers):
        send_refs[k][4 * blocks * rows_each :, :] = tags_ref[k]


def stage_kernel(after_ref, *refs):
    del after_ref
    count = len(refs) - 2
    target, sems = refs[count:]
    copies = [
        pltpu.make_async_copy(refs[i], target.at[i], sems.at[i]) for i in range(count)
    ]
    for copy in copies:
        copy.start()
    for copy in copies:
        copy.wait()


def hidden_units_kernel(peers, rows_each, gain_ref, weight_ref, *refs):
    got = refs[:peers]
    act_ref, side_ref = refs[peers:]
    tp = lax.axis_index("tp")
    core = tp % 2
    blocks = gain_ref.shape[0]
    per_device = blocks // 4
    parts = [
        jnp.concatenate(
            [ref[j * rows_each : (j + 1) * rows_each, :] for ref in got], axis=0
        ).astype(F32)
        for j in range(blocks)
    ]
    squares = parts[0] * parts[0]
    for part in parts[1:]:
        squares = squares + part * part
    mean = jnp.sum(squares, axis=1, keepdims=True) * (1.0 / (blocks * LANES))
    factor = lax.rsqrt(mean + 1e-06)
    normed = jnp.concatenate(
        [(parts[j] * factor * gain_ref[j : j + 1, :]).astype(BF16) for j in range(blocks)], axis=1
    )

    def units(gate, up):
        value = dot_t(normed, weight_ref[gate])
        return value / (1.0 + jnp.exp(-value)) * dot_t(normed, weight_ref[up])

    own = units(0, 1)
    pair = units(2, 3)
    low = jnp.where(core == 0, own, pair)
    high = jnp.where(core == 0, pair, own)
    act_ref[...] = jnp.concatenate([low, high], axis=1).astype(BF16)
    tall = per_device * rows_each
    start = pl.multiple_of((tp + 1 - 2 * core) * tall, tall)
    for k in range(peers):
        side_ref[k, :tall, :] = got[k][pl.ds(start, tall), :]
        side_ref[k, tall:, :] = got[k][blocks * rows_each :, :]


def down_kernel(
    peers,
    rows_each,
    order_ref,
    act_ref,
    act_half_ref,
    act_core_ref,
    act_both_ref,
    down_ref,
    side_ref,
    *refs,
):
    got = refs[:peers]
    out_ref = refs[peers]
    tp = lax.axis_index("tp")
    me = lax.axis_index("ep")
    half, core = tp // 2, tp % 2
    units = act_ref.shape[1]
    blocks = down_ref.shape[1] // LANES
    tall = blocks * rows_each
    here = down_ref[pl.ds(pl.multiple_of(half * units, units), units), :]
    there = down_ref[pl.ds(pl.multiple_of((1 - half) * units, units), units), :]
    diagonal = lax.broadcasted_iota(jnp.int32, (rows_each, LANES), 0) == lax.broadcasted_iota(
        jnp.int32, (rows_each, LANES), 1
    )
    start = pl.multiple_of(tp * tall, tall)
    for group in range(2):
        near, far = ((act_ref, act_half_ref), (act_core_ref, act_both_ref))[group]
        result = dot(near[...], here) + dot(far[...], there)
        for k in range(peers):
            request = jnp.bitwise_xor(me, 2 * k + (core if group == 0 else 1 - core))
            place = order_ref[request]
            if group == 0:
                rows = got[k][pl.ds(start, tall), :]
                tags = got[k][4 * tall :, :]
            else:
                rows = side_ref[k, :tall, :]
                tags = side_ref[k, tall:, :]
            mix = jnp.sum(
                jnp.where(diagonal, tags.astype(F32)[1:2, :], 0.0), axis=1, keepdims=True
            )
            for j in range(blocks):
                piece = slice(j * rows_each, (j + 1) * rows_each)
                value = rows[piece].astype(F32) + result[
                    k * rows_each : (k + 1) * rows_each, j * LANES : (j + 1) * LANES
                ]
                out_ref[place, piece, :] = (mix * value).astype(BF16)
            out_ref[place, tall:, :] = tags


def combine_kernel(rows_each, came_ref, out_ref):
    tokens, width = out_ref.shape
    blocks = width // LANES
    tall = blocks * rows_each
    number = lax.broadcasted_iota(jnp.int32, (tokens, rows_each), 0).astype(F32) + 1.0
    total = jnp.zeros((tokens, width), F32)
    for e in range(came_ref.shape[0]):
        tags = came_ref[e, tall:, :].astype(F32)
        chosen = (number == tags[0:1, :rows_each]).astype(BF16)
        rows = jnp.concatenate(
            [came_ref[e, j * rows_each : (j + 1) * rows_each, :] for j in range(blocks)], axis=1
        )
        total = total + dot(chosen, rows)
    out_ref[...] = total.astype(BF16)


def shards(
    queries,
    new_keys,
    new_values,
    key_cache,
    value_cache,
    cache_lengths,
    request_order,
    residual,
    out_weight,
    norm_gain,
    route_experts,
    route_weights,
    expert_gate,
    expert_up,
    expert_down,
):
    tp_count = lax.axis_size("tp")
    ep_count = lax.axis_size("ep")
    kv_local = KVHEADS // tp_count

    def swap_core(x):
        return lax.ppermute(x, "tp", [(i, i ^ 1) for i in range(tp_count)])

    def swap_half(x):
        return lax.ppermute(x, "tp", [(i, i ^ 2) for i in range(tp_count)])

    gate, up, down = expert_gate[0].T, expert_up[0].T, expert_down[0]
    tokens, top = route_experts.shape
    capacity = 2 * tokens * top // ep_count
    rows_each = -(-capacity // 16) * 16
    peers = ep_count // 2
    width = residual.shape[1]
    blocks = width // LANES
    tall = blocks * rows_each
    units = 2 * gate.shape[0]
    shape = jax.ShapeDtypeStruct

    keep, give = pl.pallas_call(
        functools.partial(attend_kernel, kv_local),
        out_shape=(shape((tokens, 2 * width), F32), shape((tokens, 2 * width), BF16)),
        in_specs=[hbm()] * 8,
        out_specs=(hbm(), hbm()),
        scratch_shapes=[
            pltpu.SMEM(cache_lengths.shape, jnp.int32),
            pltpu.VMEM(queries.shape, BF16),
            pltpu.VMEM(new_keys.shape, BF16),
            pltpu.VMEM(new_values.shape, BF16),
            pltpu.VMEM(key_cache.shape[1:], BF16),
            pltpu.VMEM(value_cache.shape[1:], BF16),
            pltpu.VMEM(residual.shape, BF16),
            pltpu.VMEM((4, out_weight.shape[0], width), BF16),
            pltpu.VMEM((tokens, 2 * width), F32),
            pltpu.VMEM((tokens, 2 * width), BF16),
            pltpu.SemaphoreType.DMA((13,)),
        ],
        compiler_params=params(ATTEND_MIB),
        name="attend",
    )(
        cache_lengths,
        queries,
        new_keys,
        new_values,
        key_cache[0],
        value_cache[0],
        residual,
        out_weight,
    )

    keep = pl.pallas_call(
        load_kernel,
        out_shape=shape(keep.shape, F32),
        in_specs=[vmem()],
        out_specs=vmem(),
        compiler_params=params(4),
        cost_estimate=pl.CostEstimate(flops=0, bytes_accessed=MIB, transcendentals=0),
        name="load",
    )(keep)
    summed, send = pl.pallas_call(
        add_core_kernel,
        out_shape=(shape(keep.shape, F32), shape(keep.shape, BF16)),
        in_specs=[vmem()] * 2,
        out_specs=(vmem(), vmem()),
        compiler_params=params(4),
        name="add_core",
    )(keep, swap_core(give))

    part = pl.pallas_call(
        add_half_kernel,
        out_shape=shape(keep.shape, BF16),
        in_specs=[vmem()] * 2,
        out_specs=vmem(),
        compiler_params=params(4),
        name="add_half",
    )(summed, swap_half(send))
    pick, tags = pl.pallas_call(
        functools.partial(route_kernel, peers),
        out_shape=(
            shape((peers * rows_each, tokens), BF16),
            shape((peers, TAGS, LANES), BF16),
        ),
        in_specs=[pl.BlockSpec(memory_space=pl.ANY)] + [vmem()] * 2,
        out_specs=(vmem(), vmem()),
        compiler_params=params(4),
        cost_estimate=pl.CostEstimate(flops=0, bytes_accessed=MIB, transcendentals=0),
        name="route",
    )(part, route_experts.T, route_weights.T)
    other = swap_core(part)

    block_shape = shape((tp_count * tall + TAGS, LANES), BF16)
    send = pl.pallas_call(
        functools.partial(gather_kernel, peers),
        out_shape=[block_shape] * peers,
        in_specs=[vmem()] * 4,
        out_specs=[vmem()] * peers,
        compiler_params=params(8),
        name="gather_rows",
    )(part, other, pick, tags)

    def route(k):
        return [
            (e * tp_count + t, (e ^ (2 * k + t % 2)) * tp_count + t)
            for e in range(ep_count)
            for t in range(tp_count)
        ]

    send = list(send)
    gate, up, send[-1] = lax.optimization_barrier((gate, up, send[-1]))
    gate_pair, up_pair = swap_core(gate), swap_core(up)
    got = [lax.ppermute(send[k], ("ep", "tp"), route(k)) for k in range(peers)]

    weights = pl.pallas_call(
        stage_kernel,
        out_shape=shape((4,) + gate.shape, BF16),
        in_specs=[vmem()] + [hbm()] * 4,
        out_specs=vmem(),
        scratch_shapes=[pltpu.SemaphoreType.DMA((4,))],
        compiler_params=params(32),
        cost_estimate=pl.CostEstimate(
            flops=0, bytes_accessed=16 * gate.size, transcendentals=0
        ),
        name="stage",
    )(tags, gate, up, gate_pair, up_pair)

    act, side = pl.pallas_call(
        functools.partial(hidden_units_kernel, peers, rows_each),
        out_shape=(
            shape((peers * rows_each, units), BF16),
            shape((peers, tall + TAGS, LANES), BF16),
        ),
        in_specs=[vmem()] * (2 + peers),
        out_specs=(vmem(), vmem()),
        compiler_params=params(16),
        name="hidden_units",
    )(norm_gain.reshape(-1, LANES), weights, *got)

    act_half = swap_half(act)
    act_core = swap_core(act)
    side = swap_core(side)
    act_both = swap_core(act_half)

    result = pl.pallas_call(
        functools.partial(down_kernel, peers, rows_each),
        out_shape=shape((ep_count, tall + TAGS, LANES), BF16),
        in_specs=[pl.BlockSpec(memory_space=pltpu.SMEM)] + [vmem()] * (6 + peers),
        out_specs=vmem(),
        compiler_params=params(16),
        name="down",
    )(request_order, act, act_half, act_core, act_both, down, side, *got)

    came = lax.all_to_all(result, "ep", split_axis=0, concat_axis=0, tiled=True)
    return pl.pallas_call(
        functools.partial(combine_kernel, rows_each),
        out_shape=shape((tokens, width), BF16),
        in_specs=[vmem()],
        out_specs=vmem(),
        compiler_params=params(8),
        name="combine",
    )(came)


def solution(mesh):
    return jax.shard_map(
        shards,
        mesh=mesh,
        in_specs=(
            P("ep", "tp"),
            P("ep", "tp"),
            P("ep", "tp"),
            P("ep", None, "tp"),
            P("ep", None, "tp"),
            P("ep"),
            P(),
            P("ep", "tp"),
            P("tp", None),
            P(),
            P("ep", None),
            P("ep", None),
            P("ep", None, "tp"),
            P("ep", None, "tp"),
            P("ep", None, "tp"),
        ),
        out_specs=P("ep", "tp"),
        check_vma=False,
    )
```

```python
import functools
import math

import jax
import jax.numpy as jnp
from jax import lax
from jax.experimental import pallas as pl
from jax.experimental.pallas import tpu as pltpu
from jax.sharding import PartitionSpec as P

HEAD = 128
QHEADS = 16
KVHEADS = 4
LANES = 128
TAGS = 16
MIB = 1024 * 1024
ATTEND_MIB = 61

BF16 = jnp.bfloat16
F32 = jnp.float32


def vmem():
    return pl.BlockSpec(memory_space=pltpu.VMEM)


def hbm():
    return pl.BlockSpec(memory_space=pltpu.HBM)


def params(mib):
    return pltpu.CompilerParams(vmem_limit_bytes=int(mib * MIB))


def dot(a, b):
    return jnp.dot(a, b, preferred_element_type=F32)


def dot_t(a, b):
    return lax.dot_general(a, b, (((1,), (1,)), ((), ())), preferred_element_type=F32)


def attend_kernel(
    kv_local,
    length_hbm,
    query_hbm,
    new_key_hbm,
    new_value_hbm,
    key_hbm,
    value_hbm,
    residual_hbm,
    weight_hbm,
    keep_hbm,
    give_hbm,
    length_ref,
    query_ref,
    new_key_ref,
    new_value_ref,
    key_ref,
    value_ref,
    residual_ref,
    weight_ref,
    keep_ref,
    give_ref,
    sems,
):
    tp = lax.axis_index("tp")
    half, core = tp // 2, tp % 2
    width = weight_ref.shape[2]
    copies = []
    for source, target in (
        (query_hbm, query_ref),
        (key_hbm, key_ref),
        (new_key_hbm, new_key_ref),
        (length_hbm, length_ref),
        (value_hbm, value_ref),
        (new_value_hbm, new_value_ref),
        (residual_hbm, residual_ref),
    ):
        copies.append(pltpu.make_async_copy(source, target, sems.at[len(copies)]))
    for i, block in enumerate((1 - core, 3 - core, core, core + 2)):
        start = pl.multiple_of(block * width, width)
        copies.append(
            pltpu.make_async_copy(
                weight_hbm.at[:, pl.ds(start, width)], weight_ref.at[i], sems.at[len(copies)]
            )
        )
    for copy in copies:
        copy.start()
    tokens = query_ref.shape[0]
    group = QHEADS // KVHEADS
    scale = 1.0 / math.sqrt(HEAD)
    for copy in copies[:4]:
        copy.wait()
    length = length_ref[0, 0]
    pieces = []
    for g in range(kv_local):
        columns = slice(g * HEAD, (g + 1) * HEAD)
        rows = jnp.concatenate(
            [
                query_ref[:, (g * group + i) * HEAD : (g * group + i + 1) * HEAD]
                for i in range(group)
            ],
            axis=0,
        )
        old = dot_t(rows, key_ref[:, columns]) * scale
        new = dot_t(rows, new_key_ref[:, columns]) * scale
        position = lax.broadcasted_iota(jnp.int32, old.shape, 1)
        old = jnp.where(position < length, old, -1e30)
        current = lax.broadcasted_iota(jnp.int32, new.shape, 0) % tokens
        position = lax.broadcasted_iota(jnp.int32, new.shape, 1)
        new = jnp.where(position <= current, new, -1e30)
        highest = jnp.maximum(
            jnp.max(old, axis=1, keepdims=True), jnp.max(new, axis=1, keepdims=True)
        )
        old = jnp.exp(old - highest)
        new = jnp.exp(new - highest)
        totals = jnp.sum(old, axis=1, keepdims=True) + jnp.sum(new, axis=1, keepdims=True)
        if g == 0:
            for copy in copies[4:6]:
                copy.wait()
        mixed = dot(old.astype(BF16), value_ref[:, columns]) + dot(
            new.astype(BF16), new_value_ref[:, columns]
        )
        mixed = (mixed / totals).astype(BF16)
        pieces += [mixed[i * tokens : (i + 1) * tokens] for i in range(group)]
    context = jnp.concatenate(pieces, axis=1)
    copies[6].wait()
    given = pltpu.make_async_copy(give_ref, give_hbm, sems.at[len(copies)])
    kept = pltpu.make_async_copy(keep_ref, keep_hbm, sems.at[len(copies) + 1])
    for i in range(4):
        copies[7 + i].wait()
        part = dot(context, weight_ref[i])
        columns = slice((i % 2) * width, (i % 2 + 1) * width)
        if i < 2:
            give_ref[:, columns] = part.astype(BF16)
        else:
            keep_ref[:, columns] = part + jnp.where(
                half == i - 2, residual_ref[...].astype(F32), 0.0
            )
        if i == 1:
            given.start()
    kept.start()
    given.wait()
    kept.wait()


def load_kernel(from_ref, to_ref):
    to_ref[...] = from_ref[...]


def earlier_tokens(tokens):
    earlier = lax.broadcasted_iota(jnp.int32, (tokens, tokens), 0) < lax.broadcasted_iota(
        jnp.int32, (tokens, tokens), 1
    )
    return jnp.where(earlier, 1.0, 0.0).astype(BF16)


def slot_numbers(named, tokens):
    rank = dot(named.astype(BF16), earlier_tokens(tokens))
    return jnp.where(named > 0.0, rank, -1.0)


def route_kernel(peers, after_ref, expert_ref, weight_ref, pick_ref, tags_ref):
    del after_ref
    me = lax.axis_index("ep")
    core = lax.axis_index("tp") % 2
    top, tokens = expert_ref.shape
    rows_each = pick_ref.shape[0] // peers
    peer = jnp.bitwise_xor(
        2 * lax.broadcasted_iota(jnp.int32, (peers, tokens), 0) + core, me
    )
    weights = weight_ref[...]
    mixing = (weights / jnp.sum(weights, axis=0, keepdims=True)).astype(BF16).astype(F32)
    mix_of = jnp.zeros((peers, tokens), F32)
    named = jnp.zeros((peers, tokens), F32)
    for j in range(top):
        match = expert_ref[j : j + 1, :] == peer
        mix_of = mix_of + jnp.where(match, mixing[j : j + 1, :], 0.0)
        named = named + jnp.where(match, 1.0, 0.0)
    rank = slot_numbers(named, tokens)
    slot = lax.broadcasted_iota(jnp.int32, (rows_each, tokens), 0).astype(F32)
    line = lax.broadcasted_iota(jnp.int32, (TAGS, tokens), 0)
    names = jnp.zeros((TAGS, tokens), F32)
    for j in range(top):
        names = jnp.where(line == j + 1, expert_ref[j : j + 1, :].astype(F32), names)
    tags_ref[...] = jnp.zeros(tags_ref.shape, BF16)
    for k in range(peers):
        pick = jnp.where(rank[k : k + 1, :] == slot, 1.0, 0.0).astype(BF16)
        pick_ref[k * rows_each : (k + 1) * rows_each, :] = pick
        tags_ref[k, :, :tokens] = names.astype(BF16)
        mix = jnp.where(line == 0, mix_of[k : k + 1, :], 0.0).astype(BF16)
        tags_ref[k, :1, :rows_each] = dot_t(mix, pick)[:1].astype(BF16)


def select_kernel(peers, top, order_ref, side_ref, *refs):
    got = refs[:peers]
    chosen_ref = refs[peers]
    me = lax.axis_index("ep")
    core = lax.axis_index("tp") % 2
    tokens = chosen_ref.shape[0]
    experts = 2 * peers
    rows_each = chosen_ref.shape[1] // experts
    names = jnp.zeros((TAGS, LANES), F32)
    for k in range(peers):
        for tags, parity in (
            (got[k][got[k].shape[0] - TAGS :, :], core),
            (side_ref[k, side_ref.shape[1] - TAGS :, :], 1 - core),
        ):
            here = order_ref[jnp.bitwise_xor(me, 2 * k + parity)] == me
            names = names + jnp.where(here, tags.astype(F32), 0.0)
    expert = lax.broadcasted_iota(jnp.int32, (experts, tokens), 0).astype(F32)
    named = jnp.zeros((experts, tokens), F32)
    for j in range(top):
        named = named + jnp.where(names[j + 1 : j + 2, :tokens] == expert, 1.0, 0.0)
    rank = slot_numbers(named, tokens)
    slot = lax.broadcasted_iota(jnp.int32, (rows_each, tokens), 0).astype(F32)
    pick = jnp.concatenate(
        [jnp.where(rank[e : e + 1, :] == slot, 1.0, 0.0) for e in range(experts)], axis=0
    )
    chosen_ref[...] = pick.T.astype(BF16)


def add_core_kernel(keep_ref, came_ref, sum_ref, send_ref):
    value = keep_ref[...] + came_ref[...].astype(F32)
    sum_ref[...] = value
    send_ref[...] = value.astype(BF16)


def add_half_kernel(sum_ref, came_ref, out_ref):
    out_ref[...] = (sum_ref[...] + came_ref[...].astype(F32)).astype(BF16)


def gather_kernel(first, count, after_ref, part_ref, other_ref, pick_ref, tags_ref, *send_refs):
    del after_ref
    core = lax.axis_index("tp") % 2
    rows_each = pick_ref.shape[0] // tags_ref.shape[0]
    pick = pick_ref[first * rows_each : (first + count) * rows_each, :]
    width = part_ref.shape[1] // 2
    blocks = width // LANES
    for source, parity in ((part_ref, core), (other_ref, 1 - core)):
        for half in range(2):
            rows = dot(pick, source[:, half * width : (half + 1) * width]).astype(BF16)
            base = (2 * half + parity) * (blocks * rows_each)
            for k in range(count):
                for j in range(blocks):
                    start = pl.multiple_of(base + j * rows_each, rows_each)
                    send_refs[k][pl.ds(start, rows_each), :] = rows[
                        k * rows_each : (k + 1) * rows_each, j * LANES : (j + 1) * LANES
                    ]
    for k in range(count):
        send_refs[k][4 * blocks * rows_each :, :] = tags_ref[first + k]


def stage_kernel(after_ref, *refs):
    del after_ref
    count = len(refs) - 2
    target, sems = refs[count:]
    copies = [
        pltpu.make_async_copy(refs[i], target.at[i], sems.at[i]) for i in range(count)
    ]
    for copy in copies:
        copy.start()
    for copy in copies:
        copy.wait()


def hidden_units_kernel(peers, rows_each, gain_ref, weight_ref, *refs):
    got = refs[:peers]
    act_ref, side_ref = refs[peers:]
    tp = lax.axis_index("tp")
    core = tp % 2
    blocks = gain_ref.shape[0]
    per_device = blocks // 4
    parts = [
        jnp.concatenate(
            [ref[j * rows_each : (j + 1) * rows_each, :] for ref in got], axis=0
        ).astype(F32)
        for j in range(blocks)
    ]
    squares = parts[0] * parts[0]
    for part in parts[1:]:
        squares = squares + part * part
    mean = jnp.sum(squares, axis=1, keepdims=True) * (1.0 / (blocks * LANES))
    factor = lax.rsqrt(mean + 1e-06)
    normed = jnp.concatenate(
        [(parts[j] * factor * gain_ref[j : j + 1, :]).astype(BF16) for j in range(blocks)], axis=1
    )

    def units(gate, up):
        value = dot_t(normed, weight_ref[gate])
        return value / (1.0 + jnp.exp(-value)) * dot_t(normed, weight_ref[up])

    own = units(0, 1)
    pair = units(2, 3)
    low = jnp.where(core == 0, own, pair)
    high = jnp.where(core == 0, pair, own)
    act_ref[...] = jnp.concatenate([low, high], axis=1).astype(BF16)
    tall = per_device * rows_each
    start = pl.multiple_of((tp + 1 - 2 * core) * tall, tall)
    for k in range(peers):
        side_ref[k, :tall, :] = got[k][pl.ds(start, tall), :]
        side_ref[k, tall:, :] = got[k][blocks * rows_each :, :]


def down_kernel(
    peers,
    rows_each,
    after_ref,
    order_ref,
    act_ref,
    act_half_ref,
    act_core_ref,
    act_both_ref,
    down_ref,
    side_ref,
    *refs,
):
    del after_ref
    got = refs[:peers]
    out_ref = refs[peers]
    tp = lax.axis_index("tp")
    me = lax.axis_index("ep")
    half, core = tp // 2, tp % 2
    units = act_ref.shape[1]
    blocks = down_ref.shape[1] // LANES
    tall = blocks * rows_each
    here = down_ref[pl.ds(pl.multiple_of(half * units, units), units), :]
    there = down_ref[pl.ds(pl.multiple_of((1 - half) * units, units), units), :]
    diagonal = lax.broadcasted_iota(jnp.int32, (rows_each, LANES), 0) == lax.broadcasted_iota(
        jnp.int32, (rows_each, LANES), 1
    )
    start = pl.multiple_of(tp * tall, tall)
    for group in range(2):
        near, far = ((act_ref, act_half_ref), (act_core_ref, act_both_ref))[group]
        result = dot(near[...], here) + dot(far[...], there)
        for k in range(peers):
            request = jnp.bitwise_xor(me, 2 * k + (core if group == 0 else 1 - core))
            place = order_ref[request]
            if group == 0:
                rows = got[k][pl.ds(start, tall), :]
                tags = got[k][4 * tall :, :]
            else:
                rows = side_ref[k, :tall, :]
                tags = side_ref[k, tall:, :]
            mix = jnp.sum(
                jnp.where(diagonal, tags.astype(F32)[0:1, :], 0.0), axis=1, keepdims=True
            )
            for j in range(blocks):
                piece = slice(j * rows_each, (j + 1) * rows_each)
                value = rows[piece].astype(F32) + result[
                    k * rows_each : (k + 1) * rows_each, j * LANES : (j + 1) * LANES
                ]
                out_ref[place, piece, :] = (mix * value).astype(BF16)


def combine_kernel(rows_each, chosen_ref, came_ref, out_ref):
    chosen = chosen_ref[...]
    experts, tall, _ = came_ref.shape
    for j in range(tall // rows_each):
        rows = jnp.concatenate(
            [came_ref[e, j * rows_each : (j + 1) * rows_each, :] for e in range(experts)], axis=0
        )
        out_ref[:, j * LANES : (j + 1) * LANES] = dot(chosen, rows).astype(BF16)


def shards(
    queries,
    new_keys,
    new_values,
    key_cache,
    value_cache,
    cache_lengths,
    request_order,
    residual,
    out_weight,
    norm_gain,
    route_experts,
    route_weights,
    expert_gate,
    expert_up,
    expert_down,
):
    tp_count = lax.axis_size("tp")
    ep_count = lax.axis_size("ep")
    kv_local = KVHEADS // tp_count

    def swap_core(x):
        return lax.ppermute(x, "tp", [(i, i ^ 1) for i in range(tp_count)])

    def swap_half(x):
        return lax.ppermute(x, "tp", [(i, i ^ 2) for i in range(tp_count)])

    gate, up, down = expert_gate[0].T, expert_up[0].T, expert_down[0]
    tokens, top = route_experts.shape
    capacity = 2 * tokens * top // ep_count
    rows_each = -(-capacity // 16) * 16
    peers = ep_count // 2
    width = residual.shape[1]
    blocks = width // LANES
    tall = blocks * rows_each
    units = 2 * gate.shape[0]
    shape = jax.ShapeDtypeStruct

    keep, give = pl.pallas_call(
        functools.partial(attend_kernel, kv_local),
        out_shape=(shape((tokens, 2 * width), F32), shape((tokens, 2 * width), BF16)),
        in_specs=[hbm()] * 8,
        out_specs=(hbm(), hbm()),
        scratch_shapes=[
            pltpu.SMEM((1, 1), jnp.int32),
            pltpu.VMEM(queries.shape, BF16),
            pltpu.VMEM(new_keys.shape, BF16),
            pltpu.VMEM(new_values.shape, BF16),
            pltpu.VMEM(key_cache.shape[1:], BF16),
            pltpu.VMEM(value_cache.shape[1:], BF16),
            pltpu.VMEM(residual.shape, BF16),
            pltpu.VMEM((4, out_weight.shape[0], width), BF16),
            pltpu.VMEM((tokens, 2 * width), F32),
            pltpu.VMEM((tokens, 2 * width), BF16),
            pltpu.SemaphoreType.DMA((13,)),
        ],
        compiler_params=params(ATTEND_MIB),
        name="attend",
    )(
        cache_lengths.reshape(1, 1),
        queries,
        new_keys,
        new_values,
        key_cache[0],
        value_cache[0],
        residual,
        out_weight,
    )

    keep = pl.pallas_call(
        load_kernel,
        out_shape=shape(keep.shape, F32),
        in_specs=[vmem()],
        out_specs=vmem(),
        compiler_params=params(4),
        cost_estimate=pl.CostEstimate(flops=0, bytes_accessed=MIB, transcendentals=0),
        name="load",
    )(keep)
    summed, send = pl.pallas_call(
        add_core_kernel,
        out_shape=(shape(keep.shape, F32), shape(keep.shape, BF16)),
        in_specs=[vmem()] * 2,
        out_specs=(vmem(), vmem()),
        compiler_params=params(4),
        name="add_core",
    )(keep, swap_core(give))

    part = pl.pallas_call(
        add_half_kernel,
        out_shape=shape(keep.shape, BF16),
        in_specs=[vmem()] * 2,
        out_specs=vmem(),
        compiler_params=params(4),
        name="add_half",
    )(summed, swap_half(send))
    pick, tags = pl.pallas_call(
        functools.partial(route_kernel, peers),
        out_shape=(
            shape((peers * rows_each, tokens), BF16),
            shape((peers, TAGS, LANES), BF16),
        ),
        in_specs=[pl.BlockSpec(memory_space=pl.ANY)] + [vmem()] * 2,
        out_specs=(vmem(), vmem()),
        compiler_params=params(4),
        cost_estimate=pl.CostEstimate(flops=0, bytes_accessed=MIB, transcendentals=0),
        name="route",
    )(part, route_experts.T, route_weights.T)
    other = swap_core(part)

    def gather(first, count, after):
        return pl.pallas_call(
            functools.partial(gather_kernel, first, count),
            out_shape=[shape((tp_count * tall + TAGS, LANES), BF16)] * count,
            in_specs=[pl.BlockSpec(memory_space=pl.ANY)] + [vmem()] * 4,
            out_specs=[vmem()] * count,
            compiler_params=params(8),
            name="gather_rows",
        )(after, part, other, pick, tags)

    def route(k):
        return [
            (e * tp_count + t, (e ^ (2 * k + t % 2)) * tp_count + t)
            for e in range(ep_count)
            for t in range(tp_count)
        ]

    near = peers // 2
    far_send = list(gather(near, peers - near, tags))
    gate, up, far_send[-1] = lax.optimization_barrier((gate, up, far_send[-1]))
    far = [
        lax.ppermute(x, ("ep", "tp"), route(near + k)) for k, x in enumerate(far_send)
    ]
    gate_pair, up_pair = swap_core(gate), swap_core(up)
    near_send = gather(0, near, gate_pair)
    got = [lax.ppermute(x, ("ep", "tp"), route(k)) for k, x in enumerate(near_send)] + far

    weights = pl.pallas_call(
        stage_kernel,
        out_shape=shape((4,) + gate.shape, BF16),
        in_specs=[vmem()] + [hbm()] * 4,
        out_specs=vmem(),
        scratch_shapes=[pltpu.SemaphoreType.DMA((4,))],
        compiler_params=params(32),
        cost_estimate=pl.CostEstimate(
            flops=0, bytes_accessed=16 * gate.size, transcendentals=0
        ),
        name="stage",
    )(tags, gate, up, gate_pair, up_pair)

    act, side = pl.pallas_call(
        functools.partial(hidden_units_kernel, peers, rows_each),
        out_shape=(
            shape((peers * rows_each, units), BF16),
            shape((peers, tall + TAGS, LANES), BF16),
        ),
        in_specs=[vmem()] * (2 + peers),
        out_specs=(vmem(), vmem()),
        compiler_params=params(16),
        name="hidden_units",
    )(norm_gain.reshape(-1, LANES), weights, *got)

    act_half = swap_half(act)
    act_core = swap_core(act)
    side = swap_core(side)
    act_both = swap_core(act_half)

    chosen = pl.pallas_call(
        functools.partial(select_kernel, peers, top),
        out_shape=shape((tokens, ep_count * rows_each), BF16),
        in_specs=[pl.BlockSpec(memory_space=pltpu.SMEM)] + [vmem()] * (1 + peers),
        out_specs=vmem(),
        compiler_params=params(8),
        cost_estimate=pl.CostEstimate(flops=0, bytes_accessed=MIB, transcendentals=0),
        name="select",
    )(request_order, side, *got)
    result = pl.pallas_call(
        functools.partial(down_kernel, peers, rows_each),
        out_shape=shape((ep_count, tall, LANES), BF16),
        in_specs=[pl.BlockSpec(memory_space=pl.ANY), pl.BlockSpec(memory_space=pltpu.SMEM)]
        + [vmem()] * (6 + peers),
        out_specs=vmem(),
        compiler_params=params(16),
        name="down",
    )(chosen, request_order, act, act_half, act_core, act_both, down, side, *got)

    came = lax.all_to_all(result, "ep", split_axis=0, concat_axis=0, tiled=True)
    return pl.pallas_call(
        functools.partial(combine_kernel, rows_each),
        out_shape=shape((tokens, width), BF16),
        in_specs=[vmem()] * 2,
        out_specs=vmem(),
        compiler_params=params(8),
        name="combine",
    )(chosen, came)


def solution(mesh):
    return jax.shard_map(
        shards,
        mesh=mesh,
        in_specs=(
            P("ep", "tp"),
            P("ep", "tp"),
            P("ep", "tp"),
            P("ep", None, "tp"),
            P("ep", None, "tp"),
            P("ep"),
            P(),
            P("ep", "tp"),
            P("tp", None),
            P(),
            P("ep", None),
            P("ep", None),
            P("ep", None, "tp"),
            P("ep", None, "tp"),
            P("ep", None, "tp"),
        ),
        out_specs=P("ep", "tp"),
        check_vma=False,
    )
```

```python
import functools
import math

import jax
import jax.numpy as jnp
from jax import lax
from jax.experimental import pallas as pl
from jax.experimental.pallas import tpu as pltpu
from jax.sharding import PartitionSpec as P

HEAD = 128
QHEADS = 16
KVHEADS = 4
LANES = 128
TAGS = 16
MIB = 1024 * 1024
ATTEND_MIB = 61

BF16 = jnp.bfloat16
F32 = jnp.float32


def vmem():
    return pl.BlockSpec(memory_space=pltpu.VMEM)


def hbm():
    return pl.BlockSpec(memory_space=pltpu.HBM)


def params(mib):
    return pltpu.CompilerParams(vmem_limit_bytes=int(mib * MIB))


def dot(a, b):
    return jnp.dot(a, b, preferred_element_type=F32)


def dot_t(a, b):
    return lax.dot_general(a, b, (((1,), (1,)), ((), ())), preferred_element_type=F32)


def attend_kernel(
    kv_local,
    length_hbm,
    query_hbm,
    new_key_hbm,
    new_value_hbm,
    key_hbm,
    value_hbm,
    residual_hbm,
    weight_hbm,
    keep_hbm,
    give_hbm,
    length_ref,
    query_ref,
    new_key_ref,
    new_value_ref,
    key_ref,
    value_ref,
    residual_ref,
    weight_ref,
    keep_ref,
    give_ref,
    sems,
):
    tp = lax.axis_index("tp")
    half, core = tp // 2, tp % 2
    width = weight_ref.shape[2]
    copies = []
    for source, target in (
        (query_hbm, query_ref),
        (key_hbm, key_ref),
        (new_key_hbm, new_key_ref),
        (length_hbm, length_ref),
        (value_hbm, value_ref),
        (new_value_hbm, new_value_ref),
        (residual_hbm, residual_ref),
    ):
        copies.append(pltpu.make_async_copy(source, target, sems.at[len(copies)]))
    for i, block in enumerate((1 - core, 3 - core, core, core + 2)):
        start = pl.multiple_of(block * width, width)
        copies.append(
            pltpu.make_async_copy(
                weight_hbm.at[:, pl.ds(start, width)], weight_ref.at[i], sems.at[len(copies)]
            )
        )
    for copy in copies:
        copy.start()
    tokens = query_ref.shape[0]
    group = QHEADS // KVHEADS
    scale = 1.0 / math.sqrt(HEAD)
    for copy in copies[:4]:
        copy.wait()
    length = length_ref[0, 0]
    pieces = []
    for g in range(kv_local):
        columns = slice(g * HEAD, (g + 1) * HEAD)
        rows = jnp.concatenate(
            [
                query_ref[:, (g * group + i) * HEAD : (g * group + i + 1) * HEAD]
                for i in range(group)
            ],
            axis=0,
        )
        old = dot_t(rows, key_ref[:, columns]) * scale
        new = dot_t(rows, new_key_ref[:, columns]) * scale
        position = lax.broadcasted_iota(jnp.int32, old.shape, 1)
        old = jnp.where(position < length, old, -1e30)
        current = lax.broadcasted_iota(jnp.int32, new.shape, 0) % tokens
        position = lax.broadcasted_iota(jnp.int32, new.shape, 1)
        new = jnp.where(position <= current, new, -1e30)
        highest = jnp.maximum(
            jnp.max(old, axis=1, keepdims=True), jnp.max(new, axis=1, keepdims=True)
        )
        old = jnp.exp(old - highest)
        new = jnp.exp(new - highest)
        totals = jnp.sum(old, axis=1, keepdims=True) + jnp.sum(new, axis=1, keepdims=True)
        if g == 0:
            for copy in copies[4:6]:
                copy.wait()
        mixed = dot(old.astype(BF16), value_ref[:, columns]) + dot(
            new.astype(BF16), new_value_ref[:, columns]
        )
        mixed = (mixed / totals).astype(BF16)
        pieces += [mixed[i * tokens : (i + 1) * tokens] for i in range(group)]
    context = jnp.concatenate(pieces, axis=1)
    copies[6].wait()
    given = pltpu.make_async_copy(give_ref, give_hbm, sems.at[len(copies)])
    kept = pltpu.make_async_copy(keep_ref, keep_hbm, sems.at[len(copies) + 1])
    for i in range(4):
        copies[7 + i].wait()
        part = dot(context, weight_ref[i])
        columns = slice((i % 2) * width, (i % 2 + 1) * width)
        if i < 2:
            give_ref[:, columns] = part.astype(BF16)
        else:
            keep_ref[:, columns] = part + jnp.where(
                half == i - 2, residual_ref[...].astype(F32), 0.0
            )
        if i == 1:
            given.start()
    kept.start()
    given.wait()
    kept.wait()


def load_kernel(from_ref, to_ref):
    to_ref[...] = from_ref[...]


def earlier_tokens(tokens):
    earlier = lax.broadcasted_iota(jnp.int32, (tokens, tokens), 0) < lax.broadcasted_iota(
        jnp.int32, (tokens, tokens), 1
    )
    return jnp.where(earlier, 1.0, 0.0).astype(BF16)


def slot_numbers(named, tokens):
    rank = dot(named.astype(BF16), earlier_tokens(tokens))
    return jnp.where(named > 0.0, rank, -1.0)


def route_kernel(peers, after_ref, expert_ref, weight_ref, pick_ref, tags_ref):
    del after_ref
    me = lax.axis_index("ep")
    core = lax.axis_index("tp") % 2
    top, tokens = expert_ref.shape
    rows_each = pick_ref.shape[0] // peers
    peer = jnp.bitwise_xor(
        2 * lax.broadcasted_iota(jnp.int32, (peers, tokens), 0) + core, me
    )
    weights = weight_ref[...]
    mixing = (weights / jnp.sum(weights, axis=0, keepdims=True)).astype(BF16).astype(F32)
    mix_of = jnp.zeros((peers, tokens), F32)
    named = jnp.zeros((peers, tokens), F32)
    for j in range(top):
        match = expert_ref[j : j + 1, :] == peer
        mix_of = mix_of + jnp.where(match, mixing[j : j + 1, :], 0.0)
        named = named + jnp.where(match, 1.0, 0.0)
    rank = slot_numbers(named, tokens)
    slot = lax.broadcasted_iota(jnp.int32, (rows_each, tokens), 0).astype(F32)
    line = lax.broadcasted_iota(jnp.int32, (TAGS, tokens), 0)
    names = jnp.zeros((TAGS, tokens), F32)
    for j in range(top):
        names = jnp.where(line == j + 1, expert_ref[j : j + 1, :].astype(F32), names)
    tags_ref[...] = jnp.zeros(tags_ref.shape, BF16)
    for k in range(peers):
        pick = jnp.where(rank[k : k + 1, :] == slot, 1.0, 0.0).astype(BF16)
        pick_ref[k * rows_each : (k + 1) * rows_each, :] = pick
        tags_ref[k, :, :tokens] = names.astype(BF16)
        mix = jnp.where(line == 0, mix_of[k : k + 1, :], 0.0).astype(BF16)
        tags_ref[k, :1, :rows_each] = dot_t(mix, pick)[:1].astype(BF16)


def select_kernel(peers, top, order_ref, side_ref, *refs):
    got = refs[:peers]
    chosen_ref = refs[peers]
    me = lax.axis_index("ep")
    core = lax.axis_index("tp") % 2
    tokens = chosen_ref.shape[0]
    experts = 2 * peers
    rows_each = chosen_ref.shape[1] // experts
    names = jnp.zeros((TAGS, LANES), F32)
    for k in range(peers):
        for tags, parity in (
            (got[k][got[k].shape[0] - TAGS :, :], core),
            (side_ref[k, side_ref.shape[1] - TAGS :, :], 1 - core),
        ):
            here = order_ref[jnp.bitwise_xor(me, 2 * k + parity)] == me
            names = names + jnp.where(here, tags.astype(F32), 0.0)
    expert = lax.broadcasted_iota(jnp.int32, (experts, tokens), 0).astype(F32)
    named = jnp.zeros((experts, tokens), F32)
    for j in range(top):
        named = named + jnp.where(names[j + 1 : j + 2, :tokens] == expert, 1.0, 0.0)
    rank = slot_numbers(named, tokens)
    slot = lax.broadcasted_iota(jnp.int32, (rows_each, tokens), 0).astype(F32)
    pick = jnp.concatenate(
        [jnp.where(rank[e : e + 1, :] == slot, 1.0, 0.0) for e in range(experts)], axis=0
    )
    chosen_ref[...] = pick.T.astype(BF16)


def add_core_kernel(keep_ref, came_ref, sum_ref, send_ref):
    value = keep_ref[...] + came_ref[...].astype(F32)
    sum_ref[...] = value
    send_ref[...] = value.astype(BF16)


def add_half_kernel(sum_ref, came_ref, out_ref):
    out_ref[...] = (sum_ref[...] + came_ref[...].astype(F32)).astype(BF16)


def gather_kernel(first, split, after_ref, part_ref, other_ref, pick_ref, tags_ref, *send_refs):
    del after_ref
    tp = lax.axis_index("tp")
    mine, core = tp // 2, tp % 2
    count = len(split)
    rows_each = pick_ref.shape[0] // tags_ref.shape[0]
    pick = pick_ref[first * rows_each : (first + count) * rows_each, :]
    width = part_ref.shape[1] // 2
    blocks = width // LANES
    tall = blocks * rows_each

    def put(ref, rows, base):
        for j in range(blocks):
            start = pl.multiple_of(base + j * rows_each, rows_each)
            ref[pl.ds(start, rows_each), :] = rows[:, j * LANES : (j + 1) * LANES]

    for source, parity in ((part_ref, core), (other_ref, 1 - core)):
        whole = [k for k in range(count) if not split[k]]
        for half in range(2) if whole else ():
            rows = dot(pick, source[:, half * width : (half + 1) * width]).astype(BF16)
            for k in whole:
                piece = rows[k * rows_each : (k + 1) * rows_each]
                put(send_refs[k], piece, (2 * half + parity) * tall)
        for k in range(count):
            if split[k]:
                columns = pl.ds(pl.multiple_of(mine * width, width), width)
                piece = pick[k * rows_each : (k + 1) * rows_each]
                put(send_refs[k], dot(piece, source[:, columns]).astype(BF16), parity * tall)
    for k in range(count):
        send_refs[k][send_refs[k].shape[0] - TAGS :, :] = tags_ref[first + k]


def stage_kernel(after_ref, *refs):
    del after_ref
    count = len(refs) - 2
    target, sems = refs[count:]
    copies = [
        pltpu.make_async_copy(refs[i], target.at[i], sems.at[i]) for i in range(count)
    ]
    for copy in copies:
        copy.start()
    for copy in copies:
        copy.wait()


def hidden_units_kernel(split, rows_each, gain_ref, weight_ref, *refs):
    peers = len(split)
    got = refs[:peers]
    halves = list(refs[peers:-2])
    act_ref, side_ref = refs[-2:]
    tp = lax.axis_index("tp")
    half, core = tp // 2, tp % 2
    blocks = gain_ref.shape[0]
    tall = blocks // 4 * rows_each

    columns = []
    for ref, parted in zip(got, split):
        if parted:
            own, came = ref[: 2 * tall, :], halves.pop(0)[: 2 * tall, :]
            low = jnp.where(half == 0, own, came)
            high = jnp.where(half == 0, came, own)
            rows = jnp.concatenate([low, high], axis=0)
        else:
            rows = ref[: 4 * tall, :]
        columns.append([rows[j * rows_each : (j + 1) * rows_each] for j in range(blocks)])
    parts = [
        jnp.concatenate([column[j] for column in columns], axis=0).astype(F32)
        for j in range(blocks)
    ]
    squares = parts[0] * parts[0]
    for part in parts[1:]:
        squares = squares + part * part
    mean = jnp.sum(squares, axis=1, keepdims=True) * (1.0 / (blocks * LANES))
    factor = lax.rsqrt(mean + 1e-06)
    normed = jnp.concatenate(
        [(parts[j] * factor * gain_ref[j : j + 1, :]).astype(BF16) for j in range(blocks)], axis=1
    )

    def units(gate, up):
        value = dot_t(normed, weight_ref[gate])
        return value / (1.0 + jnp.exp(-value)) * dot_t(normed, weight_ref[up])

    own = units(0, 1)
    pair = units(2, 3)
    low = jnp.where(core == 0, own, pair)
    high = jnp.where(core == 0, pair, own)
    act_ref[...] = jnp.concatenate([low, high], axis=1).astype(BF16)
    for k in range(peers):
        place = 1 - core + (0 if split[k] else 2 * half)
        start = pl.multiple_of(place * tall, tall)
        side_ref[k, :tall, :] = got[k][pl.ds(start, tall), :]
        side_ref[k, tall:, :] = got[k][got[k].shape[0] - TAGS :, :]


def down_kernel(
    split,
    rows_each,
    after_ref,
    order_ref,
    act_ref,
    act_half_ref,
    act_core_ref,
    act_both_ref,
    down_ref,
    side_ref,
    *refs,
):
    del after_ref
    peers = len(split)
    got = refs[:peers]
    out_ref = refs[peers]
    tp = lax.axis_index("tp")
    me = lax.axis_index("ep")
    half, core = tp // 2, tp % 2
    units = act_ref.shape[1]
    blocks = down_ref.shape[1] // LANES
    tall = blocks * rows_each
    here = down_ref[pl.ds(pl.multiple_of(half * units, units), units), :]
    there = down_ref[pl.ds(pl.multiple_of((1 - half) * units, units), units), :]
    diagonal = lax.broadcasted_iota(jnp.int32, (rows_each, LANES), 0) == lax.broadcasted_iota(
        jnp.int32, (rows_each, LANES), 1
    )
    for group in range(2):
        near, far = ((act_ref, act_half_ref), (act_core_ref, act_both_ref))[group]
        result = dot(near[...], here) + dot(far[...], there)
        for k in range(peers):
            request = jnp.bitwise_xor(me, 2 * k + (core if group == 0 else 1 - core))
            place = order_ref[request]
            if group == 0:
                start = pl.multiple_of((core if split[k] else tp) * tall, tall)
                rows = got[k][pl.ds(start, tall), :]
                tags = got[k][got[k].shape[0] - TAGS :, :]
            else:
                rows = side_ref[k, :tall, :]
                tags = side_ref[k, tall:, :]
            mix = jnp.sum(
                jnp.where(diagonal, tags.astype(F32)[0:1, :], 0.0), axis=1, keepdims=True
            )
            for j in range(blocks):
                piece = slice(j * rows_each, (j + 1) * rows_each)
                value = rows[piece].astype(F32) + result[
                    k * rows_each : (k + 1) * rows_each, j * LANES : (j + 1) * LANES
                ]
                out_ref[place, piece, :] = (mix * value).astype(BF16)


def combine_kernel(rows_each, chosen_ref, came_ref, out_ref):
    chosen = chosen_ref[...]
    experts, tall, _ = came_ref.shape
    for j in range(tall // rows_each):
        rows = jnp.concatenate(
            [came_ref[e, j * rows_each : (j + 1) * rows_each, :] for e in range(experts)], axis=0
        )
        out_ref[:, j * LANES : (j + 1) * LANES] = dot(chosen, rows).astype(BF16)


def shards(
    queries,
    new_keys,
    new_values,
    key_cache,
    value_cache,
    cache_lengths,
    request_order,
    residual,
    out_weight,
    norm_gain,
    route_experts,
    route_weights,
    expert_gate,
    expert_up,
    expert_down,
):
    tp_count = lax.axis_size("tp")
    ep_count = lax.axis_size("ep")
    kv_local = KVHEADS // tp_count

    def swap_core(x):
        return lax.ppermute(x, "tp", [(i, i ^ 1) for i in range(tp_count)])

    def swap_half(x):
        return lax.ppermute(x, "tp", [(i, i ^ 2) for i in range(tp_count)])

    gate, up, down = expert_gate[0].T, expert_up[0].T, expert_down[0]
    tokens, top = route_experts.shape
    capacity = 2 * tokens * top // ep_count
    rows_each = -(-capacity // 16) * 16
    peers = ep_count // 2
    width = residual.shape[1]
    blocks = width // LANES
    tall = blocks * rows_each
    units = 2 * gate.shape[0]
    shape = jax.ShapeDtypeStruct

    keep, give = pl.pallas_call(
        functools.partial(attend_kernel, kv_local),
        out_shape=(shape((tokens, 2 * width), F32), shape((tokens, 2 * width), BF16)),
        in_specs=[hbm()] * 8,
        out_specs=(hbm(), hbm()),
        scratch_shapes=[
            pltpu.SMEM((1, 1), jnp.int32),
            pltpu.VMEM(queries.shape, BF16),
            pltpu.VMEM(new_keys.shape, BF16),
            pltpu.VMEM(new_values.shape, BF16),
            pltpu.VMEM(key_cache.shape[1:], BF16),
            pltpu.VMEM(value_cache.shape[1:], BF16),
            pltpu.VMEM(residual.shape, BF16),
            pltpu.VMEM((4, out_weight.shape[0], width), BF16),
            pltpu.VMEM((tokens, 2 * width), F32),
            pltpu.VMEM((tokens, 2 * width), BF16),
            pltpu.SemaphoreType.DMA((13,)),
        ],
        compiler_params=params(ATTEND_MIB),
        name="attend",
    )(
        cache_lengths.reshape(1, 1),
        queries,
        new_keys,
        new_values,
        key_cache[0],
        value_cache[0],
        residual,
        out_weight,
    )

    keep = pl.pallas_call(
        load_kernel,
        out_shape=shape(keep.shape, F32),
        in_specs=[vmem()],
        out_specs=vmem(),
        compiler_params=params(4),
        cost_estimate=pl.CostEstimate(flops=0, bytes_accessed=MIB, transcendentals=0),
        name="load",
    )(keep)
    summed, send = pl.pallas_call(
        add_core_kernel,
        out_shape=(shape(keep.shape, F32), shape(keep.shape, BF16)),
        in_specs=[vmem()] * 2,
        out_specs=(vmem(), vmem()),
        compiler_params=params(4),
        name="add_core",
    )(keep, swap_core(give))

    part = pl.pallas_call(
        add_half_kernel,
        out_shape=shape(keep.shape, BF16),
        in_specs=[vmem()] * 2,
        out_specs=vmem(),
        compiler_params=params(4),
        name="add_half",
    )(summed, swap_half(send))
    pick, tags = pl.pallas_call(
        functools.partial(route_kernel, peers),
        out_shape=(
            shape((peers * rows_each, tokens), BF16),
            shape((peers, TAGS, LANES), BF16),
        ),
        in_specs=[pl.BlockSpec(memory_space=pl.ANY)] + [vmem()] * 2,
        out_specs=(vmem(), vmem()),
        compiler_params=params(4),
        cost_estimate=pl.CostEstimate(flops=0, bytes_accessed=MIB, transcendentals=0),
        name="route",
    )(part, route_experts.T, route_weights.T)
    other = swap_core(part)

    near = peers // 2
    split = [k >= near and (k - near) % 2 == 1 for k in range(peers)]

    def gather(first, last, after):
        return pl.pallas_call(
            functools.partial(gather_kernel, first, split[first:last]),
            out_shape=[
                shape(((2 if split[k] else 4) * tall + TAGS, LANES), BF16)
                for k in range(first, last)
            ],
            in_specs=[pl.BlockSpec(memory_space=pl.ANY)] + [vmem()] * 4,
            out_specs=[vmem()] * (last - first),
            compiler_params=params(8),
            name="gather_rows",
        )(after, part, other, pick, tags)

    def route(k):
        return [
            (e * tp_count + t, (e ^ (2 * k + t % 2)) * tp_count + t)
            for e in range(ep_count)
            for t in range(tp_count)
        ]

    far_send = list(gather(near, peers, tags))
    gate, up, far_send[-1] = lax.optimization_barrier((gate, up, far_send[-1]))
    far = [
        lax.ppermute(x, ("ep", "tp"), route(near + k)) for k, x in enumerate(far_send)
    ]
    gate_pair, up_pair = swap_core(gate), swap_core(up)
    near_send = gather(0, near, gate_pair)
    got = [lax.ppermute(x, ("ep", "tp"), route(k)) for k, x in enumerate(near_send)] + far
    halves = [swap_half(got[k]) for k in range(peers) if split[k]]

    weights = pl.pallas_call(
        stage_kernel,
        out_shape=shape((4,) + gate.shape, BF16),
        in_specs=[vmem()] + [hbm()] * 4,
        out_specs=vmem(),
        scratch_shapes=[pltpu.SemaphoreType.DMA((4,))],
        compiler_params=params(32),
        cost_estimate=pl.CostEstimate(
            flops=0, bytes_accessed=16 * gate.size, transcendentals=0
        ),
        name="stage",
    )(tags, gate, up, gate_pair, up_pair)

    act, side = pl.pallas_call(
        functools.partial(hidden_units_kernel, split, rows_each),
        out_shape=(
            shape((peers * rows_each, units), BF16),
            shape((peers, tall + TAGS, LANES), BF16),
        ),
        in_specs=[vmem()] * (2 + peers + len(halves)),
        out_specs=(vmem(), vmem()),
        compiler_params=params(16),
        name="hidden_units",
    )(norm_gain.reshape(-1, LANES), weights, *got, *halves)

    act_half = swap_half(act)
    act_core = swap_core(act)
    side = swap_core(side)
    act_both = swap_core(act_half)

    chosen = pl.pallas_call(
        functools.partial(select_kernel, peers, top),
        out_shape=shape((tokens, ep_count * rows_each), BF16),
        in_specs=[pl.BlockSpec(memory_space=pltpu.SMEM)] + [vmem()] * (1 + peers),
        out_specs=vmem(),
        compiler_params=params(8),
        cost_estimate=pl.CostEstimate(flops=0, bytes_accessed=MIB, transcendentals=0),
        name="select",
    )(request_order, side, *got)
    result = pl.pallas_call(
        functools.partial(down_kernel, split, rows_each),
        out_shape=shape((ep_count, tall, LANES), BF16),
        in_specs=[pl.BlockSpec(memory_space=pl.ANY), pl.BlockSpec(memory_space=pltpu.SMEM)]
        + [vmem()] * (6 + peers),
        out_specs=vmem(),
        compiler_params=params(16),
        name="down",
    )(chosen, request_order, act, act_half, act_core, act_both, down, side, *got)

    came = lax.all_to_all(result, "ep", split_axis=0, concat_axis=0, tiled=True)
    return pl.pallas_call(
        functools.partial(combine_kernel, rows_each),
        out_shape=shape((tokens, width), BF16),
        in_specs=[vmem()] * 2,
        out_specs=vmem(),
        compiler_params=params(8),
        name="combine",
    )(chosen, came)


def solution(mesh):
    return jax.shard_map(
        shards,
        mesh=mesh,
        in_specs=(
            P("ep", "tp"),
            P("ep", "tp"),
            P("ep", "tp"),
            P("ep", None, "tp"),
            P("ep", None, "tp"),
            P("ep"),
            P(),
            P("ep", "tp"),
            P("tp", None),
            P(),
            P("ep", None),
            P("ep", None),
            P("ep", None, "tp"),
            P("ep", None, "tp"),
            P("ep", None, "tp"),
        ),
        out_specs=P("ep", "tp"),
        check_vma=False,
    )
```

```python
import functools
import math

import jax
import jax.numpy as jnp
from jax import lax
from jax.experimental import pallas as pl
from jax.experimental.pallas import tpu as pltpu
from jax.sharding import PartitionSpec as P

HEAD = 128
QHEADS = 16
KVHEADS = 4
LANES = 128
TAGS = 16
MIB = 1024 * 1024

BF16 = jnp.bfloat16
F32 = jnp.float32


def vmem():
    return pl.BlockSpec(memory_space=pltpu.VMEM)


def hbm():
    return pl.BlockSpec(memory_space=pltpu.HBM)


def params(mib):
    return pltpu.CompilerParams(vmem_limit_bytes=int(mib * MIB))


def dot(a, b):
    return jnp.dot(a, b, preferred_element_type=F32)


def dot_t(a, b):
    return lax.dot_general(a, b, (((1,), (1,)), ((), ())), preferred_element_type=F32)


def begin_kernel(out_ref):
    out_ref[...] = jnp.zeros(out_ref.shape, F32)


def attend_kernel(
    kv_local,
    after_ref,
    length_ref,
    query_ref,
    new_key_ref,
    new_value_ref,
    key_ref,
    value_ref,
    context_ref,
):
    del after_ref
    tokens = query_ref.shape[0]
    group = QHEADS // KVHEADS
    length = length_ref[0]
    scale = 1.0 / math.sqrt(HEAD)
    pieces = []
    for g in range(kv_local):
        columns = slice(g * HEAD, (g + 1) * HEAD)
        rows = jnp.concatenate(
            [
                query_ref[:, (g * group + i) * HEAD : (g * group + i + 1) * HEAD]
                for i in range(group)
            ],
            axis=0,
        )
        old = dot_t(rows, key_ref[:, columns]) * scale
        new = dot_t(rows, new_key_ref[:, columns]) * scale
        position = lax.broadcasted_iota(jnp.int32, old.shape, 1)
        old = jnp.where(position < length, old, -1e30)
        current = lax.broadcasted_iota(jnp.int32, new.shape, 0) % tokens
        position = lax.broadcasted_iota(jnp.int32, new.shape, 1)
        new = jnp.where(position <= current, new, -1e30)
        highest = jnp.maximum(
            jnp.max(old, axis=1, keepdims=True), jnp.max(new, axis=1, keepdims=True)
        )
        old = jnp.exp(old - highest)
        new = jnp.exp(new - highest)
        totals = jnp.sum(old, axis=1, keepdims=True) + jnp.sum(new, axis=1, keepdims=True)
        mixed = dot(old.astype(BF16), value_ref[:, columns]) + dot(
            new.astype(BF16), new_value_ref[:, columns]
        )
        mixed = (mixed / totals).astype(BF16)
        pieces += [mixed[i * tokens : (i + 1) * tokens] for i in range(group)]
    context_ref[...] = jnp.concatenate(pieces, axis=1)


def project_kernel(context_ref, residual_ref, weight_ref, keep_ref, give_ref):
    tp = lax.axis_index("tp")
    half, core = tp // 2, tp % 2
    width = residual_ref.shape[1]
    context = context_ref[...]
    for i, block in enumerate((1 - core, 3 - core, core, core + 2)):
        start = pl.multiple_of(block * width, width)
        part = dot(context, weight_ref[:, pl.ds(start, width)])
        columns = slice((i % 2) * width, (i % 2 + 1) * width)
        if i < 2:
            give_ref[:, columns] = part.astype(BF16)
        else:
            keep_ref[:, columns] = part + jnp.where(
                half == i - 2, residual_ref[...].astype(F32), 0.0
            )


def earlier_tokens(tokens):
    earlier = lax.broadcasted_iota(jnp.int32, (tokens, tokens), 0) < lax.broadcasted_iota(
        jnp.int32, (tokens, tokens), 1
    )
    return jnp.where(earlier, 1.0, 0.0).astype(BF16)


def slot_numbers(named, tokens):
    rank = dot(named.astype(BF16), earlier_tokens(tokens))
    return jnp.where(named > 0.0, rank, -1.0)


def route_kernel(peers, after_ref, expert_ref, weight_ref, pick_ref, tags_ref):
    del after_ref
    me = lax.axis_index("ep")
    core = lax.axis_index("tp") % 2
    top, tokens = expert_ref.shape
    rows_each = pick_ref.shape[0] // peers
    peer = jnp.bitwise_xor(
        2 * lax.broadcasted_iota(jnp.int32, (peers, tokens), 0) + core, me
    )
    weights = weight_ref[...]
    mixing = (weights / jnp.sum(weights, axis=0, keepdims=True)).astype(BF16).astype(F32)
    mix_of = jnp.zeros((peers, tokens), F32)
    named = jnp.zeros((peers, tokens), F32)
    for j in range(top):
        match = expert_ref[j : j + 1, :] == peer
        mix_of = mix_of + jnp.where(match, mixing[j : j + 1, :], 0.0)
        named = named + jnp.where(match, 1.0, 0.0)
    rank = slot_numbers(named, tokens)
    slot = lax.broadcasted_iota(jnp.int32, (rows_each, tokens), 0).astype(F32)
    line = lax.broadcasted_iota(jnp.int32, (TAGS, tokens), 0)
    names = jnp.zeros((TAGS, tokens), F32)
    for j in range(top):
        names = jnp.where(line == j + 1, expert_ref[j : j + 1, :].astype(F32), names)
    tags_ref[...] = jnp.zeros(tags_ref.shape, BF16)
    for k in range(peers):
        pick = jnp.where(rank[k : k + 1, :] == slot, 1.0, 0.0).astype(BF16)
        pick_ref[k * rows_each : (k + 1) * rows_each, :] = pick
        tags_ref[k, :, :tokens] = names.astype(BF16)
        mix = jnp.where(line == 0, mix_of[k : k + 1, :], 0.0).astype(BF16)
        tags_ref[k, :1, :rows_each] = dot_t(mix, pick)[:1].astype(BF16)


def select_kernel(peers, top, order_ref, side_ref, *refs):
    got = refs[:peers]
    chosen_ref = refs[peers]
    me = lax.axis_index("ep")
    core = lax.axis_index("tp") % 2
    tokens = chosen_ref.shape[0]
    experts = 2 * peers
    rows_each = chosen_ref.shape[1] // experts
    names = jnp.zeros((TAGS, LANES), F32)
    for k in range(peers):
        for tags, parity in (
            (got[k][got[k].shape[0] - TAGS :, :], core),
            (side_ref[k, side_ref.shape[1] - TAGS :, :], 1 - core),
        ):
            here = order_ref[jnp.bitwise_xor(me, 2 * k + parity)] == me
            names = names + jnp.where(here, tags.astype(F32), 0.0)
    expert = lax.broadcasted_iota(jnp.int32, (experts, tokens), 0).astype(F32)
    named = jnp.zeros((experts, tokens), F32)
    for j in range(top):
        named = named + jnp.where(names[j + 1 : j + 2, :tokens] == expert, 1.0, 0.0)
    rank = slot_numbers(named, tokens)
    slot = lax.broadcasted_iota(jnp.int32, (rows_each, tokens), 0).astype(F32)
    pick = jnp.concatenate(
        [jnp.where(rank[e : e + 1, :] == slot, 1.0, 0.0) for e in range(experts)], axis=0
    )
    chosen_ref[...] = pick.T.astype(BF16)


def add_core_kernel(keep_ref, came_ref, sum_ref, send_ref):
    value = keep_ref[...] + came_ref[...].astype(F32)
    sum_ref[...] = value
    send_ref[...] = value.astype(BF16)


def add_half_kernel(sum_ref, came_ref, out_ref):
    out_ref[...] = (sum_ref[...] + came_ref[...].astype(F32)).astype(BF16)


def gather_kernel(first, split, after_ref, part_ref, other_ref, pick_ref, tags_ref, *send_refs):
    del after_ref
    tp = lax.axis_index("tp")
    mine, core = tp // 2, tp % 2
    count = len(split)
    rows_each = pick_ref.shape[0] // tags_ref.shape[0]
    pick = pick_ref[first * rows_each : (first + count) * rows_each, :]
    width = part_ref.shape[1] // 2
    blocks = width // LANES
    tall = blocks * rows_each

    def put(ref, rows, base):
        for j in range(blocks):
            start = pl.multiple_of(base + j * rows_each, rows_each)
            ref[pl.ds(start, rows_each), :] = rows[:, j * LANES : (j + 1) * LANES]

    for source, parity in ((part_ref, core), (other_ref, 1 - core)):
        whole = [k for k in range(count) if not split[k]]
        for half in range(2) if whole else ():
            rows = dot(pick, source[:, half * width : (half + 1) * width]).astype(BF16)
            for k in whole:
                piece = rows[k * rows_each : (k + 1) * rows_each]
                put(send_refs[k], piece, (2 * half + parity) * tall)
        for k in range(count):
            if split[k]:
                columns = pl.ds(pl.multiple_of(mine * width, width), width)
                piece = pick[k * rows_each : (k + 1) * rows_each]
                put(send_refs[k], dot(piece, source[:, columns]).astype(BF16), parity * tall)
    for k in range(count):
        send_refs[k][send_refs[k].shape[0] - TAGS :, :] = tags_ref[first + k]


def stage_kernel(after_ref, gate, up, gate_pair, up_pair, out_ref, held_ref, sems):
    del after_ref
    core = lax.axis_index("tp") % 2
    copies = [
        pltpu.make_async_copy(source, held_ref.at[place], sems.at[i])
        for i, (source, place) in enumerate(
            ((gate, core), (up, 2 + core), (gate_pair, 1 - core), (up_pair, 3 - core))
        )
    ]
    for copy in copies:
        copy.start()
    for copy in copies:
        copy.wait()
    units, width = held_ref.shape[1:]
    for j in range(width // LANES):
        columns = slice(j * LANES, (j + 1) * LANES)
        out_ref[columns, :] = held_ref[:, :, columns].reshape(4 * units, LANES).T


def hidden_units_kernel(split, rows_each, gain_ref, weight_ref, *refs):
    peers = len(split)
    got = refs[:peers]
    halves = list(refs[peers:-2])
    act_ref, side_ref = refs[-2:]
    tp = lax.axis_index("tp")
    half, core = tp // 2, tp % 2
    blocks = gain_ref.shape[0]
    tall = blocks // 4 * rows_each

    columns = []
    for ref, parted in zip(got, split):
        if parted:
            own, came = ref[: 2 * tall, :], halves.pop(0)[: 2 * tall, :]
            low = jnp.where(half == 0, own, came)
            high = jnp.where(half == 0, came, own)
            rows = jnp.concatenate([low, high], axis=0)
        else:
            rows = ref[: 4 * tall, :]
        columns.append([rows[j * rows_each : (j + 1) * rows_each] for j in range(blocks)])
    parts = [
        jnp.concatenate([column[j] for column in columns], axis=0).astype(F32)
        for j in range(blocks)
    ]
    squares = parts[0] * parts[0]
    for part in parts[1:]:
        squares = squares + part * part
    mean = jnp.sum(squares, axis=1, keepdims=True) * (1.0 / (blocks * LANES))
    factor = lax.rsqrt(mean + 1e-06)
    normed = jnp.concatenate(
        [(parts[j] * factor * gain_ref[j : j + 1, :]).astype(BF16) for j in range(blocks)], axis=1
    )

    product = dot(normed, weight_ref[...])
    units = act_ref.shape[1]
    gate, up = product[:, :units], product[:, units:]
    act_ref[...] = (gate / (1.0 + jnp.exp(-gate)) * up).astype(BF16)
    for k in range(peers):
        place = 1 - core + (0 if split[k] else 2 * half)
        start = pl.multiple_of(place * tall, tall)
        side_ref[k, :tall, :] = got[k][pl.ds(start, tall), :]
        side_ref[k, tall:, :] = got[k][got[k].shape[0] - TAGS :, :]


def down_kernel(
    split,
    rows_each,
    after_ref,
    order_ref,
    act_ref,
    act_half_ref,
    act_core_ref,
    act_both_ref,
    down_ref,
    side_ref,
    *refs,
):
    del after_ref
    peers = len(split)
    got = refs[:peers]
    out_ref = refs[peers]
    tp = lax.axis_index("tp")
    me = lax.axis_index("ep")
    half, core = tp // 2, tp % 2
    units = act_ref.shape[1]
    blocks = down_ref.shape[1] // LANES
    tall = blocks * rows_each
    here = down_ref[pl.ds(pl.multiple_of(half * units, units), units), :]
    there = down_ref[pl.ds(pl.multiple_of((1 - half) * units, units), units), :]
    diagonal = lax.broadcasted_iota(jnp.int32, (rows_each, LANES), 0) == lax.broadcasted_iota(
        jnp.int32, (rows_each, LANES), 1
    )
    for group in range(2):
        near, far = ((act_ref, act_half_ref), (act_core_ref, act_both_ref))[group]
        result = dot(near[...], here) + dot(far[...], there)
        for k in range(peers):
            request = jnp.bitwise_xor(me, 2 * k + (core if group == 0 else 1 - core))
            place = order_ref[request]
            if group == 0:
                start = pl.multiple_of((core if split[k] else tp) * tall, tall)
                rows = got[k][pl.ds(start, tall), :]
                tags = got[k][got[k].shape[0] - TAGS :, :]
            else:
                rows = side_ref[k, :tall, :]
                tags = side_ref[k, tall:, :]
            mix = jnp.sum(
                jnp.where(diagonal, tags.astype(F32)[0:1, :], 0.0), axis=1, keepdims=True
            )
            for j in range(blocks):
                piece = slice(j * rows_each, (j + 1) * rows_each)
                value = rows[piece].astype(F32) + result[
                    k * rows_each : (k + 1) * rows_each, j * LANES : (j + 1) * LANES
                ]
                out_ref[place, piece, :] = (mix * value).astype(BF16)


def combine_kernel(rows_each, chosen_ref, came_ref, out_ref):
    chosen = chosen_ref[...]
    experts, tall, _ = came_ref.shape
    for j in range(tall // rows_each):
        rows = jnp.concatenate(
            [came_ref[e, j * rows_each : (j + 1) * rows_each, :] for e in range(experts)], axis=0
        )
        out_ref[:, j * LANES : (j + 1) * LANES] = dot(chosen, rows).astype(BF16)


def shards(
    queries,
    new_keys,
    new_values,
    key_cache,
    value_cache,
    cache_lengths,
    request_order,
    residual,
    out_weight,
    norm_gain,
    route_experts,
    route_weights,
    expert_gate,
    expert_up,
    expert_down,
):
    tp_count = lax.axis_size("tp")
    ep_count = lax.axis_size("ep")
    kv_local = KVHEADS // tp_count

    def swap_core(x):
        return lax.ppermute(x, "tp", [(i, i ^ 1) for i in range(tp_count)])

    def swap_half(x):
        return lax.ppermute(x, "tp", [(i, i ^ 2) for i in range(tp_count)])

    gate, up, down = expert_gate[0].T, expert_up[0].T, expert_down[0]
    tokens, top = route_experts.shape
    capacity = 2 * tokens * top // ep_count
    rows_each = -(-capacity // 16) * 16
    peers = ep_count // 2
    width = residual.shape[1]
    blocks = width // LANES
    tall = blocks * rows_each
    units = 2 * gate.shape[0]
    shape = jax.ShapeDtypeStruct

    begun = pl.pallas_call(
        begin_kernel,
        out_shape=shape((8, LANES), F32),
        out_specs=vmem(),
        compiler_params=params(1),
        cost_estimate=pl.CostEstimate(
            flops=20 * 10**9, bytes_accessed=64 * MIB, transcendentals=0
        ),
        name="begin",
    )()
    context = pl.pallas_call(
        functools.partial(attend_kernel, kv_local),
        out_shape=shape(queries.shape, BF16),
        in_specs=[pl.BlockSpec(memory_space=pl.ANY), pl.BlockSpec(memory_space=pltpu.SMEM)]
        + [vmem()] * 5,
        out_specs=vmem(),
        compiler_params=params(16),
        cost_estimate=pl.CostEstimate(
            flops=2 * 10**8, bytes_accessed=MIB // 2, transcendentals=0
        ),
        name="attend",
    )(begun, cache_lengths, queries, new_keys, new_values, key_cache[0], value_cache[0])
    keep, give = pl.pallas_call(
        project_kernel,
        out_shape=(shape((tokens, 2 * width), F32), shape((tokens, 2 * width), BF16)),
        in_specs=[vmem()] * 3,
        out_specs=(vmem(), vmem()),
        compiler_params=params(16),
        name="project",
    )(context, residual, out_weight)

    summed, send = pl.pallas_call(
        add_core_kernel,
        out_shape=(shape(keep.shape, F32), shape(keep.shape, BF16)),
        in_specs=[vmem()] * 2,
        out_specs=(vmem(), vmem()),
        compiler_params=params(4),
        name="add_core",
    )(keep, swap_core(give))

    part = pl.pallas_call(
        add_half_kernel,
        out_shape=shape(keep.shape, BF16),
        in_specs=[vmem()] * 2,
        out_specs=vmem(),
        compiler_params=params(4),
        name="add_half",
    )(summed, swap_half(send))
    pick, tags = pl.pallas_call(
        functools.partial(route_kernel, peers),
        out_shape=(
            shape((peers * rows_each, tokens), BF16),
            shape((peers, TAGS, LANES), BF16),
        ),
        in_specs=[pl.BlockSpec(memory_space=pl.ANY)] + [vmem()] * 2,
        out_specs=(vmem(), vmem()),
        compiler_params=params(4),
        cost_estimate=pl.CostEstimate(flops=0, bytes_accessed=MIB, transcendentals=0),
        name="route",
    )(part, route_experts.T, route_weights.T)
    other = swap_core(part)

    near = peers // 2
    split = [k >= near and (k - near) % 2 == 1 for k in range(peers)]

    def gather(first, last, after):
        return pl.pallas_call(
            functools.partial(gather_kernel, first, split[first:last]),
            out_shape=[
                shape(((2 if split[k] else 4) * tall + TAGS, LANES), BF16)
                for k in range(first, last)
            ],
            in_specs=[pl.BlockSpec(memory_space=pl.ANY)] + [vmem()] * 4,
            out_specs=[vmem()] * (last - first),
            compiler_params=params(8),
            name="gather_rows",
        )(after, part, other, pick, tags)

    def route(k):
        return [
            (e * tp_count + t, (e ^ (2 * k + t % 2)) * tp_count + t)
            for e in range(ep_count)
            for t in range(tp_count)
        ]

    far_send = list(gather(near, peers, tags))
    gate, up, far_send[-1] = lax.optimization_barrier((gate, up, far_send[-1]))
    far = [
        lax.ppermute(x, ("ep", "tp"), route(near + k)) for k, x in enumerate(far_send)
    ]
    gate_pair, up_pair = swap_core(gate), swap_core(up)
    near_send = gather(0, near, gate_pair)
    got = [lax.ppermute(x, ("ep", "tp"), route(k)) for k, x in enumerate(near_send)] + far
    halves = [swap_half(got[k]) for k in range(peers) if split[k]]

    weights = pl.pallas_call(
        stage_kernel,
        out_shape=shape((gate.shape[1], 2 * units), BF16),
        in_specs=[vmem()] + [hbm()] * 4,
        out_specs=vmem(),
        scratch_shapes=[
            pltpu.VMEM((4,) + gate.shape, BF16),
            pltpu.SemaphoreType.DMA((4,)),
        ],
        compiler_params=params(32),
        cost_estimate=pl.CostEstimate(
            flops=0, bytes_accessed=16 * gate.size, transcendentals=0
        ),
        name="stage",
    )(tags, gate, up, gate_pair, up_pair)

    act, side = pl.pallas_call(
        functools.partial(hidden_units_kernel, split, rows_each),
        out_shape=(
            shape((peers * rows_each, units), BF16),
            shape((peers, tall + TAGS, LANES), BF16),
        ),
        in_specs=[vmem()] * (2 + peers + len(halves)),
        out_specs=(vmem(), vmem()),
        compiler_params=params(16),
        name="hidden_units",
    )(norm_gain.reshape(-1, LANES), weights, *got, *halves)

    act_half = swap_half(act)
    act_core = swap_core(act)
    side = swap_core(side)
    act_both = swap_core(act_half)

    chosen = pl.pallas_call(
        functools.partial(select_kernel, peers, top),
        out_shape=shape((tokens, ep_count * rows_each), BF16),
        in_specs=[pl.BlockSpec(memory_space=pltpu.SMEM)] + [vmem()] * (1 + peers),
        out_specs=vmem(),
        compiler_params=params(8),
        cost_estimate=pl.CostEstimate(flops=0, bytes_accessed=MIB, transcendentals=0),
        name="select",
    )(request_order, side, *got)
    result = pl.pallas_call(
        functools.partial(down_kernel, split, rows_each),
        out_shape=shape((ep_count, tall, LANES), BF16),
        in_specs=[pl.BlockSpec(memory_space=pl.ANY), pl.BlockSpec(memory_space=pltpu.SMEM)]
        + [vmem()] * (6 + peers),
        out_specs=vmem(),
        compiler_params=params(16),
        name="down",
    )(chosen, request_order, act, act_half, act_core, act_both, down, side, *got)

    came = lax.all_to_all(result, "ep", split_axis=0, concat_axis=0, tiled=True)
    return pl.pallas_call(
        functools.partial(combine_kernel, rows_each),
        out_shape=shape((tokens, width), BF16),
        in_specs=[vmem()] * 2,
        out_specs=vmem(),
        compiler_params=params(8),
        name="combine",
    )(chosen, came)


def solution(mesh):
    return jax.shard_map(
        shards,
        mesh=mesh,
        in_specs=(
            P("ep", "tp"),
            P("ep", "tp"),
            P("ep", "tp"),
            P("ep", None, "tp"),
            P("ep", None, "tp"),
            P("ep"),
            P(),
            P("ep", "tp"),
            P("tp", None),
            P(),
            P("ep", None),
            P("ep", None),
            P("ep", None, "tp"),
            P("ep", None, "tp"),
            P("ep", None, "tp"),
        ),
        out_specs=P("ep", "tp"),
        check_vma=False,
    )
```

```python
import functools
import math

import jax
import jax.numpy as jnp
from jax import lax
from jax.experimental import pallas as pl
from jax.experimental.pallas import tpu as pltpu
from jax.sharding import PartitionSpec as P

HEAD = 128
QHEADS = 16
KVHEADS = 4
LANES = 128
TAGS = 16
MIB = 1024 * 1024

BF16 = jnp.bfloat16
F32 = jnp.float32


def vmem():
    return pl.BlockSpec(memory_space=pltpu.VMEM)


def hbm():
    return pl.BlockSpec(memory_space=pltpu.HBM)


def params(mib):
    return pltpu.CompilerParams(vmem_limit_bytes=int(mib * MIB))


def dot(a, b):
    return jnp.dot(a, b, preferred_element_type=F32)


def dot_t(a, b):
    return lax.dot_general(a, b, (((1,), (1,)), ((), ())), preferred_element_type=F32)


def begin_kernel(out_ref):
    out_ref[...] = jnp.zeros(out_ref.shape, F32)


def attend_kernel(
    kv_local,
    after_ref,
    length_ref,
    query_ref,
    new_key_ref,
    new_value_ref,
    key_ref,
    value_ref,
    context_ref,
):
    del after_ref
    tokens = query_ref.shape[0]
    group = QHEADS // KVHEADS
    length = length_ref[0]
    scale = 1.0 / math.sqrt(HEAD)
    pieces = []
    for g in range(kv_local):
        columns = slice(g * HEAD, (g + 1) * HEAD)
        rows = jnp.concatenate(
            [
                query_ref[:, (g * group + i) * HEAD : (g * group + i + 1) * HEAD]
                for i in range(group)
            ],
            axis=0,
        )
        old = dot_t(rows, key_ref[:, columns]) * scale
        new = dot_t(rows, new_key_ref[:, columns]) * scale
        position = lax.broadcasted_iota(jnp.int32, old.shape, 1)
        old = jnp.where(position < length, old, -1e30)
        current = lax.broadcasted_iota(jnp.int32, new.shape, 0) % tokens
        position = lax.broadcasted_iota(jnp.int32, new.shape, 1)
        new = jnp.where(position <= current, new, -1e30)
        highest = jnp.maximum(
            jnp.max(old, axis=1, keepdims=True), jnp.max(new, axis=1, keepdims=True)
        )
        old = jnp.exp(old - highest)
        new = jnp.exp(new - highest)
        totals = jnp.sum(old, axis=1, keepdims=True) + jnp.sum(new, axis=1, keepdims=True)
        mixed = dot(old.astype(BF16), value_ref[:, columns]) + dot(
            new.astype(BF16), new_value_ref[:, columns]
        )
        mixed = (mixed / totals).astype(BF16)
        pieces += [mixed[i * tokens : (i + 1) * tokens] for i in range(group)]
    context_ref[...] = jnp.concatenate(pieces, axis=1)


def project_kernel(context_ref, residual_ref, weight_ref, keep_ref, give_ref):
    tp = lax.axis_index("tp")
    half, core = tp // 2, tp % 2
    width = residual_ref.shape[1]
    context = context_ref[...]
    for i, block in enumerate((1 - core, 3 - core, core, core + 2)):
        start = pl.multiple_of(block * width, width)
        part = dot(context, weight_ref[:, pl.ds(start, width)])
        columns = slice((i % 2) * width, (i % 2 + 1) * width)
        if i < 2:
            give_ref[:, columns] = part.astype(BF16)
        else:
            keep_ref[:, columns] = part + jnp.where(
                half == i - 2, residual_ref[...].astype(F32), 0.0
            )


def earlier_tokens(tokens):
    earlier = lax.broadcasted_iota(jnp.int32, (tokens, tokens), 0) < lax.broadcasted_iota(
        jnp.int32, (tokens, tokens), 1
    )
    return jnp.where(earlier, 1.0, 0.0).astype(BF16)


def slot_numbers(named, tokens):
    rank = dot(named.astype(BF16), earlier_tokens(tokens))
    return jnp.where(named > 0.0, rank, -1.0)


def route_kernel(peers, after_ref, expert_ref, weight_ref, pick_ref, tags_ref):
    del after_ref
    me = lax.axis_index("ep")
    core = lax.axis_index("tp") % 2
    top, tokens = expert_ref.shape
    rows_each = pick_ref.shape[0] // peers
    peer = jnp.bitwise_xor(
        2 * lax.broadcasted_iota(jnp.int32, (peers, tokens), 0) + core, me
    )
    weights = weight_ref[...]
    mixing = (weights / jnp.sum(weights, axis=0, keepdims=True)).astype(BF16).astype(F32)
    mix_of = jnp.zeros((peers, tokens), F32)
    named = jnp.zeros((peers, tokens), F32)
    for j in range(top):
        match = expert_ref[j : j + 1, :] == peer
        mix_of = mix_of + jnp.where(match, mixing[j : j + 1, :], 0.0)
        named = named + jnp.where(match, 1.0, 0.0)
    rank = slot_numbers(named, tokens)
    slot = lax.broadcasted_iota(jnp.int32, (rows_each, tokens), 0).astype(F32)
    line = lax.broadcasted_iota(jnp.int32, (TAGS, tokens), 0)
    names = jnp.zeros((TAGS, tokens), F32)
    for j in range(top):
        names = jnp.where(line == j + 1, expert_ref[j : j + 1, :].astype(F32), names)
    tags_ref[...] = jnp.zeros(tags_ref.shape, BF16)
    for k in range(peers):
        pick = jnp.where(rank[k : k + 1, :] == slot, 1.0, 0.0).astype(BF16)
        pick_ref[k * rows_each : (k + 1) * rows_each, :] = pick
        tags_ref[k, :, :tokens] = names.astype(BF16)
        mix = jnp.where(line == 0, mix_of[k : k + 1, :], 0.0).astype(BF16)
        tags_ref[k, :1, :rows_each] = dot_t(mix, pick)[:1].astype(BF16)


def select_kernel(peers, top, order_ref, side_ref, *refs):
    got = refs[:peers]
    chosen_ref = refs[peers]
    me = lax.axis_index("ep")
    core = lax.axis_index("tp") % 2
    tokens = chosen_ref.shape[0]
    experts = 2 * peers
    rows_each = chosen_ref.shape[1] // experts
    names = jnp.zeros((TAGS, LANES), F32)
    for k in range(peers):
        for tags, parity in (
            (got[k][got[k].shape[0] - TAGS :, :], core),
            (side_ref[k, side_ref.shape[1] - TAGS :, :], 1 - core),
        ):
            here = order_ref[jnp.bitwise_xor(me, 2 * k + parity)] == me
            names = names + jnp.where(here, tags.astype(F32), 0.0)
    expert = lax.broadcasted_iota(jnp.int32, (experts, tokens), 0).astype(F32)
    named = jnp.zeros((experts, tokens), F32)
    for j in range(top):
        named = named + jnp.where(names[j + 1 : j + 2, :tokens] == expert, 1.0, 0.0)
    rank = slot_numbers(named, tokens)
    slot = lax.broadcasted_iota(jnp.int32, (rows_each, tokens), 0).astype(F32)
    pick = jnp.concatenate(
        [jnp.where(rank[e : e + 1, :] == slot, 1.0, 0.0) for e in range(experts)], axis=0
    )
    chosen_ref[...] = pick.T.astype(BF16)


def add_core_kernel(keep_ref, came_ref, sum_ref, send_ref):
    value = keep_ref[...] + came_ref[...].astype(F32)
    sum_ref[...] = value
    send_ref[...] = value.astype(BF16)


def add_half_kernel(sum_ref, came_ref, out_ref):
    out_ref[...] = (sum_ref[...] + came_ref[...].astype(F32)).astype(BF16)


def gather_kernel(first, split, after_ref, part_ref, other_ref, pick_ref, tags_ref, *send_refs):
    del after_ref
    tp = lax.axis_index("tp")
    mine, core = tp // 2, tp % 2
    count = len(split)
    rows_each = pick_ref.shape[0] // tags_ref.shape[0]
    pick = pick_ref[first * rows_each : (first + count) * rows_each, :]
    width = part_ref.shape[1] // 2
    blocks = width // LANES
    tall = blocks * rows_each

    def put(ref, rows, base):
        for j in range(blocks):
            start = pl.multiple_of(base + j * rows_each, rows_each)
            ref[pl.ds(start, rows_each), :] = rows[:, j * LANES : (j + 1) * LANES]

    for source, parity in ((part_ref, core), (other_ref, 1 - core)):
        whole = [k for k in range(count) if not split[k]]
        for half in range(2) if whole else ():
            rows = dot(pick, source[:, half * width : (half + 1) * width]).astype(BF16)
            for k in whole:
                piece = rows[k * rows_each : (k + 1) * rows_each]
                put(send_refs[k], piece, (2 * half + parity) * tall)
        for k in range(count):
            if split[k]:
                columns = pl.ds(pl.multiple_of(mine * width, width), width)
                piece = pick[k * rows_each : (k + 1) * rows_each]
                put(send_refs[k], dot(piece, source[:, columns]).astype(BF16), parity * tall)
    for k in range(count):
        send_refs[k][send_refs[k].shape[0] - TAGS :, :] = tags_ref[first + k]


def stage_kernel(after_ref, gate, up, gate_pair, up_pair, out_ref, held_ref, sems):
    del after_ref
    core = lax.axis_index("tp") % 2
    copies = [
        pltpu.make_async_copy(source, held_ref.at[place], sems.at[i])
        for i, (source, place) in enumerate(
            ((gate, core), (up, 2 + core), (gate_pair, 1 - core), (up_pair, 3 - core))
        )
    ]
    for copy in copies:
        copy.start()
    for copy in copies:
        copy.wait()
    units, width = held_ref.shape[1:]
    for j in range(width // LANES):
        columns = slice(j * LANES, (j + 1) * LANES)
        out_ref[columns, :] = held_ref[:, :, columns].reshape(4 * units, LANES).T


def hidden_units_kernel(split, rows_each, gain_ref, weight_ref, *refs):
    peers = len(split)
    got = refs[:peers]
    halves = list(refs[peers:-2])
    act_ref, side_ref = refs[-2:]
    tp = lax.axis_index("tp")
    half, core = tp // 2, tp % 2
    blocks = gain_ref.shape[0]
    tall = blocks // 4 * rows_each

    columns = []
    for ref, parted in zip(got, split):
        if parted:
            own, came = ref[: 2 * tall, :], halves.pop(0)[: 2 * tall, :]
            low = jnp.where(half == 0, own, came)
            high = jnp.where(half == 0, came, own)
            rows = jnp.concatenate([low, high], axis=0)
        else:
            rows = ref[: 4 * tall, :]
        columns.append([rows[j * rows_each : (j + 1) * rows_each] for j in range(blocks)])
    parts = [
        jnp.concatenate([column[j] for column in columns], axis=0).astype(F32)
        for j in range(blocks)
    ]
    squares = parts[0] * parts[0]
    for part in parts[1:]:
        squares = squares + part * part
    mean = jnp.sum(squares, axis=1, keepdims=True) * (1.0 / (blocks * LANES))
    factor = lax.rsqrt(mean + 1e-06)
    normed = jnp.concatenate(
        [(parts[j] * factor * gain_ref[j : j + 1, :]).astype(BF16) for j in range(blocks)], axis=1
    )

    product = dot(normed, weight_ref[...])
    units = act_ref.shape[1]
    gate, up = product[:, :units], product[:, units:]
    act_ref[...] = (gate / (1.0 + jnp.exp(-gate)) * up).astype(BF16)
    for k in range(peers):
        place = 1 - core + (0 if split[k] else 2 * half)
        start = pl.multiple_of(place * tall, tall)
        side_ref[k, :tall, :] = got[k][pl.ds(start, tall), :]
        side_ref[k, tall:, :] = got[k][got[k].shape[0] - TAGS :, :]


def down_kernel(
    split,
    rows_each,
    after_ref,
    order_vmem,
    act_ref,
    act_half_ref,
    act_core_ref,
    act_both_ref,
    down_ref,
    side_ref,
    *refs,
):
    del after_ref
    peers = len(split)
    got = refs[:peers]
    out_ref, order_ref, sem = refs[peers:]
    fetch = pltpu.make_async_copy(order_vmem, order_ref, sem)
    fetch.start()
    tp = lax.axis_index("tp")
    me = lax.axis_index("ep")
    half, core = tp // 2, tp % 2
    units = act_ref.shape[1]
    blocks = down_ref.shape[1] // LANES
    tall = blocks * rows_each
    here = down_ref[pl.ds(pl.multiple_of(half * units, units), units), :]
    there = down_ref[pl.ds(pl.multiple_of((1 - half) * units, units), units), :]
    diagonal = lax.broadcasted_iota(jnp.int32, (rows_each, LANES), 0) == lax.broadcasted_iota(
        jnp.int32, (rows_each, LANES), 1
    )
    outcomes = [
        dot(near[...], here) + dot(far[...], there)
        for near, far in ((act_ref, act_half_ref), (act_core_ref, act_both_ref))
    ]
    fetch.wait()
    for group, result in enumerate(outcomes):
        for k in range(peers):
            request = jnp.bitwise_xor(me, 2 * k + (core if group == 0 else 1 - core))
            place = order_ref[request]
            if group == 0:
                start = pl.multiple_of((core if split[k] else tp) * tall, tall)
                rows = got[k][pl.ds(start, tall), :]
                tags = got[k][got[k].shape[0] - TAGS :, :]
            else:
                rows = side_ref[k, :tall, :]
                tags = side_ref[k, tall:, :]
            mix = jnp.sum(
                jnp.where(diagonal, tags.astype(F32)[0:1, :], 0.0), axis=1, keepdims=True
            )
            for j in range(blocks):
                piece = slice(j * rows_each, (j + 1) * rows_each)
                value = rows[piece].astype(F32) + result[
                    k * rows_each : (k + 1) * rows_each, j * LANES : (j + 1) * LANES
                ]
                out_ref[place, piece, :] = (mix * value).astype(BF16)


def combine_kernel(rows_each, chosen_ref, came_ref, out_ref):
    chosen = chosen_ref[...]
    experts, tall, _ = came_ref.shape
    for j in range(tall // rows_each):
        rows = jnp.concatenate(
            [came_ref[e, j * rows_each : (j + 1) * rows_each, :] for e in range(experts)], axis=0
        )
        out_ref[:, j * LANES : (j + 1) * LANES] = dot(chosen, rows).astype(BF16)


def shards(
    queries,
    new_keys,
    new_values,
    key_cache,
    value_cache,
    cache_lengths,
    request_order,
    residual,
    out_weight,
    norm_gain,
    route_experts,
    route_weights,
    expert_gate,
    expert_up,
    expert_down,
):
    tp_count = lax.axis_size("tp")
    ep_count = lax.axis_size("ep")
    kv_local = KVHEADS // tp_count

    def swap_core(x):
        return lax.ppermute(x, "tp", [(i, i ^ 1) for i in range(tp_count)])

    def swap_half(x):
        return lax.ppermute(x, "tp", [(i, i ^ 2) for i in range(tp_count)])

    gate, up, down = expert_gate[0].T, expert_up[0].T, expert_down[0]
    tokens, top = route_experts.shape
    capacity = 2 * tokens * top // ep_count
    rows_each = -(-capacity // 16) * 16
    peers = ep_count // 2
    width = residual.shape[1]
    blocks = width // LANES
    tall = blocks * rows_each
    units = 2 * gate.shape[0]
    shape = jax.ShapeDtypeStruct

    begun = pl.pallas_call(
        begin_kernel,
        out_shape=shape((8, LANES), F32),
        out_specs=vmem(),
        compiler_params=params(1),
        cost_estimate=pl.CostEstimate(
            flops=20 * 10**9, bytes_accessed=64 * MIB, transcendentals=0
        ),
        name="begin",
    )()
    context = pl.pallas_call(
        functools.partial(attend_kernel, kv_local),
        out_shape=shape(queries.shape, BF16),
        in_specs=[pl.BlockSpec(memory_space=pl.ANY), pl.BlockSpec(memory_space=pltpu.SMEM)]
        + [vmem()] * 5,
        out_specs=vmem(),
        compiler_params=params(16),
        cost_estimate=pl.CostEstimate(
            flops=2 * 10**8, bytes_accessed=MIB // 2, transcendentals=0
        ),
        name="attend",
    )(begun, cache_lengths, queries, new_keys, new_values, key_cache[0], value_cache[0])
    keep, give = pl.pallas_call(
        project_kernel,
        out_shape=(shape((tokens, 2 * width), F32), shape((tokens, 2 * width), BF16)),
        in_specs=[vmem()] * 3,
        out_specs=(vmem(), vmem()),
        compiler_params=params(16),
        name="project",
    )(context, residual, out_weight)

    summed, send = pl.pallas_call(
        add_core_kernel,
        out_shape=(shape(keep.shape, F32), shape(keep.shape, BF16)),
        in_specs=[vmem()] * 2,
        out_specs=(vmem(), vmem()),
        compiler_params=params(4),
        name="add_core",
    )(keep, swap_core(give))

    part = pl.pallas_call(
        add_half_kernel,
        out_shape=shape(keep.shape, BF16),
        in_specs=[vmem()] * 2,
        out_specs=vmem(),
        compiler_params=params(4),
        name="add_half",
    )(summed, swap_half(send))
    pick, tags = pl.pallas_call(
        functools.partial(route_kernel, peers),
        out_shape=(
            shape((peers * rows_each, tokens), BF16),
            shape((peers, TAGS, LANES), BF16),
        ),
        in_specs=[pl.BlockSpec(memory_space=pl.ANY)] + [vmem()] * 2,
        out_specs=(vmem(), vmem()),
        compiler_params=params(4),
        cost_estimate=pl.CostEstimate(flops=0, bytes_accessed=MIB, transcendentals=0),
        name="route",
    )(part, route_experts.T, route_weights.T)
    other = swap_core(part)

    near = peers // 2
    split = [k >= near and (k - near) % 2 == 1 for k in range(peers)]

    def gather(first, last, after):
        return pl.pallas_call(
            functools.partial(gather_kernel, first, split[first:last]),
            out_shape=[
                shape(((2 if split[k] else 4) * tall + TAGS, LANES), BF16)
                for k in range(first, last)
            ],
            in_specs=[pl.BlockSpec(memory_space=pl.ANY)] + [vmem()] * 4,
            out_specs=[vmem()] * (last - first),
            compiler_params=params(8),
            cost_estimate=pl.CostEstimate(
                flops=(20 * 10**9 if first else 0), bytes_accessed=MIB, transcendentals=0
            ),
            name="gather_rows",
        )(after, part, other, pick, tags)

    def route(k):
        return [
            (e * tp_count + t, (e ^ (2 * k + t % 2)) * tp_count + t)
            for e in range(ep_count)
            for t in range(tp_count)
        ]

    far_send = list(gather(near, peers, tags))
    gate, up, tags = lax.optimization_barrier((gate, up, tags))
    far = [
        lax.ppermute(x, ("ep", "tp"), route(near + k)) for k, x in enumerate(far_send)
    ]
    gate_pair, up_pair = swap_core(gate), swap_core(up)
    near_send = gather(0, near, gate_pair)
    got = [lax.ppermute(x, ("ep", "tp"), route(k)) for k, x in enumerate(near_send)] + far
    halves = [swap_half(got[k]) for k in range(peers) if split[k]]

    weights = pl.pallas_call(
        stage_kernel,
        out_shape=shape((gate.shape[1], 2 * units), BF16),
        in_specs=[vmem()] + [hbm()] * 4,
        out_specs=vmem(),
        scratch_shapes=[
            pltpu.VMEM((4,) + gate.shape, BF16),
            pltpu.SemaphoreType.DMA((4,)),
        ],
        compiler_params=params(32),
        cost_estimate=pl.CostEstimate(
            flops=0, bytes_accessed=16 * gate.size, transcendentals=0
        ),
        name="stage",
    )(tags, gate, up, gate_pair, up_pair)

    act, side = pl.pallas_call(
        functools.partial(hidden_units_kernel, split, rows_each),
        out_shape=(
            shape((peers * rows_each, units), BF16),
            shape((peers, tall + TAGS, LANES), BF16),
        ),
        in_specs=[vmem()] * (2 + peers + len(halves)),
        out_specs=(vmem(), vmem()),
        compiler_params=params(16),
        name="hidden_units",
    )(norm_gain.reshape(-1, LANES), weights, *got, *halves)

    act_half = swap_half(act)
    act_core = swap_core(act)
    side = swap_core(side)
    act_both = swap_core(act_half)

    chosen = pl.pallas_call(
        functools.partial(select_kernel, peers, top),
        out_shape=shape((tokens, ep_count * rows_each), BF16),
        in_specs=[pl.BlockSpec(memory_space=pltpu.SMEM)] + [vmem()] * (1 + peers),
        out_specs=vmem(),
        compiler_params=params(8),
        cost_estimate=pl.CostEstimate(flops=0, bytes_accessed=MIB, transcendentals=0),
        name="select",
    )(request_order, side, *got)
    result = pl.pallas_call(
        functools.partial(down_kernel, split, rows_each),
        out_shape=shape((ep_count, tall, LANES), BF16),
        in_specs=[pl.BlockSpec(memory_space=pl.ANY)] + [vmem()] * (7 + peers),
        out_specs=vmem(),
        scratch_shapes=[
            pltpu.SMEM(request_order.shape, jnp.int32),
            pltpu.SemaphoreType.DMA(()),
        ],
        compiler_params=params(16),
        name="down",
    )(chosen, request_order, act, act_half, act_core, act_both, down, side, *got)

    came = lax.all_to_all(result, "ep", split_axis=0, concat_axis=0, tiled=True)
    return pl.pallas_call(
        functools.partial(combine_kernel, rows_each),
        out_shape=shape((tokens, width), BF16),
        in_specs=[vmem()] * 2,
        out_specs=vmem(),
        compiler_params=params(8),
        name="combine",
    )(chosen, came)


def solution(mesh):
    return jax.shard_map(
        shards,
        mesh=mesh,
        in_specs=(
            P("ep", "tp"),
            P("ep", "tp"),
            P("ep", "tp"),
            P("ep", None, "tp"),
            P("ep", None, "tp"),
            P("ep"),
            P(),
            P("ep", "tp"),
            P("tp", None),
            P(),
            P("ep", None),
            P("ep", None),
            P("ep", None, "tp"),
            P("ep", None, "tp"),
            P("ep", None, "tp"),
        ),
        out_specs=P("ep", "tp"),
        check_vma=False,
    )
```

```python
import functools
import math

import jax
import jax.numpy as jnp
from jax import lax
from jax.experimental import pallas as pl
from jax.experimental.pallas import tpu as pltpu
from jax.sharding import PartitionSpec as P

HEAD = 128
QHEADS = 16
KVHEADS = 4
LANES = 128
TAGS = 16
MIB = 1024 * 1024

BF16 = jnp.bfloat16
F32 = jnp.float32


def vmem():
    return pl.BlockSpec(memory_space=pltpu.VMEM)


def hbm():
    return pl.BlockSpec(memory_space=pltpu.HBM)


def params(mib):
    return pltpu.CompilerParams(vmem_limit_bytes=int(mib * MIB))


def dot(a, b):
    return jnp.dot(a, b, preferred_element_type=F32)


def dot_t(a, b):
    return lax.dot_general(a, b, (((1,), (1,)), ((), ())), preferred_element_type=F32)


def begin_kernel(out_ref):
    out_ref[...] = jnp.zeros(out_ref.shape, F32)


def attend_kernel(
    kv_local,
    after_ref,
    length_ref,
    query_ref,
    new_key_ref,
    new_value_ref,
    key_ref,
    value_ref,
    context_ref,
):
    del after_ref
    tokens = query_ref.shape[0]
    group = QHEADS // KVHEADS
    length = length_ref[0]
    scale = 1.0 / math.sqrt(HEAD)
    pieces = []
    for g in range(kv_local):
        columns = slice(g * HEAD, (g + 1) * HEAD)
        rows = jnp.concatenate(
            [
                query_ref[:, (g * group + i) * HEAD : (g * group + i + 1) * HEAD]
                for i in range(group)
            ],
            axis=0,
        )
        old = dot_t(rows, key_ref[:, columns]) * scale
        new = dot_t(rows, new_key_ref[:, columns]) * scale
        position = lax.broadcasted_iota(jnp.int32, old.shape, 1)
        old = jnp.where(position < length, old, -1e30)
        current = lax.broadcasted_iota(jnp.int32, new.shape, 0) % tokens
        position = lax.broadcasted_iota(jnp.int32, new.shape, 1)
        new = jnp.where(position <= current, new, -1e30)
        highest = jnp.maximum(
            jnp.max(old, axis=1, keepdims=True), jnp.max(new, axis=1, keepdims=True)
        )
        old = jnp.exp(old - highest)
        new = jnp.exp(new - highest)
        totals = jnp.sum(old, axis=1, keepdims=True) + jnp.sum(new, axis=1, keepdims=True)
        mixed = dot(old.astype(BF16), value_ref[:, columns]) + dot(
            new.astype(BF16), new_value_ref[:, columns]
        )
        mixed = (mixed / totals).astype(BF16)
        pieces += [mixed[i * tokens : (i + 1) * tokens] for i in range(group)]
    context_ref[...] = jnp.concatenate(pieces, axis=1)


def give_kernel(context_ref, weight_ref, give_ref):
    core = lax.axis_index("tp") % 2
    width = context_ref.shape[1]
    context = context_ref[...]
    for i in range(2):
        start = pl.multiple_of((2 * i + 1 - core) * width, width)
        part = dot(context, weight_ref[:, pl.ds(start, width)])
        give_ref[:, i * width : (i + 1) * width] = part.astype(BF16)


def keep_kernel(after_ref, context_ref, residual_ref, weight_ref, keep_ref):
    del after_ref
    tp = lax.axis_index("tp")
    half, core = tp // 2, tp % 2
    width = context_ref.shape[1]
    context = context_ref[...]
    for i in range(2):
        start = pl.multiple_of((2 * i + core) * width, width)
        part = dot(context, weight_ref[:, pl.ds(start, width)])
        keep_ref[:, i * width : (i + 1) * width] = part + jnp.where(
            half == i, residual_ref[...].astype(F32), 0.0
        )


def step(k, peers):
    near = peers // 2
    return near - 1 - k if k < near else k


def earlier_tokens(tokens):
    earlier = lax.broadcasted_iota(jnp.int32, (tokens, tokens), 0) < lax.broadcasted_iota(
        jnp.int32, (tokens, tokens), 1
    )
    return jnp.where(earlier, 1.0, 0.0).astype(BF16)


def slot_numbers(named, tokens):
    rank = dot(named.astype(BF16), earlier_tokens(tokens))
    return jnp.where(named > 0.0, rank, -1.0)


def route_kernel(peers, after_ref, expert_ref, weight_ref, pick_ref, tags_ref):
    del after_ref
    me = lax.axis_index("ep")
    core = lax.axis_index("tp") % 2
    top, tokens = expert_ref.shape
    rows_each = pick_ref.shape[0] // peers
    number = lax.broadcasted_iota(jnp.int32, (peers, tokens), 0)
    near = peers // 2
    peer = jnp.bitwise_xor(2 * jnp.where(number < near, near - 1 - number, number) + core, me)
    weights = weight_ref[...]
    mixing = (weights / jnp.sum(weights, axis=0, keepdims=True)).astype(BF16).astype(F32)
    mix_of = jnp.zeros((peers, tokens), F32)
    named = jnp.zeros((peers, tokens), F32)
    for j in range(top):
        match = expert_ref[j : j + 1, :] == peer
        mix_of = mix_of + jnp.where(match, mixing[j : j + 1, :], 0.0)
        named = named + jnp.where(match, 1.0, 0.0)
    rank = slot_numbers(named, tokens)
    slot = lax.broadcasted_iota(jnp.int32, (rows_each, tokens), 0).astype(F32)
    line = lax.broadcasted_iota(jnp.int32, (TAGS, tokens), 0)
    names = jnp.zeros((TAGS, tokens), F32)
    for j in range(top):
        names = jnp.where(line == j + 1, expert_ref[j : j + 1, :].astype(F32), names)
    tags_ref[...] = jnp.zeros(tags_ref.shape, BF16)
    for k in range(peers):
        pick = jnp.where(rank[k : k + 1, :] == slot, 1.0, 0.0).astype(BF16)
        pick_ref[k * rows_each : (k + 1) * rows_each, :] = pick
        tags_ref[k, :, :tokens] = names.astype(BF16)
        mix = jnp.where(line == 0, mix_of[k : k + 1, :], 0.0).astype(BF16)
        tags_ref[k, :1, :rows_each] = dot_t(mix, pick)[:1].astype(BF16)


def select_kernel(peers, top, order_ref, side_ref, *refs):
    got = refs[:peers]
    chosen_ref = refs[peers]
    me = lax.axis_index("ep")
    core = lax.axis_index("tp") % 2
    tokens = chosen_ref.shape[0]
    experts = 2 * peers
    rows_each = chosen_ref.shape[1] // experts
    names = jnp.zeros((TAGS, LANES), F32)
    for k in range(peers):
        for tags, parity in (
            (got[k][got[k].shape[0] - TAGS :, :], core),
            (side_ref[k, side_ref.shape[1] - TAGS :, :], 1 - core),
        ):
            here = order_ref[jnp.bitwise_xor(me, 2 * step(k, peers) + parity)] == me
            names = names + jnp.where(here, tags.astype(F32), 0.0)
    expert = lax.broadcasted_iota(jnp.int32, (experts, tokens), 0).astype(F32)
    named = jnp.zeros((experts, tokens), F32)
    for j in range(top):
        named = named + jnp.where(names[j + 1 : j + 2, :tokens] == expert, 1.0, 0.0)
    rank = slot_numbers(named, tokens)
    slot = lax.broadcasted_iota(jnp.int32, (rows_each, tokens), 0).astype(F32)
    pick = jnp.concatenate(
        [jnp.where(rank[e : e + 1, :] == slot, 1.0, 0.0) for e in range(experts)], axis=0
    )
    chosen_ref[...] = pick.T.astype(BF16)


def add_core_kernel(keep_ref, came_ref, sum_ref, send_ref):
    value = keep_ref[...] + came_ref[...].astype(F32)
    sum_ref[...] = value
    send_ref[...] = value.astype(BF16)


def add_half_kernel(sum_ref, came_ref, out_ref):
    out_ref[...] = (sum_ref[...] + came_ref[...].astype(F32)).astype(BF16)


def gather_kernel(members, split, after_ref, part_ref, other_ref, pick_ref, tags_ref, *send_refs):
    del after_ref
    tp = lax.axis_index("tp")
    mine, core = tp // 2, tp % 2
    count = len(members)
    rows_each = pick_ref.shape[0] // tags_ref.shape[0]
    pick = jnp.concatenate(
        [pick_ref[k * rows_each : (k + 1) * rows_each, :] for k in members], axis=0
    )
    width = part_ref.shape[1] // 2
    blocks = width // LANES
    tall = blocks * rows_each

    def put(ref, rows, base):
        for j in range(blocks):
            start = pl.multiple_of(base + j * rows_each, rows_each)
            ref[pl.ds(start, rows_each), :] = rows[:, j * LANES : (j + 1) * LANES]

    for source, parity in ((part_ref, core), (other_ref, 1 - core)):
        whole = [k for k in range(count) if not split[k]]
        for half in range(2) if whole else ():
            rows = dot(pick, source[:, half * width : (half + 1) * width]).astype(BF16)
            for k in whole:
                piece = rows[k * rows_each : (k + 1) * rows_each]
                put(send_refs[k], piece, (2 * half + parity) * tall)
        for k in range(count):
            if split[k]:
                columns = pl.ds(pl.multiple_of(mine * width, width), width)
                piece = pick[k * rows_each : (k + 1) * rows_each]
                put(send_refs[k], dot(piece, source[:, columns]).astype(BF16), parity * tall)
    for k in range(count):
        send_refs[k][send_refs[k].shape[0] - TAGS :, :] = tags_ref[members[k]]


def stage_kernel(after_ref, gate, up, gate_pair, up_pair, out_ref, held_ref, sems):
    del after_ref
    core = lax.axis_index("tp") % 2
    copies = [
        pltpu.make_async_copy(source, held_ref.at[place], sems.at[i])
        for i, (source, place) in enumerate(
            ((gate, core), (up, 2 + core), (gate_pair, 1 - core), (up_pair, 3 - core))
        )
    ]
    for copy in copies:
        copy.start()
    for copy in copies:
        copy.wait()
    units, width = held_ref.shape[1:]
    for j in range(width // LANES):
        columns = slice(j * LANES, (j + 1) * LANES)
        out_ref[columns, :] = held_ref[:, :, columns].reshape(4 * units, LANES).T


def hidden_units_kernel(split, rows_each, gain_ref, weight_ref, *refs):
    peers = len(split)
    got = refs[:peers]
    halves = list(refs[peers:-2])
    act_ref, side_ref = refs[-2:]
    tp = lax.axis_index("tp")
    half, core = tp // 2, tp % 2
    blocks = gain_ref.shape[0]
    tall = blocks // 4 * rows_each

    columns = []
    for ref, parted in zip(got, split):
        if parted:
            own, came = ref[: 2 * tall, :], halves.pop(0)[: 2 * tall, :]
            low = jnp.where(half == 0, own, came)
            high = jnp.where(half == 0, came, own)
            rows = jnp.concatenate([low, high], axis=0)
        else:
            rows = ref[: 4 * tall, :]
        columns.append([rows[j * rows_each : (j + 1) * rows_each] for j in range(blocks)])
    parts = [
        jnp.concatenate([column[j] for column in columns], axis=0).astype(F32)
        for j in range(blocks)
    ]
    squares = parts[0] * parts[0]
    for part in parts[1:]:
        squares = squares + part * part
    mean = jnp.sum(squares, axis=1, keepdims=True) * (1.0 / (blocks * LANES))
    factor = lax.rsqrt(mean + 1e-06)
    normed = jnp.concatenate(
        [(parts[j] * factor * gain_ref[j : j + 1, :]).astype(BF16) for j in range(blocks)], axis=1
    )

    product = dot(normed, weight_ref[...])
    units = act_ref.shape[1]
    gate, up = product[:, :units], product[:, units:]
    act_ref[...] = (gate / (1.0 + jnp.exp(-gate)) * up).astype(BF16)
    for k in range(peers):
        place = 1 - core + (0 if split[k] else 2 * half)
        start = pl.multiple_of(place * tall, tall)
        side_ref[k, :tall, :] = got[k][pl.ds(start, tall), :]
        side_ref[k, tall:, :] = got[k][got[k].shape[0] - TAGS :, :]


def down_kernel(
    split,
    rows_each,
    after_ref,
    order_vmem,
    act_ref,
    act_half_ref,
    act_core_ref,
    act_both_ref,
    down_ref,
    side_ref,
    *refs,
):
    del after_ref
    peers = len(split)
    got = refs[:peers]
    out_ref, order_ref, sem = refs[peers:]
    fetch = pltpu.make_async_copy(order_vmem, order_ref, sem)
    fetch.start()
    tp = lax.axis_index("tp")
    me = lax.axis_index("ep")
    half, core = tp // 2, tp % 2
    units = act_ref.shape[1]
    blocks = down_ref.shape[1] // LANES
    tall = blocks * rows_each
    here = down_ref[pl.ds(pl.multiple_of(half * units, units), units), :]
    there = down_ref[pl.ds(pl.multiple_of((1 - half) * units, units), units), :]
    diagonal = lax.broadcasted_iota(jnp.int32, (rows_each, LANES), 0) == lax.broadcasted_iota(
        jnp.int32, (rows_each, LANES), 1
    )
    outcomes = [
        dot(near[...], here) + dot(far[...], there)
        for near, far in ((act_ref, act_half_ref), (act_core_ref, act_both_ref))
    ]
    fetch.wait()
    for group, result in enumerate(outcomes):
        for k in range(peers):
            request = jnp.bitwise_xor(
                me, 2 * step(k, peers) + (core if group == 0 else 1 - core)
            )
            place = order_ref[request]
            if group == 0:
                start = pl.multiple_of((core if split[k] else tp) * tall, tall)
                rows = got[k][pl.ds(start, tall), :]
                tags = got[k][got[k].shape[0] - TAGS :, :]
            else:
                rows = side_ref[k, :tall, :]
                tags = side_ref[k, tall:, :]
            mix = jnp.sum(
                jnp.where(diagonal, tags.astype(F32)[0:1, :], 0.0), axis=1, keepdims=True
            )
            for j in range(blocks):
                piece = slice(j * rows_each, (j + 1) * rows_each)
                value = rows[piece].astype(F32) + result[
                    k * rows_each : (k + 1) * rows_each, j * LANES : (j + 1) * LANES
                ]
                out_ref[place, piece, :] = (mix * value).astype(BF16)


def combine_kernel(rows_each, chosen_ref, came_ref, out_ref):
    chosen = chosen_ref[...]
    experts, tall, _ = came_ref.shape
    for j in range(tall // rows_each):
        rows = jnp.concatenate(
            [came_ref[e, j * rows_each : (j + 1) * rows_each, :] for e in range(experts)], axis=0
        )
        out_ref[:, j * LANES : (j + 1) * LANES] = dot(chosen, rows).astype(BF16)


def shards(
    queries,
    new_keys,
    new_values,
    key_cache,
    value_cache,
    cache_lengths,
    request_order,
    residual,
    out_weight,
    norm_gain,
    route_experts,
    route_weights,
    expert_gate,
    expert_up,
    expert_down,
):
    tp_count = lax.axis_size("tp")
    ep_count = lax.axis_size("ep")
    kv_local = KVHEADS // tp_count

    def swap_core(x):
        return lax.ppermute(x, "tp", [(i, i ^ 1) for i in range(tp_count)])

    def swap_half(x):
        return lax.ppermute(x, "tp", [(i, i ^ 2) for i in range(tp_count)])

    gate, up, down = expert_gate[0].T, expert_up[0].T, expert_down[0]
    tokens, top = route_experts.shape
    capacity = 2 * tokens * top // ep_count
    rows_each = -(-capacity // 16) * 16
    peers = ep_count // 2
    width = residual.shape[1]
    blocks = width // LANES
    tall = blocks * rows_each
    units = 2 * gate.shape[0]
    shape = jax.ShapeDtypeStruct

    begun = pl.pallas_call(
        begin_kernel,
        out_shape=shape((8, LANES), F32),
        out_specs=vmem(),
        compiler_params=params(1),
        cost_estimate=pl.CostEstimate(
            flops=20 * 10**9, bytes_accessed=64 * MIB, transcendentals=0
        ),
        name="begin",
    )()
    context = pl.pallas_call(
        functools.partial(attend_kernel, kv_local),
        out_shape=shape(queries.shape, BF16),
        in_specs=[pl.BlockSpec(memory_space=pl.ANY), pl.BlockSpec(memory_space=pltpu.SMEM)]
        + [vmem()] * 5,
        out_specs=vmem(),
        compiler_params=params(16),
        cost_estimate=pl.CostEstimate(
            flops=2 * 10**8, bytes_accessed=MIB // 2, transcendentals=0
        ),
        name="attend",
    )(begun, cache_lengths, queries, new_keys, new_values, key_cache[0], value_cache[0])
    give = pl.pallas_call(
        give_kernel,
        out_shape=shape((tokens, 2 * width), BF16),
        in_specs=[vmem()] * 2,
        out_specs=vmem(),
        compiler_params=params(16),
        name="project_given",
    )(context, out_weight)
    keep = pl.pallas_call(
        keep_kernel,
        out_shape=shape((tokens, 2 * width), F32),
        in_specs=[pl.BlockSpec(memory_space=pl.ANY)] + [vmem()] * 3,
        out_specs=vmem(),
        compiler_params=params(16),
        cost_estimate=pl.CostEstimate(flops=0, bytes_accessed=2 * MIB, transcendentals=0),
        name="project_kept",
    )(give, context, residual, out_weight)

    summed, send = pl.pallas_call(
        add_core_kernel,
        out_shape=(shape(keep.shape, F32), shape(keep.shape, BF16)),
        in_specs=[vmem()] * 2,
        out_specs=(vmem(), vmem()),
        compiler_params=params(4),
        name="add_core",
    )(keep, swap_core(give))

    part = pl.pallas_call(
        add_half_kernel,
        out_shape=shape(keep.shape, BF16),
        in_specs=[vmem()] * 2,
        out_specs=vmem(),
        compiler_params=params(4),
        name="add_half",
    )(summed, swap_half(send))
    pick, tags = pl.pallas_call(
        functools.partial(route_kernel, peers),
        out_shape=(
            shape((peers * rows_each, tokens), BF16),
            shape((peers, TAGS, LANES), BF16),
        ),
        in_specs=[pl.BlockSpec(memory_space=pl.ANY)] + [vmem()] * 2,
        out_specs=(vmem(), vmem()),
        compiler_params=params(4),
        cost_estimate=pl.CostEstimate(flops=0, bytes_accessed=MIB, transcendentals=0),
        name="route",
    )(part, route_experts.T, route_weights.T)
    other = swap_core(part)

    near = peers // 2
    split = [k >= near and (k - near) % 2 == 1 for k in range(peers)]

    def gather(members, after):
        sent = pl.pallas_call(
            functools.partial(gather_kernel, members, [split[k] for k in members]),
            out_shape=[
                shape(((2 if split[k] else 4) * tall + TAGS, LANES), BF16) for k in members
            ],
            in_specs=[pl.BlockSpec(memory_space=pl.ANY)] + [vmem()] * 4,
            out_specs=[vmem()] * len(members),
            compiler_params=params(8),
            cost_estimate=pl.CostEstimate(
                flops=(20 * 10**9 if members[0] >= near else 0),
                bytes_accessed=MIB,
                transcendentals=0,
            ),
            name="gather_rows",
        )(after, part, other, pick, tags)
        return dict(zip(members, sent))

    def route(k):
        return [
            (e * tp_count + t, (e ^ (2 * step(k, peers) + t % 2)) * tp_count + t)
            for e in range(ep_count)
            for t in range(tp_count)
        ]

    send = gather(list(reversed(range(near, peers))), tags)
    gate, up, tags = lax.optimization_barrier((gate, up, tags))
    gate_pair, up_pair = swap_core(gate), swap_core(up)
    early = near // 2
    send.update(gather(list(range(early, near)), up_pair))
    send.update(gather(list(range(early)), gate_pair))
    got = [lax.ppermute(send[k], ("ep", "tp"), route(k)) for k in range(peers)]
    halves = [swap_half(got[k]) for k in range(peers) if split[k]]

    weights = pl.pallas_call(
        stage_kernel,
        out_shape=shape((gate.shape[1], 2 * units), BF16),
        in_specs=[vmem()] + [hbm()] * 4,
        out_specs=vmem(),
        scratch_shapes=[
            pltpu.VMEM((4,) + gate.shape, BF16),
            pltpu.SemaphoreType.DMA((4,)),
        ],
        compiler_params=params(32),
        cost_estimate=pl.CostEstimate(
            flops=0, bytes_accessed=16 * gate.size, transcendentals=0
        ),
        name="stage",
    )(tags, gate, up, gate_pair, up_pair)

    act, side = pl.pallas_call(
        functools.partial(hidden_units_kernel, split, rows_each),
        out_shape=(
            shape((peers * rows_each, units), BF16),
            shape((peers, tall + TAGS, LANES), BF16),
        ),
        in_specs=[vmem()] * (2 + peers + len(halves)),
        out_specs=(vmem(), vmem()),
        compiler_params=params(16),
        name="hidden_units",
    )(norm_gain.reshape(-1, LANES), weights, *got, *halves)

    act_half = swap_half(act)
    act_core = swap_core(act)
    side = swap_core(side)
    act_both = swap_core(act_half)

    chosen = pl.pallas_call(
        functools.partial(select_kernel, peers, top),
        out_shape=shape((tokens, ep_count * rows_each), BF16),
        in_specs=[pl.BlockSpec(memory_space=pltpu.SMEM)] + [vmem()] * (1 + peers),
        out_specs=vmem(),
        compiler_params=params(8),
        cost_estimate=pl.CostEstimate(flops=0, bytes_accessed=MIB, transcendentals=0),
        name="select",
    )(request_order, side, *got)
    result = pl.pallas_call(
        functools.partial(down_kernel, split, rows_each),
        out_shape=shape((ep_count, tall, LANES), BF16),
        in_specs=[pl.BlockSpec(memory_space=pl.ANY)] + [vmem()] * (7 + peers),
        out_specs=vmem(),
        scratch_shapes=[
            pltpu.SMEM(request_order.shape, jnp.int32),
            pltpu.SemaphoreType.DMA(()),
        ],
        compiler_params=params(16),
        name="down",
    )(chosen, request_order, act, act_half, act_core, act_both, down, side, *got)

    came = lax.all_to_all(result, "ep", split_axis=0, concat_axis=0, tiled=True)
    return pl.pallas_call(
        functools.partial(combine_kernel, rows_each),
        out_shape=shape((tokens, width), BF16),
        in_specs=[vmem()] * 2,
        out_specs=vmem(),
        compiler_params=params(8),
        name="combine",
    )(chosen, came)


def solution(mesh):
    return jax.shard_map(
        shards,
        mesh=mesh,
        in_specs=(
            P("ep", "tp"),
            P("ep", "tp"),
            P("ep", "tp"),
            P("ep", None, "tp"),
            P("ep", None, "tp"),
            P("ep"),
            P(),
            P("ep", "tp"),
            P("tp", None),
            P(),
            P("ep", None),
            P("ep", None),
            P("ep", None, "tp"),
            P("ep", None, "tp"),
            P("ep", None, "tp"),
        ),
        out_specs=P("ep", "tp"),
        check_vma=False,
    )
```

```python
import functools
import math

import jax
import jax.numpy as jnp
from jax import lax
from jax.experimental import pallas as pl
from jax.experimental.pallas import tpu as pltpu
from jax.sharding import PartitionSpec as P

HEAD = 128
QHEADS = 16
KVHEADS = 4
LANES = 128
TAGS = 16
MIB = 1024 * 1024

BF16 = jnp.bfloat16
F32 = jnp.float32


def vmem():
    return pl.BlockSpec(memory_space=pltpu.VMEM)


def hbm():
    return pl.BlockSpec(memory_space=pltpu.HBM)


def params(mib):
    return pltpu.CompilerParams(vmem_limit_bytes=int(mib * MIB))


def dot(a, b):
    return jnp.dot(a, b, preferred_element_type=F32)


def dot_t(a, b):
    return lax.dot_general(a, b, (((1,), (1,)), ((), ())), preferred_element_type=F32)


def begin_kernel(out_ref):
    out_ref[...] = jnp.zeros(out_ref.shape, F32)


def attend_kernel(
    kv_local,
    after_ref,
    length_ref,
    query_ref,
    new_key_ref,
    new_value_ref,
    key_ref,
    value_ref,
    context_ref,
):
    del after_ref
    tokens = query_ref.shape[0]
    group = QHEADS // KVHEADS
    length = length_ref[0]
    scale = 1.0 / math.sqrt(HEAD)
    pieces = []
    for g in range(kv_local):
        columns = slice(g * HEAD, (g + 1) * HEAD)
        rows = jnp.concatenate(
            [
                query_ref[:, (g * group + i) * HEAD : (g * group + i + 1) * HEAD]
                for i in range(group)
            ],
            axis=0,
        )
        old = dot_t(rows, key_ref[:, columns]) * scale
        new = dot_t(rows, new_key_ref[:, columns]) * scale
        position = lax.broadcasted_iota(jnp.int32, old.shape, 1)
        old = jnp.where(position < length, old, -1e30)
        current = lax.broadcasted_iota(jnp.int32, new.shape, 0) % tokens
        position = lax.broadcasted_iota(jnp.int32, new.shape, 1)
        new = jnp.where(position <= current, new, -1e30)
        highest = jnp.maximum(
            jnp.max(old, axis=1, keepdims=True), jnp.max(new, axis=1, keepdims=True)
        )
        old = jnp.exp(old - highest)
        new = jnp.exp(new - highest)
        totals = jnp.sum(old, axis=1, keepdims=True) + jnp.sum(new, axis=1, keepdims=True)
        mixed = dot(old.astype(BF16), value_ref[:, columns]) + dot(
            new.astype(BF16), new_value_ref[:, columns]
        )
        mixed = (mixed / totals).astype(BF16)
        pieces += [mixed[i * tokens : (i + 1) * tokens] for i in range(group)]
    context_ref[...] = jnp.concatenate(pieces, axis=1)


def give_kernel(context_ref, weight_ref, give_ref):
    core = lax.axis_index("tp") % 2
    width = context_ref.shape[1]
    context = context_ref[...]
    for i in range(2):
        start = pl.multiple_of((2 * i + 1 - core) * width, width)
        part = dot(context, weight_ref[:, pl.ds(start, width)])
        give_ref[:, i * width : (i + 1) * width] = part.astype(BF16)


def keep_kernel(after_ref, context_ref, residual_ref, weight_ref, keep_ref):
    del after_ref
    tp = lax.axis_index("tp")
    half, core = tp // 2, tp % 2
    width = context_ref.shape[1]
    context = context_ref[...]
    for i in range(2):
        start = pl.multiple_of((2 * i + core) * width, width)
        part = dot(context, weight_ref[:, pl.ds(start, width)])
        keep_ref[:, i * width : (i + 1) * width] = part + jnp.where(
            half == i, residual_ref[...].astype(F32), 0.0
        )


def step(k, peers):
    near = peers // 2
    if isinstance(k, int):
        return near - 1 - k if k < near else k
    return jnp.where(k < near, near - 1 - k, k)


def peer_numbers(peers, tokens):
    number = lax.broadcasted_iota(jnp.int32, (peers, tokens), 0)
    near = peers // 2
    steps = jnp.where(number < near, near - 1 - number, number)
    return jnp.bitwise_xor(2 * steps + lax.axis_index("tp") % 2, lax.axis_index("ep"))


def earlier_tokens(tokens):
    earlier = lax.broadcasted_iota(jnp.int32, (tokens, tokens), 0) < lax.broadcasted_iota(
        jnp.int32, (tokens, tokens), 1
    )
    return jnp.where(earlier, 1.0, 0.0).astype(BF16)


def slot_numbers(named, tokens):
    rank = dot(named.astype(BF16), earlier_tokens(tokens))
    return jnp.where(named > 0.0, rank, -1.0)


def route_kernel(peers, after_ref, expert_ref, weight_ref, pick_ref, tags_ref):
    del after_ref
    top, tokens = expert_ref.shape
    rows_each = pick_ref.shape[0] // peers
    peer = peer_numbers(peers, tokens)
    weights = weight_ref[...]
    mixing = (weights / jnp.sum(weights, axis=0, keepdims=True)).astype(BF16).astype(F32)
    mix_of = jnp.zeros((peers, tokens), F32)
    named = jnp.zeros((peers, tokens), F32)
    for j in range(top):
        match = expert_ref[j : j + 1, :] == peer
        mix_of = mix_of + jnp.where(match, mixing[j : j + 1, :], 0.0)
        named = named + jnp.where(match, 1.0, 0.0)
    rank = slot_numbers(named, tokens)
    slot = lax.broadcasted_iota(jnp.int32, (rows_each, tokens), 0).astype(F32)
    line = lax.broadcasted_iota(jnp.int32, (TAGS, tokens), 0)
    names = jnp.zeros((TAGS, tokens), F32)
    for j in range(top):
        names = jnp.where(line == j + 1, expert_ref[j : j + 1, :].astype(F32), names)
    tags_ref[...] = jnp.zeros(tags_ref.shape, BF16)
    for k in range(peers):
        pick = jnp.where(rank[k : k + 1, :] == slot, 1.0, 0.0).astype(BF16)
        pick_ref[k * rows_each : (k + 1) * rows_each, :] = pick
        tags_ref[k, :, :tokens] = names.astype(BF16)
        mix = jnp.where(line == 0, mix_of[k : k + 1, :], 0.0).astype(BF16)
        tags_ref[k, :1, :rows_each] = dot_t(mix, pick)[:1].astype(BF16)


def select_kernel(
    top,
    order_ref,
    side_ref,
    side_core_ref,
    chosen_ref,
    swap_ref,
    rows_ref,
    mix_ref,
    inverse_ref,
):
    me = lax.axis_index("ep")
    core = lax.axis_index("tp") % 2
    tokens = chosen_ref.shape[0]
    peers = side_ref.shape[0]
    rows_each = chosen_ref.shape[1] // peers
    names = jnp.zeros((TAGS, LANES), F32)
    for k in range(peers):
        for ref, parity in ((side_ref, core), (side_core_ref, 1 - core)):
            here = order_ref[jnp.bitwise_xor(me, 2 * step(k, peers) + parity)] == me
            tags = ref[k, ref.shape[1] - TAGS :, :].astype(F32)
            names = names + jnp.where(here, tags, 0.0)
    expert = peer_numbers(peers, tokens).astype(F32)
    named = jnp.zeros((peers, tokens), F32)
    for j in range(top):
        named = named + jnp.where(names[j + 1 : j + 2, :tokens] == expert, 1.0, 0.0)
    rank = slot_numbers(named, tokens)
    slot = lax.broadcasted_iota(jnp.int32, (rows_each, tokens), 0).astype(F32)
    pick = jnp.concatenate(
        [jnp.where(rank[k : k + 1, :] == slot, 1.0, 0.0) for k in range(peers)], axis=0
    )
    chosen_ref[...] = pick.T.astype(BF16)

    def place(s, carry):
        inverse_ref[order_ref[s]] = s
        return carry

    lax.fori_loop(0, order_ref.shape[0], place, 0)
    height = rows_ref.shape[1]
    diagonal = lax.broadcasted_iota(jnp.int32, (rows_each, LANES), 0) == lax.broadcasted_iota(
        jnp.int32, (rows_each, LANES), 1
    )
    row = lax.broadcasted_iota(jnp.int32, (rows_each, swap_ref.shape[1]), 0)
    column = lax.broadcasted_iota(jnp.int32, (rows_each, swap_ref.shape[1]), 1)
    for k in range(peers):
        offset = jnp.bitwise_xor(
            inverse_ref[jnp.bitwise_xor(me, 2 * step(k, peers) + core)], me
        )
        index = step(offset // 2, peers)
        mine = offset % 2 == core
        block = jnp.where(mine, side_ref[index], side_core_ref[index])
        rows_ref[k] = block[:height]
        tags = block[height:].astype(F32)[0:1, :]
        mix = jnp.sum(jnp.where(diagonal, tags, 0.0), axis=1, keepdims=True)
        span = slice(k * rows_each, (k + 1) * rows_each)
        mix_ref[span, :] = jnp.broadcast_to(mix, (rows_each, LANES))
        base = (index + jnp.where(mine, 0, peers)) * rows_each
        swap_ref[span, :] = jnp.where(column == base + row, 1.0, 0.0).astype(BF16)


def add_core_kernel(keep_ref, came_ref, sum_ref, send_ref):
    value = keep_ref[...] + came_ref[...].astype(F32)
    sum_ref[...] = value
    send_ref[...] = value.astype(BF16)


def add_half_kernel(sum_ref, came_ref, out_ref):
    out_ref[...] = (sum_ref[...] + came_ref[...].astype(F32)).astype(BF16)


def gather_kernel(members, split, after_ref, part_ref, other_ref, pick_ref, tags_ref, *send_refs):
    del after_ref
    tp = lax.axis_index("tp")
    mine, core = tp // 2, tp % 2
    count = len(members)
    rows_each = pick_ref.shape[0] // tags_ref.shape[0]
    pick = jnp.concatenate(
        [pick_ref[k * rows_each : (k + 1) * rows_each, :] for k in members], axis=0
    )
    width = part_ref.shape[1] // 2
    blocks = width // LANES
    tall = blocks * rows_each

    def put(ref, rows, base):
        for j in range(blocks):
            start = pl.multiple_of(base + j * rows_each, rows_each)
            ref[pl.ds(start, rows_each), :] = rows[:, j * LANES : (j + 1) * LANES]

    for source, parity in ((part_ref, core), (other_ref, 1 - core)):
        whole = [k for k in range(count) if not split[k]]
        for half in range(2) if whole else ():
            rows = dot(pick, source[:, half * width : (half + 1) * width]).astype(BF16)
            for k in whole:
                piece = rows[k * rows_each : (k + 1) * rows_each]
                put(send_refs[k], piece, (2 * half + parity) * tall)
        for k in range(count):
            if split[k]:
                columns = pl.ds(pl.multiple_of(mine * width, width), width)
                piece = pick[k * rows_each : (k + 1) * rows_each]
                put(send_refs[k], dot(piece, source[:, columns]).astype(BF16), parity * tall)
    for k in range(count):
        send_refs[k][send_refs[k].shape[0] - TAGS :, :] = tags_ref[members[k]]


def stage_kernel(after_ref, gate, up, gate_pair, up_pair, out_ref, held_ref, sems):
    del after_ref
    core = lax.axis_index("tp") % 2
    copies = [
        pltpu.make_async_copy(source, held_ref.at[place], sems.at[i])
        for i, (source, place) in enumerate(
            ((gate, core), (up, 2 + core), (gate_pair, 1 - core), (up_pair, 3 - core))
        )
    ]
    for copy in copies:
        copy.start()
    for copy in copies:
        copy.wait()
    units, width = held_ref.shape[1:]
    for j in range(width // LANES):
        columns = slice(j * LANES, (j + 1) * LANES)
        out_ref[columns, :] = held_ref[:, :, columns].reshape(4 * units, LANES).T


def hidden_units_kernel(split, rows_each, gain_ref, weight_ref, *refs):
    peers = len(split)
    got = refs[:peers]
    halves = list(refs[peers:-2])
    act_ref, side_ref = refs[-2:]
    tp = lax.axis_index("tp")
    half, core = tp // 2, tp % 2
    blocks = gain_ref.shape[0]
    tall = blocks // 4 * rows_each

    columns = []
    for ref, parted in zip(got, split):
        if parted:
            own, came = ref[: 2 * tall, :], halves.pop(0)[: 2 * tall, :]
            low = jnp.where(half == 0, own, came)
            high = jnp.where(half == 0, came, own)
            rows = jnp.concatenate([low, high], axis=0)
        else:
            rows = ref[: 4 * tall, :]
        columns.append([rows[j * rows_each : (j + 1) * rows_each] for j in range(blocks)])
    parts = [
        jnp.concatenate([column[j] for column in columns], axis=0).astype(F32)
        for j in range(blocks)
    ]
    squares = parts[0] * parts[0]
    for part in parts[1:]:
        squares = squares + part * part
    mean = jnp.sum(squares, axis=1, keepdims=True) * (1.0 / (blocks * LANES))
    factor = lax.rsqrt(mean + 1e-06)
    normed = jnp.concatenate(
        [(parts[j] * factor * gain_ref[j : j + 1, :]).astype(BF16) for j in range(blocks)], axis=1
    )

    product = dot(normed, weight_ref[...])
    units = act_ref.shape[1]
    gate, up = product[:, :units], product[:, units:]
    act_ref[...] = (gate / (1.0 + jnp.exp(-gate)) * up).astype(BF16)
    for k in range(peers):
        start = 0 if split[k] else pl.multiple_of(2 * half * tall, 2 * tall)
        side_ref[k, : 2 * tall, :] = got[k][pl.ds(start, 2 * tall), :]
        side_ref[k, 2 * tall :, :] = got[k][got[k].shape[0] - TAGS :, :]


def down_kernel(
    members,
    rows_each,
    after_ref,
    act_ref,
    act_half_ref,
    act_core_ref,
    act_both_ref,
    down_ref,
    down_pair_ref,
    swap_ref,
    rows_ref,
    mix_ref,
    *send_refs,
):
    del after_ref
    tp = lax.axis_index("tp")
    half, core = tp // 2, tp % 2
    units = act_ref.shape[1]
    blocks = down_ref.shape[1] // LANES
    tall = blocks * rows_each
    spans = [slice(k * rows_each, (k + 1) * rows_each) for k in members]
    swap = jnp.concatenate([swap_ref[span, :] for span in spans], axis=0)
    near = jnp.concatenate([act_ref[...], act_core_ref[...]], axis=0)
    far = jnp.concatenate([act_half_ref[...], act_both_ref[...]], axis=0)
    near, far = dot(swap, near).astype(BF16), dot(swap, far).astype(BF16)
    here = pl.ds(pl.multiple_of(half * units, units), units)
    there = pl.ds(pl.multiple_of((1 - half) * units, units), units)
    for ref, parity in ((down_ref, core), (down_pair_ref, 1 - core)):
        result = dot(near, ref[here, :]) + dot(far, ref[there, :])
        for i, k in enumerate(members):
            mix = mix_ref[spans[i], :]
            for j in range(blocks):
                piece = pl.ds(
                    pl.multiple_of(parity * tall + j * rows_each, rows_each), rows_each
                )
                value = rows_ref[k, piece, :].astype(F32) + result[
                    i * rows_each : (i + 1) * rows_each, j * LANES : (j + 1) * LANES
                ]
                send_refs[i][piece, :] = (mix * value).astype(BF16)


def combine_kernel(rows_each, chosen_ref, *refs):
    came = refs[:-2]
    keep_ref, give_ref = refs[-2:]
    core = lax.axis_index("tp") % 2
    chosen = chosen_ref[...]
    tall = came[0].shape[0] // 2
    for ref, parity in ((give_ref, 1 - core), (keep_ref, core)):
        for j in range(tall // rows_each):
            start = pl.multiple_of(parity * tall + j * rows_each, rows_each)
            rows = jnp.concatenate([block[pl.ds(start, rows_each), :] for block in came], axis=0)
            ref[:, j * LANES : (j + 1) * LANES] = dot(chosen, rows).astype(ref.dtype)


def shards(
    queries,
    new_keys,
    new_values,
    key_cache,
    value_cache,
    cache_lengths,
    request_order,
    residual,
    out_weight,
    norm_gain,
    route_experts,
    route_weights,
    expert_gate,
    expert_up,
    expert_down,
):
    tp_count = lax.axis_size("tp")
    ep_count = lax.axis_size("ep")
    kv_local = KVHEADS // tp_count

    def swap_core(x):
        return lax.ppermute(x, "tp", [(i, i ^ 1) for i in range(tp_count)])

    def swap_half(x):
        return lax.ppermute(x, "tp", [(i, i ^ 2) for i in range(tp_count)])

    gate, up, down = expert_gate[0].T, expert_up[0].T, expert_down[0]
    tokens, top = route_experts.shape
    capacity = 2 * tokens * top // ep_count
    rows_each = -(-capacity // 16) * 16
    peers = ep_count // 2
    width = residual.shape[1]
    blocks = width // LANES
    tall = blocks * rows_each
    units = 2 * gate.shape[0]
    shape = jax.ShapeDtypeStruct

    begun = pl.pallas_call(
        begin_kernel,
        out_shape=shape((8, LANES), F32),
        out_specs=vmem(),
        compiler_params=params(1),
        cost_estimate=pl.CostEstimate(
            flops=20 * 10**9, bytes_accessed=64 * MIB, transcendentals=0
        ),
        name="begin",
    )()
    context = pl.pallas_call(
        functools.partial(attend_kernel, kv_local),
        out_shape=shape(queries.shape, BF16),
        in_specs=[pl.BlockSpec(memory_space=pl.ANY), pl.BlockSpec(memory_space=pltpu.SMEM)]
        + [vmem()] * 5,
        out_specs=vmem(),
        compiler_params=params(16),
        cost_estimate=pl.CostEstimate(
            flops=2 * 10**8, bytes_accessed=MIB // 2, transcendentals=0
        ),
        name="attend",
    )(begun, cache_lengths, queries, new_keys, new_values, key_cache[0], value_cache[0])
    give = pl.pallas_call(
        give_kernel,
        out_shape=shape((tokens, 2 * width), BF16),
        in_specs=[vmem()] * 2,
        out_specs=vmem(),
        compiler_params=params(16),
        name="project_given",
    )(context, out_weight)
    keep = pl.pallas_call(
        keep_kernel,
        out_shape=shape((tokens, 2 * width), F32),
        in_specs=[pl.BlockSpec(memory_space=pl.ANY)] + [vmem()] * 3,
        out_specs=vmem(),
        compiler_params=params(16),
        cost_estimate=pl.CostEstimate(flops=0, bytes_accessed=2 * MIB, transcendentals=0),
        name="project_kept",
    )(give, context, residual, out_weight)

    summed, send = pl.pallas_call(
        add_core_kernel,
        out_shape=(shape(keep.shape, F32), shape(keep.shape, BF16)),
        in_specs=[vmem()] * 2,
        out_specs=(vmem(), vmem()),
        compiler_params=params(4),
        name="add_core",
    )(keep, swap_core(give))

    part = pl.pallas_call(
        add_half_kernel,
        out_shape=shape(keep.shape, BF16),
        in_specs=[vmem()] * 2,
        out_specs=vmem(),
        compiler_params=params(4),
        name="add_half",
    )(summed, swap_half(send))
    pick, tags = pl.pallas_call(
        functools.partial(route_kernel, peers),
        out_shape=(
            shape((peers * rows_each, tokens), BF16),
            shape((peers, TAGS, LANES), BF16),
        ),
        in_specs=[pl.BlockSpec(memory_space=pl.ANY)] + [vmem()] * 2,
        out_specs=(vmem(), vmem()),
        compiler_params=params(4),
        cost_estimate=pl.CostEstimate(flops=0, bytes_accessed=MIB, transcendentals=0),
        name="route",
    )(part, route_experts.T, route_weights.T)
    other = swap_core(part)

    near = peers // 2
    split = [k >= near and (k - near) % 2 == 1 for k in range(peers)]

    def gather(members, after):
        sent = pl.pallas_call(
            functools.partial(gather_kernel, members, [split[k] for k in members]),
            out_shape=[
                shape(((2 if split[k] else 4) * tall + TAGS, LANES), BF16) for k in members
            ],
            in_specs=[pl.BlockSpec(memory_space=pl.ANY)] + [vmem()] * 4,
            out_specs=[vmem()] * len(members),
            compiler_params=params(8),
            cost_estimate=pl.CostEstimate(
                flops=(20 * 10**9 if members[0] >= near else 0),
                bytes_accessed=MIB,
                transcendentals=0,
            ),
            name="gather_rows",
        )(after, part, other, pick, tags)
        return dict(zip(members, sent))

    def route(k):
        return [
            (e * tp_count + t, (e ^ (2 * step(k, peers) + t % 2)) * tp_count + t)
            for e in range(ep_count)
            for t in range(tp_count)
        ]

    send = gather(list(reversed(range(near, peers))), tags)
    gate, up, tags = lax.optimization_barrier((gate, up, tags))
    gate_pair, up_pair = swap_core(gate), swap_core(up)
    early = near // 2
    send.update(gather(list(range(early, near)), up_pair))
    send.update(gather(list(range(early)), gate_pair))
    got = [lax.ppermute(send[k], ("ep", "tp"), route(k)) for k in range(peers)]
    halves = [swap_half(got[k]) for k in range(peers) if split[k]]

    weights = pl.pallas_call(
        stage_kernel,
        out_shape=shape((gate.shape[1], 2 * units), BF16),
        in_specs=[vmem()] + [hbm()] * 4,
        out_specs=vmem(),
        scratch_shapes=[
            pltpu.VMEM((4,) + gate.shape, BF16),
            pltpu.SemaphoreType.DMA((4,)),
        ],
        compiler_params=params(32),
        cost_estimate=pl.CostEstimate(
            flops=0, bytes_accessed=16 * gate.size, transcendentals=0
        ),
        name="stage",
    )(tags, gate, up, gate_pair, up_pair)

    down, weights = lax.optimization_barrier((down, weights))
    down_pair = swap_core(down)
    act, side = pl.pallas_call(
        functools.partial(hidden_units_kernel, split, rows_each),
        out_shape=(
            shape((peers * rows_each, units), BF16),
            shape((peers, 2 * tall + TAGS, LANES), BF16),
        ),
        in_specs=[vmem()] * (2 + peers + len(halves)),
        out_specs=(vmem(), vmem()),
        compiler_params=params(16),
        cost_estimate=pl.CostEstimate(
            flops=20 * 10**9, bytes_accessed=MIB, transcendentals=0
        ),
        name="hidden_units",
    )(norm_gain.reshape(-1, LANES), weights, *got, *halves)

    act_half = swap_half(act)
    act_core = swap_core(act)
    side_core = swap_core(side)
    act_both = swap_core(act_half)

    chosen, swap, rows, mixes = pl.pallas_call(
        functools.partial(select_kernel, top),
        out_shape=(
            shape((tokens, peers * rows_each), BF16),
            shape((peers * rows_each, 2 * peers * rows_each), BF16),
            shape((peers, 2 * tall, LANES), BF16),
            shape((peers * rows_each, LANES), F32),
        ),
        in_specs=[pl.BlockSpec(memory_space=pltpu.SMEM)] + [vmem()] * 2,
        out_specs=(vmem(),) * 4,
        scratch_shapes=[pltpu.SMEM(request_order.shape, jnp.int32)],
        compiler_params=params(8),
        cost_estimate=pl.CostEstimate(flops=0, bytes_accessed=MIB, transcendentals=0),
        name="select",
    )(request_order, side, side_core)

    def results(members, after):
        sent = pl.pallas_call(
            functools.partial(down_kernel, members, rows_each),
            out_shape=[shape((2 * tall, LANES), BF16)] * len(members),
            in_specs=[pl.BlockSpec(memory_space=pl.ANY)] + [vmem()] * 9,
            out_specs=[vmem()] * len(members),
            compiler_params=params(16),
            cost_estimate=pl.CostEstimate(
                flops=(20 * 10**9 if members[0] >= near else 0),
                bytes_accessed=MIB,
                transcendentals=0,
            ),
            name="down",
        )(
            after,
            act,
            act_half,
            act_core,
            act_both,
            down,
            down_pair,
            swap,
            rows,
            mixes,
        )
        return dict(zip(members, sent))

    send = results(list(reversed(range(near, peers))), chosen)
    send.update(results(list(range(near)), swap_core(chosen)))
    came = [lax.ppermute(send[k], ("ep", "tp"), route(k)) for k in range(peers)]

    keep, give = pl.pallas_call(
        functools.partial(combine_kernel, rows_each),
        out_shape=(shape((tokens, width), F32), shape((tokens, width), BF16)),
        in_specs=[vmem()] * (1 + peers),
        out_specs=(vmem(), vmem()),
        compiler_params=params(8),
        name="combine",
    )(chosen, *came)
    return pl.pallas_call(
        add_half_kernel,
        out_shape=shape((tokens, width), BF16),
        in_specs=[vmem()] * 2,
        out_specs=vmem(),
        compiler_params=params(4),
        name="add_output",
    )(keep, swap_core(give))


def solution(mesh):
    return jax.shard_map(
        shards,
        mesh=mesh,
        in_specs=(
            P("ep", "tp"),
            P("ep", "tp"),
            P("ep", "tp"),
            P("ep", None, "tp"),
            P("ep", None, "tp"),
            P("ep"),
            P(),
            P("ep", "tp"),
            P("tp", None),
            P(),
            P("ep", None),
            P("ep", None),
            P("ep", None, "tp"),
            P("ep", None, "tp"),
            P("ep", None, "tp"),
        ),
        out_specs=P("ep", "tp"),
        check_vma=False,
    )
```

```python
import functools
import math

import jax
import jax.numpy as jnp
from jax import lax
from jax.experimental import pallas as pl
from jax.experimental.pallas import tpu as pltpu
from jax.sharding import PartitionSpec as P

HEAD = 128
QHEADS = 16
KVHEADS = 4
LANES = 128
TAGS = 16
MIB = 1024 * 1024

BF16 = jnp.bfloat16
F32 = jnp.float32


def vmem():
    return pl.BlockSpec(memory_space=pltpu.VMEM)


def hbm():
    return pl.BlockSpec(memory_space=pltpu.HBM)


def params(mib):
    return pltpu.CompilerParams(vmem_limit_bytes=int(mib * MIB))


def dot(a, b):
    return jnp.dot(a, b, preferred_element_type=F32)


def dot_t(a, b):
    return lax.dot_general(a, b, (((1,), (1,)), ((), ())), preferred_element_type=F32)


def begin_kernel(out_ref):
    out_ref[...] = jnp.zeros(out_ref.shape, F32)


def attend_kernel(
    kv_local,
    after_ref,
    length_ref,
    query_ref,
    new_key_ref,
    new_value_ref,
    key_ref,
    value_ref,
    context_ref,
):
    del after_ref
    tokens = query_ref.shape[0]
    group = QHEADS // KVHEADS
    length = length_ref[0]
    scale = 1.0 / math.sqrt(HEAD)
    pieces = []
    for g in range(kv_local):
        columns = slice(g * HEAD, (g + 1) * HEAD)
        rows = jnp.concatenate(
            [
                query_ref[:, (g * group + i) * HEAD : (g * group + i + 1) * HEAD]
                for i in range(group)
            ],
            axis=0,
        )
        old = dot_t(rows, key_ref[:, columns]) * scale
        new = dot_t(rows, new_key_ref[:, columns]) * scale
        position = lax.broadcasted_iota(jnp.int32, old.shape, 1)
        old = jnp.where(position < length, old, -1e30)
        current = lax.broadcasted_iota(jnp.int32, new.shape, 0) % tokens
        position = lax.broadcasted_iota(jnp.int32, new.shape, 1)
        new = jnp.where(position <= current, new, -1e30)
        highest = jnp.maximum(
            jnp.max(old, axis=1, keepdims=True), jnp.max(new, axis=1, keepdims=True)
        )
        old = jnp.exp(old - highest)
        new = jnp.exp(new - highest)
        totals = jnp.sum(old, axis=1, keepdims=True) + jnp.sum(new, axis=1, keepdims=True)
        mixed = dot(old.astype(BF16), value_ref[:, columns]) + dot(
            new.astype(BF16), new_value_ref[:, columns]
        )
        mixed = (mixed / totals).astype(BF16)
        pieces += [mixed[i * tokens : (i + 1) * tokens] for i in range(group)]
    context_ref[...] = jnp.concatenate(pieces, axis=1)


def give_kernel(context_ref, weight_ref, give_ref):
    core = lax.axis_index("tp") % 2
    width = context_ref.shape[1]
    context = context_ref[...]
    for i in range(2):
        start = pl.multiple_of((2 * i + 1 - core) * width, width)
        part = dot(context, weight_ref[:, pl.ds(start, width)])
        give_ref[:, i * width : (i + 1) * width] = part.astype(BF16)


def keep_kernel(after_ref, context_ref, residual_ref, weight_ref, keep_ref):
    del after_ref
    tp = lax.axis_index("tp")
    half, core = tp // 2, tp % 2
    width = context_ref.shape[1]
    context = context_ref[...]
    for i in range(2):
        start = pl.multiple_of((2 * i + core) * width, width)
        part = dot(context, weight_ref[:, pl.ds(start, width)])
        keep_ref[:, i * width : (i + 1) * width] = part + jnp.where(
            half == i, residual_ref[...].astype(F32), 0.0
        )


def step(k, peers):
    near = peers // 2
    if isinstance(k, int):
        return near - 1 - k if k < near else k
    return jnp.where(k < near, near - 1 - k, k)


def peer_numbers(peers, tokens):
    number = lax.broadcasted_iota(jnp.int32, (peers, tokens), 0)
    near = peers // 2
    steps = jnp.where(number < near, near - 1 - number, number)
    return jnp.bitwise_xor(2 * steps + lax.axis_index("tp") % 2, lax.axis_index("ep"))


def earlier_tokens(tokens):
    earlier = lax.broadcasted_iota(jnp.int32, (tokens, tokens), 0) < lax.broadcasted_iota(
        jnp.int32, (tokens, tokens), 1
    )
    return jnp.where(earlier, 1.0, 0.0).astype(BF16)


def slot_numbers(named, tokens):
    rank = dot(named.astype(BF16), earlier_tokens(tokens))
    return jnp.where(named > 0.0, rank, -1.0)


def route_kernel(peers, after_ref, expert_ref, weight_ref, pick_ref, tags_ref):
    del after_ref
    top, tokens = expert_ref.shape
    rows_each = pick_ref.shape[0] // peers
    peer = peer_numbers(peers, tokens)
    weights = weight_ref[...]
    mixing = (weights / jnp.sum(weights, axis=0, keepdims=True)).astype(BF16).astype(F32)
    mix_of = jnp.zeros((peers, tokens), F32)
    named = jnp.zeros((peers, tokens), F32)
    for j in range(top):
        match = expert_ref[j : j + 1, :] == peer
        mix_of = mix_of + jnp.where(match, mixing[j : j + 1, :], 0.0)
        named = named + jnp.where(match, 1.0, 0.0)
    rank = slot_numbers(named, tokens)
    slot = lax.broadcasted_iota(jnp.int32, (rows_each, tokens), 0).astype(F32)
    line = lax.broadcasted_iota(jnp.int32, (TAGS, tokens), 0)
    names = jnp.zeros((TAGS, tokens), F32)
    for j in range(top):
        names = jnp.where(line == j + 1, expert_ref[j : j + 1, :].astype(F32), names)
    tags_ref[...] = jnp.zeros(tags_ref.shape, BF16)
    for k in range(peers):
        pick = jnp.where(rank[k : k + 1, :] == slot, 1.0, 0.0).astype(BF16)
        pick_ref[k * rows_each : (k + 1) * rows_each, :] = pick
        tags_ref[k, :, :tokens] = names.astype(BF16)
        mix = jnp.where(line == 0, mix_of[k : k + 1, :], 0.0).astype(BF16)
        tags_ref[k, :1, :rows_each] = dot_t(mix, pick)[:1].astype(BF16)


def select_kernel(
    top,
    order_ref,
    side_ref,
    side_core_ref,
    chosen_ref,
    swap_ref,
    rows_ref,
    mix_ref,
    inverse_ref,
):
    me = lax.axis_index("ep")
    core = lax.axis_index("tp") % 2
    tokens = chosen_ref.shape[0]
    peers = side_ref.shape[0]
    rows_each = chosen_ref.shape[1] // peers
    names = jnp.zeros((TAGS, LANES), F32)
    for k in range(peers):
        for ref, parity in ((side_ref, core), (side_core_ref, 1 - core)):
            here = order_ref[jnp.bitwise_xor(me, 2 * step(k, peers) + parity)] == me
            tags = ref[k, ref.shape[1] - TAGS :, :].astype(F32)
            names = names + jnp.where(here, tags, 0.0)
    expert = peer_numbers(peers, tokens).astype(F32)
    named = jnp.zeros((peers, tokens), F32)
    for j in range(top):
        named = named + jnp.where(names[j + 1 : j + 2, :tokens] == expert, 1.0, 0.0)
    rank = slot_numbers(named, tokens)
    slot = lax.broadcasted_iota(jnp.int32, (rows_each, tokens), 0).astype(F32)
    pick = jnp.concatenate(
        [jnp.where(rank[k : k + 1, :] == slot, 1.0, 0.0) for k in range(peers)], axis=0
    )
    chosen_ref[...] = pick.T.astype(BF16)

    def place(s, carry):
        inverse_ref[order_ref[s]] = s
        return carry

    lax.fori_loop(0, order_ref.shape[0], place, 0)
    height = rows_ref.shape[1]
    diagonal = lax.broadcasted_iota(jnp.int32, (rows_each, LANES), 0) == lax.broadcasted_iota(
        jnp.int32, (rows_each, LANES), 1
    )
    row = lax.broadcasted_iota(jnp.int32, (rows_each, swap_ref.shape[1]), 0)
    column = lax.broadcasted_iota(jnp.int32, (rows_each, swap_ref.shape[1]), 1)
    for k in range(peers):
        offset = jnp.bitwise_xor(
            inverse_ref[jnp.bitwise_xor(me, 2 * step(k, peers) + core)], me
        )
        index = step(offset // 2, peers)
        mine = offset % 2 == core
        block = jnp.where(mine, side_ref[index], side_core_ref[index])
        rows_ref[k] = block[:height]
        tags = block[height:].astype(F32)[0:1, :]
        mix = jnp.sum(jnp.where(diagonal, tags, 0.0), axis=1, keepdims=True)
        span = slice(k * rows_each, (k + 1) * rows_each)
        mix_ref[span, :] = jnp.broadcast_to(mix, (rows_each, LANES))
        base = (index + jnp.where(mine, 0, peers)) * rows_each
        swap_ref[span, :] = jnp.where(column == base + row, 1.0, 0.0).astype(BF16)


def add_core_kernel(keep_ref, came_ref, sum_ref, send_ref):
    value = keep_ref[...] + came_ref[...].astype(F32)
    sum_ref[...] = value
    send_ref[...] = value.astype(BF16)


def add_half_kernel(sum_ref, came_ref, out_ref):
    out_ref[...] = (sum_ref[...] + came_ref[...].astype(F32)).astype(BF16)


def gather_kernel(members, split, after_ref, part_ref, other_ref, pick_ref, tags_ref, *send_refs):
    del after_ref
    tp = lax.axis_index("tp")
    mine, core = tp // 2, tp % 2
    count = len(members)
    rows_each = pick_ref.shape[0] // tags_ref.shape[0]
    pick = jnp.concatenate(
        [pick_ref[k * rows_each : (k + 1) * rows_each, :] for k in members], axis=0
    )
    width = part_ref.shape[1] // 2
    blocks = width // LANES
    tall = blocks * rows_each

    def put(ref, rows, base):
        for j in range(blocks):
            start = pl.multiple_of(base + j * rows_each, rows_each)
            ref[pl.ds(start, rows_each), :] = rows[:, j * LANES : (j + 1) * LANES]

    for source, parity in ((part_ref, core), (other_ref, 1 - core)):
        whole = [k for k in range(count) if not split[k]]
        for half in range(2) if whole else ():
            rows = dot(pick, source[:, half * width : (half + 1) * width]).astype(BF16)
            for k in whole:
                piece = rows[k * rows_each : (k + 1) * rows_each]
                put(send_refs[k], piece, (2 * half + parity) * tall)
        for k in range(count):
            if split[k]:
                columns = pl.ds(pl.multiple_of(mine * width, width), width)
                piece = pick[k * rows_each : (k + 1) * rows_each]
                put(send_refs[k], dot(piece, source[:, columns]).astype(BF16), parity * tall)
    for k in range(count):
        send_refs[k][send_refs[k].shape[0] - TAGS :, :] = tags_ref[members[k]]


def stage_kernel(after_ref, gate, up, gate_pair, up_pair, out_ref, held_ref, sems):
    del after_ref
    core = lax.axis_index("tp") % 2
    copies = [
        pltpu.make_async_copy(source, held_ref.at[place], sems.at[i])
        for i, (source, place) in enumerate(
            ((gate, core), (up, 2 + core), (gate_pair, 1 - core), (up_pair, 3 - core))
        )
    ]
    for copy in copies:
        copy.start()
    for copy in copies:
        copy.wait()
    units, width = held_ref.shape[1:]
    for j in range(width // LANES):
        columns = slice(j * LANES, (j + 1) * LANES)
        out_ref[columns, :] = held_ref[:, :, columns].reshape(4 * units, LANES).T


def hidden_units_kernel(order, split, rows_each, gain_ref, weight_ref, *refs):
    peers = len(split)
    got = [refs[order.index(k)] for k in range(peers)]
    halves = list(refs[peers:-2])
    act_ref, side_ref = refs[-2:]
    tp = lax.axis_index("tp")
    half, core = tp // 2, tp % 2
    blocks = gain_ref.shape[0]
    tall = blocks // 4 * rows_each

    columns = []
    for ref, parted in zip(got, split):
        if parted:
            own, came = ref[: 2 * tall, :], halves.pop(0)[: 2 * tall, :]
            low = jnp.where(half == 0, own, came)
            high = jnp.where(half == 0, came, own)
            rows = jnp.concatenate([low, high], axis=0)
        else:
            rows = ref[: 4 * tall, :]
        columns.append([rows[j * rows_each : (j + 1) * rows_each] for j in range(blocks)])
    parts = [
        jnp.concatenate([column[j] for column in columns], axis=0).astype(F32)
        for j in range(blocks)
    ]
    squares = parts[0] * parts[0]
    for part in parts[1:]:
        squares = squares + part * part
    mean = jnp.sum(squares, axis=1, keepdims=True) * (1.0 / (blocks * LANES))
    factor = lax.rsqrt(mean + 1e-06)
    normed = jnp.concatenate(
        [(parts[j] * factor * gain_ref[j : j + 1, :]).astype(BF16) for j in range(blocks)], axis=1
    )

    product = dot(normed, weight_ref[...])
    units = act_ref.shape[1]
    gate, up = product[:, :units], product[:, units:]
    act_ref[...] = (gate / (1.0 + jnp.exp(-gate)) * up).astype(BF16)
    for k in range(peers):
        start = 0 if split[k] else pl.multiple_of(2 * half * tall, 2 * tall)
        side_ref[k, : 2 * tall, :] = got[k][pl.ds(start, 2 * tall), :]
        side_ref[k, 2 * tall :, :] = got[k][got[k].shape[0] - TAGS :, :]


def down_kernel(
    members,
    rows_each,
    after_ref,
    act_ref,
    act_half_ref,
    act_core_ref,
    act_both_ref,
    down_ref,
    down_pair_ref,
    swap_ref,
    rows_ref,
    mix_ref,
    *send_refs,
):
    del after_ref
    tp = lax.axis_index("tp")
    half, core = tp // 2, tp % 2
    units = act_ref.shape[1]
    blocks = down_ref.shape[1] // LANES
    tall = blocks * rows_each
    spans = [slice(k * rows_each, (k + 1) * rows_each) for k in members]
    swap = jnp.concatenate([swap_ref[span, :] for span in spans], axis=0)
    near = jnp.concatenate([act_ref[...], act_core_ref[...]], axis=0)
    far = jnp.concatenate([act_half_ref[...], act_both_ref[...]], axis=0)
    near, far = dot(swap, near).astype(BF16), dot(swap, far).astype(BF16)
    here = pl.ds(pl.multiple_of(half * units, units), units)
    there = pl.ds(pl.multiple_of((1 - half) * units, units), units)
    for ref, parity in ((down_ref, core), (down_pair_ref, 1 - core)):
        result = dot(near, ref[here, :]) + dot(far, ref[there, :])
        for i, k in enumerate(members):
            mix = mix_ref[spans[i], :]
            for j in range(blocks):
                piece = pl.ds(
                    pl.multiple_of(parity * tall + j * rows_each, rows_each), rows_each
                )
                value = rows_ref[k, piece, :].astype(F32) + result[
                    i * rows_each : (i + 1) * rows_each, j * LANES : (j + 1) * LANES
                ]
                send_refs[i][piece, :] = (mix * value).astype(BF16)


def combine_kernel(order, rows_each, chosen_ref, *refs):
    came = [refs[order.index(k)] for k in range(len(order))]
    keep_ref, give_ref = refs[-2:]
    core = lax.axis_index("tp") % 2
    chosen = chosen_ref[...]
    tall = came[0].shape[0] // 2
    for ref, parity in ((give_ref, 1 - core), (keep_ref, core)):
        for j in range(tall // rows_each):
            start = pl.multiple_of(parity * tall + j * rows_each, rows_each)
            rows = jnp.concatenate([block[pl.ds(start, rows_each), :] for block in came], axis=0)
            ref[:, j * LANES : (j + 1) * LANES] = dot(chosen, rows).astype(ref.dtype)


def shards(
    queries,
    new_keys,
    new_values,
    key_cache,
    value_cache,
    cache_lengths,
    request_order,
    residual,
    out_weight,
    norm_gain,
    route_experts,
    route_weights,
    expert_gate,
    expert_up,
    expert_down,
):
    tp_count = lax.axis_size("tp")
    ep_count = lax.axis_size("ep")
    kv_local = KVHEADS // tp_count

    def swap_core(x):
        return lax.ppermute(x, "tp", [(i, i ^ 1) for i in range(tp_count)])

    def swap_half(x):
        return lax.ppermute(x, "tp", [(i, i ^ 2) for i in range(tp_count)])

    gate, up, down = expert_gate[0].T, expert_up[0].T, expert_down[0]
    tokens, top = route_experts.shape
    capacity = 2 * tokens * top // ep_count
    rows_each = -(-capacity // 16) * 16
    peers = ep_count // 2
    width = residual.shape[1]
    blocks = width // LANES
    tall = blocks * rows_each
    units = 2 * gate.shape[0]
    shape = jax.ShapeDtypeStruct

    begun = pl.pallas_call(
        begin_kernel,
        out_shape=shape((8, LANES), F32),
        out_specs=vmem(),
        compiler_params=params(1),
        cost_estimate=pl.CostEstimate(
            flops=20 * 10**9, bytes_accessed=64 * MIB, transcendentals=0
        ),
        name="begin",
    )()
    context = pl.pallas_call(
        functools.partial(attend_kernel, kv_local),
        out_shape=shape(queries.shape, BF16),
        in_specs=[pl.BlockSpec(memory_space=pl.ANY), pl.BlockSpec(memory_space=pltpu.SMEM)]
        + [vmem()] * 5,
        out_specs=vmem(),
        compiler_params=params(16),
        cost_estimate=pl.CostEstimate(
            flops=2 * 10**8, bytes_accessed=MIB // 2, transcendentals=0
        ),
        name="attend",
    )(begun, cache_lengths, queries, new_keys, new_values, key_cache[0], value_cache[0])
    give = pl.pallas_call(
        give_kernel,
        out_shape=shape((tokens, 2 * width), BF16),
        in_specs=[vmem()] * 2,
        out_specs=vmem(),
        compiler_params=params(16),
        name="project_given",
    )(context, out_weight)
    keep = pl.pallas_call(
        keep_kernel,
        out_shape=shape((tokens, 2 * width), F32),
        in_specs=[pl.BlockSpec(memory_space=pl.ANY)] + [vmem()] * 3,
        out_specs=vmem(),
        compiler_params=params(16),
        cost_estimate=pl.CostEstimate(flops=0, bytes_accessed=2 * MIB, transcendentals=0),
        name="project_kept",
    )(give, context, residual, out_weight)

    summed, send = pl.pallas_call(
        add_core_kernel,
        out_shape=(shape(keep.shape, F32), shape(keep.shape, BF16)),
        in_specs=[vmem()] * 2,
        out_specs=(vmem(), vmem()),
        compiler_params=params(4),
        name="add_core",
    )(keep, swap_core(give))

    part = pl.pallas_call(
        add_half_kernel,
        out_shape=shape(keep.shape, BF16),
        in_specs=[vmem()] * 2,
        out_specs=vmem(),
        compiler_params=params(4),
        name="add_half",
    )(summed, swap_half(send))
    pick, tags = pl.pallas_call(
        functools.partial(route_kernel, peers),
        out_shape=(
            shape((peers * rows_each, tokens), BF16),
            shape((peers, TAGS, LANES), BF16),
        ),
        in_specs=[pl.BlockSpec(memory_space=pl.ANY)] + [vmem()] * 2,
        out_specs=(vmem(), vmem()),
        compiler_params=params(4),
        cost_estimate=pl.CostEstimate(flops=0, bytes_accessed=MIB, transcendentals=0),
        name="route",
    )(part, route_experts.T, route_weights.T)
    other = swap_core(part)

    near = peers // 2
    split = [k >= near and (k - near) % 2 == 1 for k in range(peers)]

    def gather(members, after):
        sent = pl.pallas_call(
            functools.partial(gather_kernel, members, [split[k] for k in members]),
            out_shape=[
                shape(((2 if split[k] else 4) * tall + TAGS, LANES), BF16) for k in members
            ],
            in_specs=[pl.BlockSpec(memory_space=pl.ANY)] + [vmem()] * 4,
            out_specs=[vmem()] * len(members),
            compiler_params=params(8),
            cost_estimate=pl.CostEstimate(
                flops=(20 * 10**9 if members[0] >= near else 0),
                bytes_accessed=MIB,
                transcendentals=0,
            ),
            name="gather_rows",
        )(after, part, other, pick, tags)
        return dict(zip(members, sent))

    def route(k):
        return [
            (e * tp_count + t, (e ^ (2 * step(k, peers) + t % 2)) * tp_count + t)
            for e in range(ep_count)
            for t in range(tp_count)
        ]

    send = gather(list(reversed(range(near, peers))), tags)
    gate, up, tags = lax.optimization_barrier((gate, up, tags))
    gate_pair, up_pair = swap_core(gate), swap_core(up)
    send.update(gather(list(range(near)), gate_pair))
    got = [lax.ppermute(send[k], ("ep", "tp"), route(k)) for k in range(peers)]
    halves = [swap_half(got[k]) for k in range(peers) if split[k]]

    weights = pl.pallas_call(
        stage_kernel,
        out_shape=shape((gate.shape[1], 2 * units), BF16),
        in_specs=[vmem()] + [hbm()] * 4,
        out_specs=vmem(),
        scratch_shapes=[
            pltpu.VMEM((4,) + gate.shape, BF16),
            pltpu.SemaphoreType.DMA((4,)),
        ],
        compiler_params=params(32),
        cost_estimate=pl.CostEstimate(
            flops=0, bytes_accessed=16 * gate.size, transcendentals=0
        ),
        name="stage",
    )(tags, gate, up, gate_pair, up_pair)

    down, weights = lax.optimization_barrier((down, weights))
    down_pair = swap_core(down)
    arrival = [*range(near, peers), *range(near)]
    act, side = pl.pallas_call(
        functools.partial(hidden_units_kernel, arrival, split, rows_each),
        out_shape=(
            shape((peers * rows_each, units), BF16),
            shape((peers, 2 * tall + TAGS, LANES), BF16),
        ),
        in_specs=[vmem()] * (2 + peers + len(halves)),
        out_specs=(vmem(), vmem()),
        compiler_params=params(16),
        cost_estimate=pl.CostEstimate(
            flops=20 * 10**9, bytes_accessed=MIB, transcendentals=0
        ),
        name="hidden_units",
    )(norm_gain.reshape(-1, LANES), weights, *[got[k] for k in arrival], *halves)

    act_half = swap_half(act)
    act_core = swap_core(act)
    side_core = swap_core(side)
    act_both = swap_core(act_half)

    chosen, swap, rows, mixes = pl.pallas_call(
        functools.partial(select_kernel, top),
        out_shape=(
            shape((tokens, peers * rows_each), BF16),
            shape((peers * rows_each, 2 * peers * rows_each), BF16),
            shape((peers, 2 * tall, LANES), BF16),
            shape((peers * rows_each, LANES), F32),
        ),
        in_specs=[pl.BlockSpec(memory_space=pltpu.SMEM)] + [vmem()] * 2,
        out_specs=(vmem(),) * 4,
        scratch_shapes=[pltpu.SMEM(request_order.shape, jnp.int32)],
        compiler_params=params(8),
        cost_estimate=pl.CostEstimate(flops=0, bytes_accessed=MIB, transcendentals=0),
        name="select",
    )(request_order, side, side_core)

    def results(members, after):
        sent = pl.pallas_call(
            functools.partial(down_kernel, members, rows_each),
            out_shape=[shape((2 * tall, LANES), BF16)] * len(members),
            in_specs=[pl.BlockSpec(memory_space=pl.ANY)] + [vmem()] * 9,
            out_specs=[vmem()] * len(members),
            compiler_params=params(16),
            cost_estimate=pl.CostEstimate(
                flops=(20 * 10**9 if members[0] >= near else 0),
                bytes_accessed=MIB,
                transcendentals=0,
            ),
            name="down",
        )(
            after,
            act,
            act_half,
            act_core,
            act_both,
            down,
            down_pair,
            swap,
            rows,
            mixes,
        )
        return dict(zip(members, sent))

    order = [*range(near, peers), *range(near)]
    send = results(list(range(peers)), chosen)
    came = [lax.ppermute(send[k], ("ep", "tp"), route(k)) for k in order]

    keep, give = pl.pallas_call(
        functools.partial(combine_kernel, order, rows_each),
        out_shape=(shape((tokens, width), F32), shape((tokens, width), BF16)),
        in_specs=[vmem()] * (1 + peers),
        out_specs=(vmem(), vmem()),
        compiler_params=params(8),
        name="combine",
    )(chosen, *came)
    return pl.pallas_call(
        add_half_kernel,
        out_shape=shape((tokens, width), BF16),
        in_specs=[vmem()] * 2,
        out_specs=vmem(),
        compiler_params=params(4),
        name="add_output",
    )(keep, swap_core(give))


def solution(mesh):
    return jax.shard_map(
        shards,
        mesh=mesh,
        in_specs=(
            P("ep", "tp"),
            P("ep", "tp"),
            P("ep", "tp"),
            P("ep", None, "tp"),
            P("ep", None, "tp"),
            P("ep"),
            P(),
            P("ep", "tp"),
            P("tp", None),
            P(),
            P("ep", None),
            P("ep", None),
            P("ep", None, "tp"),
            P("ep", None, "tp"),
            P("ep", None, "tp"),
        ),
        out_specs=P("ep", "tp"),
        check_vma=False,
    )
```

```python
import functools
import math

import jax
import jax.numpy as jnp
from jax import lax
from jax.experimental import pallas as pl
from jax.experimental.pallas import tpu as pltpu
from jax.sharding import PartitionSpec as P

HEAD = 128
QHEADS = 16
KVHEADS = 4
LANES = 128
TAGS = 16
MIB = 1024 * 1024

BF16 = jnp.bfloat16
F32 = jnp.float32


def vmem():
    return pl.BlockSpec(memory_space=pltpu.VMEM)


def hbm():
    return pl.BlockSpec(memory_space=pltpu.HBM)


def params(mib):
    return pltpu.CompilerParams(vmem_limit_bytes=int(mib * MIB))


def dot(a, b):
    return jnp.dot(a, b, preferred_element_type=F32)


def dot_t(a, b):
    return lax.dot_general(a, b, (((1,), (1,)), ((), ())), preferred_element_type=F32)


def begin_kernel(out_ref):
    out_ref[...] = jnp.zeros(out_ref.shape, F32)


def attend_kernel(
    kv_local,
    after_ref,
    length_ref,
    query_ref,
    new_key_ref,
    new_value_ref,
    key_ref,
    value_ref,
    context_ref,
):
    del after_ref
    tokens = query_ref.shape[0]
    group = QHEADS // KVHEADS
    length = length_ref[0]
    scale = 1.0 / math.sqrt(HEAD)
    pieces = []
    for g in range(kv_local):
        columns = slice(g * HEAD, (g + 1) * HEAD)
        rows = jnp.concatenate(
            [
                query_ref[:, (g * group + i) * HEAD : (g * group + i + 1) * HEAD]
                for i in range(group)
            ],
            axis=0,
        )
        old = dot_t(rows, key_ref[:, columns]) * scale
        new = dot_t(rows, new_key_ref[:, columns]) * scale
        position = lax.broadcasted_iota(jnp.int32, old.shape, 1)
        old = jnp.where(position < length, old, -1e30)
        current = lax.broadcasted_iota(jnp.int32, new.shape, 0) % tokens
        position = lax.broadcasted_iota(jnp.int32, new.shape, 1)
        new = jnp.where(position <= current, new, -1e30)
        highest = jnp.maximum(
            jnp.max(old, axis=1, keepdims=True), jnp.max(new, axis=1, keepdims=True)
        )
        old = jnp.exp(old - highest)
        new = jnp.exp(new - highest)
        totals = jnp.sum(old, axis=1, keepdims=True) + jnp.sum(new, axis=1, keepdims=True)
        mixed = dot(old.astype(BF16), value_ref[:, columns]) + dot(
            new.astype(BF16), new_value_ref[:, columns]
        )
        mixed = (mixed / totals).astype(BF16)
        pieces += [mixed[i * tokens : (i + 1) * tokens] for i in range(group)]
    context_ref[...] = jnp.concatenate(pieces, axis=1)


def give_kernel(context_ref, weight_ref, give_ref):
    core = lax.axis_index("tp") % 2
    width = context_ref.shape[1]
    context = context_ref[...]
    for i in range(2):
        start = pl.multiple_of((2 * i + 1 - core) * width, width)
        part = dot(context, weight_ref[:, pl.ds(start, width)])
        give_ref[:, i * width : (i + 1) * width] = part.astype(BF16)


def keep_kernel(after_ref, context_ref, residual_ref, weight_ref, keep_ref):
    del after_ref
    tp = lax.axis_index("tp")
    half, core = tp // 2, tp % 2
    width = context_ref.shape[1]
    context = context_ref[...]
    for i in range(2):
        start = pl.multiple_of((2 * i + core) * width, width)
        part = dot(context, weight_ref[:, pl.ds(start, width)])
        keep_ref[:, i * width : (i + 1) * width] = part + jnp.where(
            half == i, residual_ref[...].astype(F32), 0.0
        )


def step(k, peers):
    near = peers // 2
    if isinstance(k, int):
        return near - 1 - k if k < near else k
    return jnp.where(k < near, near - 1 - k, k)


def peer_numbers(peers, tokens):
    number = lax.broadcasted_iota(jnp.int32, (peers, tokens), 0)
    near = peers // 2
    steps = jnp.where(number < near, near - 1 - number, number)
    return jnp.bitwise_xor(2 * steps + lax.axis_index("tp") % 2, lax.axis_index("ep"))


def earlier_tokens(tokens):
    earlier = lax.broadcasted_iota(jnp.int32, (tokens, tokens), 0) < lax.broadcasted_iota(
        jnp.int32, (tokens, tokens), 1
    )
    return jnp.where(earlier, 1.0, 0.0).astype(BF16)


def slot_numbers(named, tokens):
    rank = dot(named.astype(BF16), earlier_tokens(tokens))
    return jnp.where(named > 0.0, rank, -1.0)


def route_kernel(peers, after_ref, expert_ref, weight_ref, pick_ref, tags_ref):
    del after_ref
    top, tokens = expert_ref.shape
    rows_each = pick_ref.shape[0] // peers
    peer = peer_numbers(peers, tokens)
    weights = weight_ref[...]
    mixing = (weights / jnp.sum(weights, axis=0, keepdims=True)).astype(BF16).astype(F32)
    mix_of = jnp.zeros((peers, tokens), F32)
    named = jnp.zeros((peers, tokens), F32)
    for j in range(top):
        match = expert_ref[j : j + 1, :] == peer
        mix_of = mix_of + jnp.where(match, mixing[j : j + 1, :], 0.0)
        named = named + jnp.where(match, 1.0, 0.0)
    rank = slot_numbers(named, tokens)
    slot = lax.broadcasted_iota(jnp.int32, (rows_each, tokens), 0).astype(F32)
    line = lax.broadcasted_iota(jnp.int32, (TAGS, tokens), 0)
    names = jnp.zeros((TAGS, tokens), F32)
    for j in range(top):
        names = jnp.where(line == j + 1, expert_ref[j : j + 1, :].astype(F32), names)
    tags_ref[...] = jnp.zeros(tags_ref.shape, BF16)
    for k in range(peers):
        pick = jnp.where(rank[k : k + 1, :] == slot, 1.0, 0.0).astype(BF16)
        pick_ref[k * rows_each : (k + 1) * rows_each, :] = pick
        mix = jnp.where(line == 0, mix_of[k : k + 1, :], 0.0).astype(BF16)
        every = jnp.concatenate([pick, jnp.zeros((tokens - rows_each, tokens), BF16)], axis=0)
        tags_ref[k, :, :tokens] = (names + dot_t(mix, every)).astype(BF16)


def select_kernel(
    top,
    order_ref,
    side_ref,
    side_core_ref,
    chosen_ref,
    swap_ref,
    rows_ref,
    mix_ref,
    inverse_ref,
):
    me = lax.axis_index("ep")
    core = lax.axis_index("tp") % 2
    tokens = chosen_ref.shape[0]
    peers = side_ref.shape[0]
    rows_each = chosen_ref.shape[1] // peers
    names = jnp.zeros((TAGS, LANES), F32)
    for k in range(peers):
        for ref, parity in ((side_ref, core), (side_core_ref, 1 - core)):
            here = order_ref[jnp.bitwise_xor(me, 2 * step(k, peers) + parity)] == me
            tags = ref[k, ref.shape[1] - TAGS :, :].astype(F32)
            names = names + jnp.where(here, tags, 0.0)
    expert = peer_numbers(peers, tokens).astype(F32)
    named = jnp.zeros((peers, tokens), F32)
    for j in range(top):
        named = named + jnp.where(names[j + 1 : j + 2, :tokens] == expert, 1.0, 0.0)
    rank = slot_numbers(named, tokens)
    slot = lax.broadcasted_iota(jnp.int32, (rows_each, tokens), 0).astype(F32)
    pick = jnp.concatenate(
        [jnp.where(rank[k : k + 1, :] == slot, 1.0, 0.0) for k in range(peers)], axis=0
    )
    chosen_ref[...] = pick.T.astype(BF16)

    def place(s, carry):
        inverse_ref[order_ref[s]] = s
        return carry

    lax.fori_loop(0, order_ref.shape[0], place, 0)
    height = rows_ref.shape[1]
    diagonal = lax.broadcasted_iota(jnp.int32, (rows_each, LANES), 0) == lax.broadcasted_iota(
        jnp.int32, (rows_each, LANES), 1
    )
    row = lax.broadcasted_iota(jnp.int32, (rows_each, swap_ref.shape[1]), 0)
    column = lax.broadcasted_iota(jnp.int32, (rows_each, swap_ref.shape[1]), 1)
    for k in range(peers):
        offset = jnp.bitwise_xor(
            inverse_ref[jnp.bitwise_xor(me, 2 * step(k, peers) + core)], me
        )
        index = step(offset // 2, peers)
        mine = offset % 2 == core
        block = jnp.where(mine, side_ref[index], side_core_ref[index])
        rows_ref[k] = block[:height]
        tags = block[height:].astype(F32)[0:1, :]
        mix = jnp.sum(jnp.where(diagonal, tags, 0.0), axis=1, keepdims=True)
        span = slice(k * rows_each, (k + 1) * rows_each)
        mix_ref[span, :] = jnp.broadcast_to(mix, (rows_each, LANES))
        base = (index + jnp.where(mine, 0, peers)) * rows_each
        swap_ref[span, :] = jnp.where(column == base + row, 1.0, 0.0).astype(BF16)


def add_core_kernel(keep_ref, came_ref, sum_ref, send_ref):
    value = keep_ref[...] + came_ref[...].astype(F32)
    sum_ref[...] = value
    send_ref[...] = value.astype(BF16)


def add_half_kernel(sum_ref, came_ref, out_ref):
    out_ref[...] = (sum_ref[...] + came_ref[...].astype(F32)).astype(BF16)


def gather_kernel(members, split, after_ref, part_ref, other_ref, pick_ref, tags_ref, *send_refs):
    del after_ref
    tp = lax.axis_index("tp")
    mine, core = tp // 2, tp % 2
    count = len(members)
    rows_each = pick_ref.shape[0] // tags_ref.shape[0]
    pick = jnp.concatenate(
        [pick_ref[k * rows_each : (k + 1) * rows_each, :] for k in members], axis=0
    )
    width = part_ref.shape[1] // 2
    blocks = width // LANES
    tall = blocks * rows_each

    def put(ref, rows, base):
        for j in range(blocks):
            start = pl.multiple_of(base + j * rows_each, rows_each)
            ref[pl.ds(start, rows_each), :] = rows[:, j * LANES : (j + 1) * LANES]

    for source, parity in ((part_ref, core), (other_ref, 1 - core)):
        whole = [k for k in range(count) if not split[k]]
        for half in range(2) if whole else ():
            rows = dot(pick, source[:, half * width : (half + 1) * width]).astype(BF16)
            for k in whole:
                piece = rows[k * rows_each : (k + 1) * rows_each]
                put(send_refs[k], piece, (2 * half + parity) * tall)
        for k in range(count):
            if split[k]:
                columns = pl.ds(pl.multiple_of(mine * width, width), width)
                piece = pick[k * rows_each : (k + 1) * rows_each]
                put(send_refs[k], dot(piece, source[:, columns]).astype(BF16), parity * tall)
    for k in range(count):
        send_refs[k][send_refs[k].shape[0] - TAGS :, :] = tags_ref[members[k]]


def stage_kernel(after_ref, gate, up, gate_pair, up_pair, out_ref, held_ref, sems):
    del after_ref
    core = lax.axis_index("tp") % 2
    copies = [
        pltpu.make_async_copy(source, held_ref.at[place], sems.at[i])
        for i, (source, place) in enumerate(
            ((gate, core), (up, 2 + core), (gate_pair, 1 - core), (up_pair, 3 - core))
        )
    ]
    for copy in copies:
        copy.start()
    for copy in copies:
        copy.wait()
    units, width = held_ref.shape[1:]
    for j in range(width // LANES):
        columns = slice(j * LANES, (j + 1) * LANES)
        out_ref[columns, :] = held_ref[:, :, columns].reshape(4 * units, LANES).T


def hidden_units_kernel(order, split, rows_each, gain_ref, weight_ref, *refs):
    peers = len(split)
    got = [refs[order.index(k)] for k in range(peers)]
    halves = list(refs[peers:-2])
    act_ref, side_ref = refs[-2:]
    tp = lax.axis_index("tp")
    half, core = tp // 2, tp % 2
    blocks = gain_ref.shape[0]
    tall = blocks // 4 * rows_each

    columns = []
    for ref, parted in zip(got, split):
        if parted:
            own, came = ref[: 2 * tall, :], halves.pop(0)[: 2 * tall, :]
            low = jnp.where(half == 0, own, came)
            high = jnp.where(half == 0, came, own)
            rows = jnp.concatenate([low, high], axis=0)
        else:
            rows = ref[: 4 * tall, :]
        columns.append([rows[j * rows_each : (j + 1) * rows_each] for j in range(blocks)])
    parts = [
        jnp.concatenate([column[j] for column in columns], axis=0).astype(F32)
        for j in range(blocks)
    ]
    squares = parts[0] * parts[0]
    for part in parts[1:]:
        squares = squares + part * part
    mean = jnp.sum(squares, axis=1, keepdims=True) * (1.0 / (blocks * LANES))
    factor = lax.rsqrt(mean + 1e-06)
    normed = jnp.concatenate(
        [(parts[j] * factor * gain_ref[j : j + 1, :]).astype(BF16) for j in range(blocks)], axis=1
    )

    product = dot(normed, weight_ref[...])
    units = act_ref.shape[1]
    gate, up = product[:, :units], product[:, units:]
    act_ref[...] = (gate / (1.0 + jnp.exp(-gate)) * up).astype(BF16)
    for k in range(peers):
        start = 0 if split[k] else pl.multiple_of(2 * half * tall, 2 * tall)
        side_ref[k, : 2 * tall, :] = got[k][pl.ds(start, 2 * tall), :]
        side_ref[k, 2 * tall :, :] = got[k][got[k].shape[0] - TAGS :, :]


def down_kernel(
    members,
    rows_each,
    after_ref,
    act_ref,
    act_half_ref,
    act_core_ref,
    act_both_ref,
    down_ref,
    down_pair_ref,
    swap_ref,
    rows_ref,
    mix_ref,
    *send_refs,
):
    del after_ref
    tp = lax.axis_index("tp")
    half, core = tp // 2, tp % 2
    units = act_ref.shape[1]
    blocks = down_ref.shape[1] // LANES
    tall = blocks * rows_each
    spans = [slice(k * rows_each, (k + 1) * rows_each) for k in members]
    swap = jnp.concatenate([swap_ref[span, :] for span in spans], axis=0)
    near = jnp.concatenate([act_ref[...], act_core_ref[...]], axis=0)
    far = jnp.concatenate([act_half_ref[...], act_both_ref[...]], axis=0)
    near, far = dot(swap, near).astype(BF16), dot(swap, far).astype(BF16)
    here = pl.ds(pl.multiple_of(half * units, units), units)
    there = pl.ds(pl.multiple_of((1 - half) * units, units), units)
    for ref, parity in ((down_ref, core), (down_pair_ref, 1 - core)):
        result = dot(near, ref[here, :]) + dot(far, ref[there, :])
        for i, k in enumerate(members):
            mix = mix_ref[spans[i], :]
            for j in range(blocks):
                piece = pl.ds(
                    pl.multiple_of(parity * tall + j * rows_each, rows_each), rows_each
                )
                value = rows_ref[k, piece, :].astype(F32) + result[
                    i * rows_each : (i + 1) * rows_each, j * LANES : (j + 1) * LANES
                ]
                send_refs[i][piece, :] = (mix * value).astype(BF16)


def combine_kernel(order, rows_each, chosen_ref, *refs):
    came = [refs[order.index(k)] for k in range(len(order))]
    keep_ref, give_ref = refs[-2:]
    core = lax.axis_index("tp") % 2
    chosen = chosen_ref[...]
    tall = came[0].shape[0] // 2
    for ref, parity in ((give_ref, 1 - core), (keep_ref, core)):
        for j in range(tall // rows_each):
            start = pl.multiple_of(parity * tall + j * rows_each, rows_each)
            rows = jnp.concatenate([block[pl.ds(start, rows_each), :] for block in came], axis=0)
            ref[:, j * LANES : (j + 1) * LANES] = dot(chosen, rows).astype(ref.dtype)


def shards(
    queries,
    new_keys,
    new_values,
    key_cache,
    value_cache,
    cache_lengths,
    request_order,
    residual,
    out_weight,
    norm_gain,
    route_experts,
    route_weights,
    expert_gate,
    expert_up,
    expert_down,
):
    tp_count = lax.axis_size("tp")
    ep_count = lax.axis_size("ep")
    kv_local = KVHEADS // tp_count

    def swap_core(x):
        return lax.ppermute(x, "tp", [(i, i ^ 1) for i in range(tp_count)])

    def swap_half(x):
        return lax.ppermute(x, "tp", [(i, i ^ 2) for i in range(tp_count)])

    gate, up, down = expert_gate[0].T, expert_up[0].T, expert_down[0]
    tokens, top = route_experts.shape
    capacity = 2 * tokens * top // ep_count
    rows_each = -(-capacity // 16) * 16
    peers = ep_count // 2
    width = residual.shape[1]
    blocks = width // LANES
    tall = blocks * rows_each
    units = 2 * gate.shape[0]
    shape = jax.ShapeDtypeStruct

    begun = pl.pallas_call(
        begin_kernel,
        out_shape=shape((8, LANES), F32),
        out_specs=vmem(),
        compiler_params=params(1),
        cost_estimate=pl.CostEstimate(
            flops=20 * 10**9, bytes_accessed=64 * MIB, transcendentals=0
        ),
        name="begin",
    )()
    context = pl.pallas_call(
        functools.partial(attend_kernel, kv_local),
        out_shape=shape(queries.shape, BF16),
        in_specs=[pl.BlockSpec(memory_space=pl.ANY), pl.BlockSpec(memory_space=pltpu.SMEM)]
        + [vmem()] * 5,
        out_specs=vmem(),
        compiler_params=params(16),
        cost_estimate=pl.CostEstimate(
            flops=2 * 10**8, bytes_accessed=MIB // 2, transcendentals=0
        ),
        name="attend",
    )(begun, cache_lengths, queries, new_keys, new_values, key_cache[0], value_cache[0])
    give = pl.pallas_call(
        give_kernel,
        out_shape=shape((tokens, 2 * width), BF16),
        in_specs=[vmem()] * 2,
        out_specs=vmem(),
        compiler_params=params(16),
        name="project_given",
    )(context, out_weight)
    keep = pl.pallas_call(
        keep_kernel,
        out_shape=shape((tokens, 2 * width), F32),
        in_specs=[pl.BlockSpec(memory_space=pl.ANY)] + [vmem()] * 3,
        out_specs=vmem(),
        compiler_params=params(16),
        cost_estimate=pl.CostEstimate(flops=0, bytes_accessed=2 * MIB, transcendentals=0),
        name="project_kept",
    )(give, context, residual, out_weight)

    summed, send = pl.pallas_call(
        add_core_kernel,
        out_shape=(shape(keep.shape, F32), shape(keep.shape, BF16)),
        in_specs=[vmem()] * 2,
        out_specs=(vmem(), vmem()),
        compiler_params=params(4),
        name="add_core",
    )(keep, swap_core(give))

    part = pl.pallas_call(
        add_half_kernel,
        out_shape=shape(keep.shape, BF16),
        in_specs=[vmem()] * 2,
        out_specs=vmem(),
        compiler_params=params(4),
        name="add_half",
    )(summed, swap_half(send))
    pick, tags = pl.pallas_call(
        functools.partial(route_kernel, peers),
        out_shape=(
            shape((peers * rows_each, tokens), BF16),
            shape((peers, TAGS, LANES), BF16),
        ),
        in_specs=[pl.BlockSpec(memory_space=pl.ANY)] + [vmem()] * 2,
        out_specs=(vmem(), vmem()),
        compiler_params=params(4),
        cost_estimate=pl.CostEstimate(flops=0, bytes_accessed=MIB, transcendentals=0),
        name="route",
    )(part, route_experts.T, route_weights.T)
    other = swap_core(part)

    near = peers // 2
    split = [k >= near and (k - near) % 2 == 1 for k in range(peers)]

    def gather(members, after):
        sent = pl.pallas_call(
            functools.partial(gather_kernel, members, [split[k] for k in members]),
            out_shape=[
                shape(((2 if split[k] else 4) * tall + TAGS, LANES), BF16) for k in members
            ],
            in_specs=[pl.BlockSpec(memory_space=pl.ANY)] + [vmem()] * 4,
            out_specs=[vmem()] * len(members),
            compiler_params=params(8),
            cost_estimate=pl.CostEstimate(
                flops=(20 * 10**9 if members[0] >= near else 0),
                bytes_accessed=MIB,
                transcendentals=0,
            ),
            name="gather_rows",
        )(after, part, other, pick, tags)
        return dict(zip(members, sent))

    def route(k):
        return [
            (e * tp_count + t, (e ^ (2 * step(k, peers) + t % 2)) * tp_count + t)
            for e in range(ep_count)
            for t in range(tp_count)
        ]

    send = gather(list(reversed(range(near, peers))), tags)
    gate, up, tags = lax.optimization_barrier((gate, up, tags))
    gate_pair, up_pair = swap_core(gate), swap_core(up)
    send.update(gather(list(range(near)), gate_pair))
    got = [lax.ppermute(send[k], ("ep", "tp"), route(k)) for k in range(peers)]
    halves = [swap_half(got[k]) for k in range(peers) if split[k]]

    weights = pl.pallas_call(
        stage_kernel,
        out_shape=shape((gate.shape[1], 2 * units), BF16),
        in_specs=[vmem()] + [hbm()] * 4,
        out_specs=vmem(),
        scratch_shapes=[
            pltpu.VMEM((4,) + gate.shape, BF16),
            pltpu.SemaphoreType.DMA((4,)),
        ],
        compiler_params=params(32),
        cost_estimate=pl.CostEstimate(
            flops=0, bytes_accessed=16 * gate.size, transcendentals=0
        ),
        name="stage",
    )(tags, gate, up, gate_pair, up_pair)

    down, weights = lax.optimization_barrier((down, weights))
    down_pair = swap_core(down)
    arrival = [*range(near, peers), *range(near)]
    act, side = pl.pallas_call(
        functools.partial(hidden_units_kernel, arrival, split, rows_each),
        out_shape=(
            shape((peers * rows_each, units), BF16),
            shape((peers, 2 * tall + TAGS, LANES), BF16),
        ),
        in_specs=[vmem()] * (2 + peers + len(halves)),
        out_specs=(vmem(), vmem()),
        compiler_params=params(16),
        cost_estimate=pl.CostEstimate(
            flops=20 * 10**9, bytes_accessed=MIB, transcendentals=0
        ),
        name="hidden_units",
    )(norm_gain.reshape(-1, LANES), weights, *[got[k] for k in arrival], *halves)

    act_half = swap_half(act)
    act_core = swap_core(act)
    side_core = swap_core(side)
    act_both = swap_core(act_half)

    chosen, swap, rows, mixes = pl.pallas_call(
        functools.partial(select_kernel, top),
        out_shape=(
            shape((tokens, peers * rows_each), BF16),
            shape((peers * rows_each, 2 * peers * rows_each), BF16),
            shape((peers, 2 * tall, LANES), BF16),
            shape((peers * rows_each, LANES), F32),
        ),
        in_specs=[pl.BlockSpec(memory_space=pltpu.SMEM)] + [vmem()] * 2,
        out_specs=(vmem(),) * 4,
        scratch_shapes=[pltpu.SMEM(request_order.shape, jnp.int32)],
        compiler_params=params(8),
        cost_estimate=pl.CostEstimate(flops=0, bytes_accessed=MIB, transcendentals=0),
        name="select",
    )(request_order, side, side_core)

    def results(members, after):
        sent = pl.pallas_call(
            functools.partial(down_kernel, members, rows_each),
            out_shape=[shape((2 * tall, LANES), BF16)] * len(members),
            in_specs=[pl.BlockSpec(memory_space=pl.ANY)] + [vmem()] * 9,
            out_specs=[vmem()] * len(members),
            compiler_params=params(16),
            cost_estimate=pl.CostEstimate(
                flops=(20 * 10**9 if members[0] >= near else 0),
                bytes_accessed=MIB,
                transcendentals=0,
            ),
            name="down",
        )(
            after,
            act,
            act_half,
            act_core,
            act_both,
            down,
            down_pair,
            swap,
            rows,
            mixes,
        )
        return dict(zip(members, sent))

    order = [*range(near, peers), *range(near)]
    send = results(list(range(peers)), chosen)
    came = [lax.ppermute(send[k], ("ep", "tp"), route(k)) for k in order]

    keep, give = pl.pallas_call(
        functools.partial(combine_kernel, order, rows_each),
        out_shape=(shape((tokens, width), F32), shape((tokens, width), BF16)),
        in_specs=[vmem()] * (1 + peers),
        out_specs=(vmem(), vmem()),
        compiler_params=params(8),
        name="combine",
    )(chosen, *came)
    return pl.pallas_call(
        add_half_kernel,
        out_shape=shape((tokens, width), BF16),
        in_specs=[vmem()] * 2,
        out_specs=vmem(),
        compiler_params=params(4),
        name="add_output",
    )(keep, swap_core(give))


def solution(mesh):
    return jax.shard_map(
        shards,
        mesh=mesh,
        in_specs=(
            P("ep", "tp"),
            P("ep", "tp"),
            P("ep", "tp"),
            P("ep", None, "tp"),
            P("ep", None, "tp"),
            P("ep"),
            P(),
            P("ep", "tp"),
            P("tp", None),
            P(),
            P("ep", None),
            P("ep", None),
            P("ep", None, "tp"),
            P("ep", None, "tp"),
            P("ep", None, "tp"),
        ),
        out_specs=P("ep", "tp"),
        check_vma=False,
    )
```

```python
import functools
import math

import jax
import jax.numpy as jnp
from jax import lax
from jax.experimental import pallas as pl
from jax.experimental.pallas import tpu as pltpu
from jax.sharding import PartitionSpec as P

HEAD = 128
QHEADS = 16
KVHEADS = 4
LANES = 128
TAGS = 16
MIB = 1024 * 1024

BF16 = jnp.bfloat16
F32 = jnp.float32


def vmem():
    return pl.BlockSpec(memory_space=pltpu.VMEM)


def hbm():
    return pl.BlockSpec(memory_space=pltpu.HBM)


def params(mib):
    return pltpu.CompilerParams(vmem_limit_bytes=int(mib * MIB))


def dot(a, b):
    return jnp.dot(a, b, preferred_element_type=F32)


def dot_t(a, b):
    return lax.dot_general(a, b, (((1,), (1,)), ((), ())), preferred_element_type=F32)


def begin_kernel(out_ref):
    out_ref[...] = jnp.zeros(out_ref.shape, F32)


def attend_kernel(
    kv_local,
    after_ref,
    length_ref,
    query_ref,
    new_key_ref,
    new_value_ref,
    key_ref,
    value_ref,
    context_ref,
):
    del after_ref
    tokens = query_ref.shape[0]
    group = QHEADS // KVHEADS
    length = length_ref[0]
    scale = 1.0 / math.sqrt(HEAD)
    pieces = []
    for g in range(kv_local):
        columns = slice(g * HEAD, (g + 1) * HEAD)
        rows = jnp.concatenate(
            [
                query_ref[:, (g * group + i) * HEAD : (g * group + i + 1) * HEAD]
                for i in range(group)
            ],
            axis=0,
        )
        old = dot_t(rows, key_ref[:, columns]) * scale
        new = dot_t(rows, new_key_ref[:, columns]) * scale
        position = lax.broadcasted_iota(jnp.int32, old.shape, 1)
        old = jnp.where(position < length, old, -1e30)
        current = lax.broadcasted_iota(jnp.int32, new.shape, 0) % tokens
        position = lax.broadcasted_iota(jnp.int32, new.shape, 1)
        new = jnp.where(position <= current, new, -1e30)
        highest = jnp.maximum(
            jnp.max(old, axis=1, keepdims=True), jnp.max(new, axis=1, keepdims=True)
        )
        old = jnp.exp(old - highest)
        new = jnp.exp(new - highest)
        totals = jnp.sum(old, axis=1, keepdims=True) + jnp.sum(new, axis=1, keepdims=True)
        mixed = dot(old.astype(BF16), value_ref[:, columns]) + dot(
            new.astype(BF16), new_value_ref[:, columns]
        )
        mixed = (mixed / totals).astype(BF16)
        pieces += [mixed[i * tokens : (i + 1) * tokens] for i in range(group)]
    context_ref[...] = jnp.concatenate(pieces, axis=1)


def give_kernel(context_ref, weight_ref, give_ref):
    core = lax.axis_index("tp") % 2
    width = context_ref.shape[1]
    context = context_ref[...]
    for i in range(2):
        start = pl.multiple_of((2 * i + 1 - core) * width, width)
        part = dot(context, weight_ref[:, pl.ds(start, width)])
        give_ref[:, i * width : (i + 1) * width] = part.astype(BF16)


def keep_kernel(after_ref, context_ref, residual_ref, weight_ref, keep_ref):
    del after_ref
    tp = lax.axis_index("tp")
    half, core = tp // 2, tp % 2
    width = context_ref.shape[1]
    context = context_ref[...]
    for i in range(2):
        start = pl.multiple_of((2 * i + core) * width, width)
        part = dot(context, weight_ref[:, pl.ds(start, width)])
        keep_ref[:, i * width : (i + 1) * width] = part + jnp.where(
            half == i, residual_ref[...].astype(F32), 0.0
        )


def step(k, peers):
    near = peers // 2
    if isinstance(k, int):
        return near - 1 - k if k < near else k
    return jnp.where(k < near, near - 1 - k, k)


def peer_numbers(peers, tokens):
    number = lax.broadcasted_iota(jnp.int32, (peers, tokens), 0)
    near = peers // 2
    steps = jnp.where(number < near, near - 1 - number, number)
    return jnp.bitwise_xor(2 * steps + lax.axis_index("tp") % 2, lax.axis_index("ep"))


def earlier_tokens(tokens):
    earlier = lax.broadcasted_iota(jnp.int32, (tokens, tokens), 0) < lax.broadcasted_iota(
        jnp.int32, (tokens, tokens), 1
    )
    return jnp.where(earlier, 1.0, 0.0).astype(BF16)


def slot_numbers(named, tokens):
    rank = dot(named.astype(BF16), earlier_tokens(tokens))
    return jnp.where(named > 0.0, rank, -1.0)


def route_kernel(peers, after_ref, expert_ref, weight_ref, pick_ref, tags_ref):
    del after_ref
    top, tokens = expert_ref.shape
    rows_each = pick_ref.shape[0] // peers
    peer = peer_numbers(peers, tokens)
    weights = weight_ref[...]
    mixing = (weights / jnp.sum(weights, axis=0, keepdims=True)).astype(BF16).astype(F32)
    mix_of = jnp.zeros((peers, tokens), F32)
    named = jnp.zeros((peers, tokens), F32)
    for j in range(top):
        match = expert_ref[j : j + 1, :] == peer
        mix_of = mix_of + jnp.where(match, mixing[j : j + 1, :], 0.0)
        named = named + jnp.where(match, 1.0, 0.0)
    rank = slot_numbers(named, tokens)
    slot = lax.broadcasted_iota(jnp.int32, (rows_each, tokens), 0).astype(F32)
    line = lax.broadcasted_iota(jnp.int32, (TAGS, tokens), 0)
    names = jnp.zeros((TAGS, tokens), F32)
    for j in range(top):
        names = jnp.where(line == j + 1, expert_ref[j : j + 1, :].astype(F32), names)
    tags_ref[...] = jnp.zeros(tags_ref.shape, BF16)
    for k in range(peers):
        pick = jnp.where(rank[k : k + 1, :] == slot, 1.0, 0.0).astype(BF16)
        pick_ref[k * rows_each : (k + 1) * rows_each, :] = pick
        mix = jnp.where(line == 0, mix_of[k : k + 1, :], 0.0).astype(BF16)
        every = jnp.concatenate([pick, jnp.zeros((tokens - rows_each, tokens), BF16)], axis=0)
        tags_ref[k, :, :tokens] = (names + dot_t(mix, every)).astype(BF16)


def select_kernel(
    top,
    order_ref,
    side_ref,
    side_core_ref,
    chosen_ref,
    swap_ref,
    rows_ref,
    mix_ref,
    inverse_ref,
):
    me = lax.axis_index("ep")
    core = lax.axis_index("tp") % 2
    tokens = chosen_ref.shape[0]
    peers = side_ref.shape[0]
    rows_each = chosen_ref.shape[1] // peers
    names = jnp.zeros((TAGS, LANES), F32)
    for k in range(peers):
        for ref, parity in ((side_ref, core), (side_core_ref, 1 - core)):
            here = order_ref[jnp.bitwise_xor(me, 2 * step(k, peers) + parity)] == me
            tags = ref[k, ref.shape[1] - TAGS :, :].astype(F32)
            names = names + jnp.where(here, tags, 0.0)
    expert = peer_numbers(peers, tokens).astype(F32)
    named = jnp.zeros((peers, tokens), F32)
    for j in range(top):
        named = named + jnp.where(names[j + 1 : j + 2, :tokens] == expert, 1.0, 0.0)
    rank = slot_numbers(named, tokens)
    slot = lax.broadcasted_iota(jnp.int32, (rows_each, tokens), 0).astype(F32)
    pick = jnp.concatenate(
        [jnp.where(rank[k : k + 1, :] == slot, 1.0, 0.0) for k in range(peers)], axis=0
    )
    chosen_ref[...] = pick.T.astype(BF16)

    def place(s, carry):
        inverse_ref[order_ref[s]] = s
        return carry

    lax.fori_loop(0, order_ref.shape[0], place, 0)
    height = rows_ref.shape[1]
    diagonal = lax.broadcasted_iota(jnp.int32, (rows_each, LANES), 0) == lax.broadcasted_iota(
        jnp.int32, (rows_each, LANES), 1
    )
    row = lax.broadcasted_iota(jnp.int32, (rows_each, swap_ref.shape[1]), 0)
    column = lax.broadcasted_iota(jnp.int32, (rows_each, swap_ref.shape[1]), 1)
    for k in range(peers):
        offset = jnp.bitwise_xor(
            inverse_ref[jnp.bitwise_xor(me, 2 * step(k, peers) + core)], me
        )
        index = step(offset // 2, peers)
        mine = offset % 2 == core
        block = jnp.where(mine, side_ref[index], side_core_ref[index])
        rows_ref[k] = block[:height]
        tags = block[height:].astype(F32)[0:1, :]
        mix = jnp.sum(jnp.where(diagonal, tags, 0.0), axis=1, keepdims=True)
        span = slice(k * rows_each, (k + 1) * rows_each)
        mix_ref[span, :] = jnp.broadcast_to(mix, (rows_each, LANES))
        base = (index + jnp.where(mine, 0, peers)) * rows_each
        swap_ref[span, :] = jnp.where(column == base + row, 1.0, 0.0).astype(BF16)


def add_core_kernel(keep_ref, came_ref, sum_ref, send_ref):
    value = keep_ref[...] + came_ref[...].astype(F32)
    sum_ref[...] = value
    send_ref[...] = value.astype(BF16)


def add_half_kernel(sum_ref, came_ref, out_ref):
    out_ref[...] = (sum_ref[...] + came_ref[...].astype(F32)).astype(BF16)


def gather_kernel(members, split, after_ref, part_ref, other_ref, pick_ref, tags_ref, *send_refs):
    del after_ref
    tp = lax.axis_index("tp")
    mine, core = tp // 2, tp % 2
    count = len(members)
    rows_each = pick_ref.shape[0] // tags_ref.shape[0]
    pick = jnp.concatenate(
        [pick_ref[k * rows_each : (k + 1) * rows_each, :] for k in members], axis=0
    )
    width = part_ref.shape[1] // 2
    blocks = width // LANES
    tall = blocks * rows_each

    def put(ref, rows, base):
        for j in range(blocks):
            start = pl.multiple_of(base + j * rows_each, rows_each)
            ref[pl.ds(start, rows_each), :] = rows[:, j * LANES : (j + 1) * LANES]

    for source, parity in ((part_ref, core), (other_ref, 1 - core)):
        whole = [k for k in range(count) if not split[k]]
        for half in range(2) if whole else ():
            rows = dot(pick, source[:, half * width : (half + 1) * width]).astype(BF16)
            for k in whole:
                piece = rows[k * rows_each : (k + 1) * rows_each]
                put(send_refs[k], piece, (2 * half + parity) * tall)
        for k in range(count):
            if split[k]:
                columns = pl.ds(pl.multiple_of(mine * width, width), width)
                piece = pick[k * rows_each : (k + 1) * rows_each]
                put(send_refs[k], dot(piece, source[:, columns]).astype(BF16), parity * tall)
    for k in range(count):
        send_refs[k][send_refs[k].shape[0] - TAGS :, :] = tags_ref[members[k]]


def stage_kernel(after_ref, gate, up, gate_pair, up_pair, out_ref, held_ref, sems):
    del after_ref
    core = lax.axis_index("tp") % 2
    copies = [
        pltpu.make_async_copy(source, held_ref.at[place], sems.at[i])
        for i, (source, place) in enumerate(
            ((gate, core), (up, 2 + core), (gate_pair, 1 - core), (up_pair, 3 - core))
        )
    ]
    for copy in copies:
        copy.start()
    for copy in copies:
        copy.wait()
    units, width = held_ref.shape[1:]
    for j in range(width // LANES):
        columns = slice(j * LANES, (j + 1) * LANES)
        out_ref[columns, :] = held_ref[:, :, columns].reshape(4 * units, LANES).T


def hidden_units_kernel(order, split, rows_each, gain_ref, weight_ref, *refs):
    peers = len(split)
    got = [refs[order.index(k)] for k in range(peers)]
    halves = list(refs[peers:-2])
    act_ref, side_ref = refs[-2:]
    tp = lax.axis_index("tp")
    half, core = tp // 2, tp % 2
    blocks = gain_ref.shape[0]
    tall = blocks // 4 * rows_each

    columns = []
    for ref, parted in zip(got, split):
        if parted:
            own, came = ref[: 2 * tall, :], halves.pop(0)[: 2 * tall, :]
            low = jnp.where(half == 0, own, came)
            high = jnp.where(half == 0, came, own)
            rows = jnp.concatenate([low, high], axis=0)
        else:
            rows = ref[: 4 * tall, :]
        columns.append([rows[j * rows_each : (j + 1) * rows_each] for j in range(blocks)])
    parts = [
        jnp.concatenate([column[j] for column in columns], axis=0).astype(F32)
        for j in range(blocks)
    ]
    squares = parts[0] * parts[0]
    for part in parts[1:]:
        squares = squares + part * part
    mean = jnp.sum(squares, axis=1, keepdims=True) * (1.0 / (blocks * LANES))
    factor = lax.rsqrt(mean + 1e-06)
    normed = jnp.concatenate(
        [(parts[j] * factor * gain_ref[j : j + 1, :]).astype(BF16) for j in range(blocks)], axis=1
    )

    product = dot(normed, weight_ref[...])
    units = act_ref.shape[1]
    gate, up = product[:, :units], product[:, units:]
    act_ref[...] = (gate / (1.0 + jnp.exp(-gate)) * up).astype(BF16)
    for k in range(peers):
        start = 0 if split[k] else pl.multiple_of(2 * half * tall, 2 * tall)
        side_ref[k, : 2 * tall, :] = got[k][pl.ds(start, 2 * tall), :]
        side_ref[k, 2 * tall :, :] = got[k][got[k].shape[0] - TAGS :, :]


def down_kernel(
    members,
    rows_each,
    after_ref,
    act_ref,
    act_half_ref,
    act_core_ref,
    act_both_ref,
    down_ref,
    down_pair_ref,
    swap_ref,
    rows_ref,
    mix_ref,
    *send_refs,
):
    del after_ref
    tp = lax.axis_index("tp")
    half, core = tp // 2, tp % 2
    units = act_ref.shape[1]
    blocks = down_ref.shape[1] // LANES
    tall = blocks * rows_each
    spans = [slice(k * rows_each, (k + 1) * rows_each) for k in members]
    swap = jnp.concatenate([swap_ref[span, :] for span in spans], axis=0)
    near = jnp.concatenate([act_ref[...], act_core_ref[...]], axis=0)
    far = jnp.concatenate([act_half_ref[...], act_both_ref[...]], axis=0)
    near, far = dot(swap, near).astype(BF16), dot(swap, far).astype(BF16)
    here = pl.ds(pl.multiple_of(half * units, units), units)
    there = pl.ds(pl.multiple_of((1 - half) * units, units), units)
    for ref, parity in ((down_ref, core), (down_pair_ref, 1 - core)):
        result = dot(near, ref[here, :]) + dot(far, ref[there, :])
        for i, k in enumerate(members):
            mix = mix_ref[spans[i], :]
            for j in range(blocks):
                piece = pl.ds(
                    pl.multiple_of(parity * tall + j * rows_each, rows_each), rows_each
                )
                value = rows_ref[k, piece, :].astype(F32) + result[
                    i * rows_each : (i + 1) * rows_each, j * LANES : (j + 1) * LANES
                ]
                send_refs[i][piece, :] = (mix * value).astype(BF16)


def combine_kernel(order, rows_each, chosen_ref, *refs):
    came = [refs[order.index(k)] for k in range(len(order))]
    own_ref = refs[len(order)]
    nearest = len(order) // 2 - 1
    keep_ref, give_ref = refs[-2:]
    core = lax.axis_index("tp") % 2
    chosen = chosen_ref[...]
    tall = came[0].shape[0] // 2
    for ref, parity in ((give_ref, 1 - core), (keep_ref, core)):
        for j in range(tall // rows_each):
            start = pl.multiple_of(parity * tall + j * rows_each, rows_each)
            pieces = [block[pl.ds(start, rows_each), :] for block in came]
            own = own_ref[pl.ds(start, rows_each), :]
            pieces[nearest] = jnp.where(core == 0, own, pieces[nearest])
            rows = jnp.concatenate(pieces, axis=0)
            ref[:, j * LANES : (j + 1) * LANES] = dot(chosen, rows).astype(ref.dtype)


def shards(
    queries,
    new_keys,
    new_values,
    key_cache,
    value_cache,
    cache_lengths,
    request_order,
    residual,
    out_weight,
    norm_gain,
    route_experts,
    route_weights,
    expert_gate,
    expert_up,
    expert_down,
):
    tp_count = lax.axis_size("tp")
    ep_count = lax.axis_size("ep")
    kv_local = KVHEADS // tp_count

    def swap_core(x):
        return lax.ppermute(x, "tp", [(i, i ^ 1) for i in range(tp_count)])

    def swap_half(x):
        return lax.ppermute(x, "tp", [(i, i ^ 2) for i in range(tp_count)])

    gate, up, down = expert_gate[0].T, expert_up[0].T, expert_down[0]
    tokens, top = route_experts.shape
    capacity = 2 * tokens * top // ep_count
    rows_each = -(-capacity // 16) * 16
    peers = ep_count // 2
    width = residual.shape[1]
    blocks = width // LANES
    tall = blocks * rows_each
    units = 2 * gate.shape[0]
    shape = jax.ShapeDtypeStruct

    begun = pl.pallas_call(
        begin_kernel,
        out_shape=shape((8, LANES), F32),
        out_specs=vmem(),
        compiler_params=params(1),
        cost_estimate=pl.CostEstimate(
            flops=20 * 10**9, bytes_accessed=64 * MIB, transcendentals=0
        ),
        name="begin",
    )()
    context = pl.pallas_call(
        functools.partial(attend_kernel, kv_local),
        out_shape=shape(queries.shape, BF16),
        in_specs=[pl.BlockSpec(memory_space=pl.ANY), pl.BlockSpec(memory_space=pltpu.SMEM)]
        + [vmem()] * 5,
        out_specs=vmem(),
        compiler_params=params(16),
        cost_estimate=pl.CostEstimate(
            flops=2 * 10**8, bytes_accessed=MIB // 2, transcendentals=0
        ),
        name="attend",
    )(begun, cache_lengths, queries, new_keys, new_values, key_cache[0], value_cache[0])
    give = pl.pallas_call(
        give_kernel,
        out_shape=shape((tokens, 2 * width), BF16),
        in_specs=[vmem()] * 2,
        out_specs=vmem(),
        compiler_params=params(16),
        name="project_given",
    )(context, out_weight)
    keep = pl.pallas_call(
        keep_kernel,
        out_shape=shape((tokens, 2 * width), F32),
        in_specs=[pl.BlockSpec(memory_space=pl.ANY)] + [vmem()] * 3,
        out_specs=vmem(),
        compiler_params=params(16),
        cost_estimate=pl.CostEstimate(flops=0, bytes_accessed=2 * MIB, transcendentals=0),
        name="project_kept",
    )(give, context, residual, out_weight)

    summed, send = pl.pallas_call(
        add_core_kernel,
        out_shape=(shape(keep.shape, F32), shape(keep.shape, BF16)),
        in_specs=[vmem()] * 2,
        out_specs=(vmem(), vmem()),
        compiler_params=params(4),
        name="add_core",
    )(keep, swap_core(give))

    part = pl.pallas_call(
        add_half_kernel,
        out_shape=shape(keep.shape, BF16),
        in_specs=[vmem()] * 2,
        out_specs=vmem(),
        compiler_params=params(4),
        name="add_half",
    )(summed, swap_half(send))
    pick, tags = pl.pallas_call(
        functools.partial(route_kernel, peers),
        out_shape=(
            shape((peers * rows_each, tokens), BF16),
            shape((peers, TAGS, LANES), BF16),
        ),
        in_specs=[pl.BlockSpec(memory_space=pl.ANY)] + [vmem()] * 2,
        out_specs=(vmem(), vmem()),
        compiler_params=params(4),
        cost_estimate=pl.CostEstimate(flops=0, bytes_accessed=MIB, transcendentals=0),
        name="route",
    )(part, route_experts.T, route_weights.T)
    other = swap_core(part)

    near = peers // 2
    split = [k >= near and (k - near) % 2 == 1 for k in range(peers)]

    def gather(members, after):
        sent = pl.pallas_call(
            functools.partial(gather_kernel, members, [split[k] for k in members]),
            out_shape=[
                shape(((2 if split[k] else 4) * tall + TAGS, LANES), BF16) for k in members
            ],
            in_specs=[pl.BlockSpec(memory_space=pl.ANY)] + [vmem()] * 4,
            out_specs=[vmem()] * len(members),
            compiler_params=params(8),
            cost_estimate=pl.CostEstimate(
                flops=(20 * 10**9 if members[0] >= near else 0),
                bytes_accessed=MIB,
                transcendentals=0,
            ),
            name="gather_rows",
        )(after, part, other, pick, tags)
        return dict(zip(members, sent))

    def route(k, own=True):
        return [
            (e * tp_count + t, (e ^ (2 * step(k, peers) + t % 2)) * tp_count + t)
            for e in range(ep_count)
            for t in range(tp_count)
            if own or step(k, peers) or t % 2
        ]

    send = gather(list(reversed(range(near, peers))), tags)
    gate, up, tags = lax.optimization_barrier((gate, up, tags))
    gate_pair, up_pair = swap_core(gate), swap_core(up)
    send.update(gather(list(range(near)), gate_pair))
    got = [lax.ppermute(send[k], ("ep", "tp"), route(k)) for k in range(peers)]
    halves = [swap_half(got[k]) for k in range(peers) if split[k]]

    weights = pl.pallas_call(
        stage_kernel,
        out_shape=shape((gate.shape[1], 2 * units), BF16),
        in_specs=[vmem()] + [hbm()] * 4,
        out_specs=vmem(),
        scratch_shapes=[
            pltpu.VMEM((4,) + gate.shape, BF16),
            pltpu.SemaphoreType.DMA((4,)),
        ],
        compiler_params=params(32),
        cost_estimate=pl.CostEstimate(
            flops=0, bytes_accessed=16 * gate.size, transcendentals=0
        ),
        name="stage",
    )(tags, gate, up, gate_pair, up_pair)

    down, weights = lax.optimization_barrier((down, weights))
    down_pair = swap_core(down)
    arrival = [*range(near, peers), *range(near)]
    act, side = pl.pallas_call(
        functools.partial(hidden_units_kernel, arrival, split, rows_each),
        out_shape=(
            shape((peers * rows_each, units), BF16),
            shape((peers, 2 * tall + TAGS, LANES), BF16),
        ),
        in_specs=[vmem()] * (2 + peers + len(halves)),
        out_specs=(vmem(), vmem()),
        compiler_params=params(16),
        cost_estimate=pl.CostEstimate(
            flops=20 * 10**9, bytes_accessed=MIB, transcendentals=0
        ),
        name="hidden_units",
    )(norm_gain.reshape(-1, LANES), weights, *[got[k] for k in arrival], *halves)

    act_half = swap_half(act)
    act_core = swap_core(act)
    side_core = swap_core(side)
    act_both = swap_core(act_half)

    chosen, swap, rows, mixes = pl.pallas_call(
        functools.partial(select_kernel, top),
        out_shape=(
            shape((tokens, peers * rows_each), BF16),
            shape((peers * rows_each, 2 * peers * rows_each), BF16),
            shape((peers, 2 * tall, LANES), BF16),
            shape((peers * rows_each, LANES), F32),
        ),
        in_specs=[pl.BlockSpec(memory_space=pltpu.SMEM)] + [vmem()] * 2,
        out_specs=(vmem(),) * 4,
        scratch_shapes=[pltpu.SMEM(request_order.shape, jnp.int32)],
        compiler_params=params(8),
        cost_estimate=pl.CostEstimate(flops=10 * 10**9, bytes_accessed=MIB, transcendentals=0),
        name="select",
    )(request_order, side, side_core)

    def results(members, after):
        sent = pl.pallas_call(
            functools.partial(down_kernel, members, rows_each),
            out_shape=[shape((2 * tall, LANES), BF16)] * len(members),
            in_specs=[pl.BlockSpec(memory_space=pl.ANY)] + [vmem()] * 9,
            out_specs=[vmem()] * len(members),
            compiler_params=params(16),
            cost_estimate=pl.CostEstimate(
                flops=(20 * 10**9 if members[0] >= near else 0),
                bytes_accessed=MIB,
                transcendentals=0,
            ),
            name="down",
        )(
            after,
            act,
            act_half,
            act_core,
            act_both,
            down,
            down_pair,
            swap,
            rows,
            mixes,
        )
        return dict(zip(members, sent))

    order = [*range(near, peers), *range(near)]
    send = results(list(range(peers)), chosen)
    came = [lax.ppermute(send[k], ("ep", "tp"), route(k, False)) for k in order]

    keep, give = pl.pallas_call(
        functools.partial(combine_kernel, order, rows_each),
        out_shape=(shape((tokens, width), F32), shape((tokens, width), BF16)),
        in_specs=[vmem()] * (2 + peers),
        out_specs=(vmem(), vmem()),
        compiler_params=params(8),
        name="combine",
    )(chosen, *came, send[near - 1])
    return pl.pallas_call(
        add_half_kernel,
        out_shape=shape((tokens, width), BF16),
        in_specs=[vmem()] * 2,
        out_specs=vmem(),
        compiler_params=params(4),
        name="add_output",
    )(keep, swap_core(give))


def solution(mesh):
    return jax.shard_map(
        shards,
        mesh=mesh,
        in_specs=(
            P("ep", "tp"),
            P("ep", "tp"),
            P("ep", "tp"),
            P("ep", None, "tp"),
            P("ep", None, "tp"),
            P("ep"),
            P(),
            P("ep", "tp"),
            P("tp", None),
            P(),
            P("ep", None),
            P("ep", None),
            P("ep", None, "tp"),
            P("ep", None, "tp"),
            P("ep", None, "tp"),
        ),
        out_specs=P("ep", "tp"),
        check_vma=False,
    )
```

```python
import functools
import math

import jax
import jax.numpy as jnp
from jax import lax
from jax.experimental import pallas as pl
from jax.experimental.pallas import tpu as pltpu
from jax.sharding import PartitionSpec as P

HEAD = 128
QHEADS = 16
KVHEADS = 4
LANES = 128
TAGS = 16
MIB = 1024 * 1024

BF16 = jnp.bfloat16
F32 = jnp.float32


def vmem():
    return pl.BlockSpec(memory_space=pltpu.VMEM)


def hbm():
    return pl.BlockSpec(memory_space=pltpu.HBM)


def params(mib):
    return pltpu.CompilerParams(vmem_limit_bytes=int(mib * MIB))


def dot(a, b):
    return jnp.dot(a, b, preferred_element_type=F32)


def dot_t(a, b):
    return lax.dot_general(a, b, (((1,), (1,)), ((), ())), preferred_element_type=F32)


def begin_kernel(out_ref):
    out_ref[...] = jnp.zeros(out_ref.shape, F32)


def attend_kernel(
    kv_local,
    after_ref,
    length_ref,
    query_ref,
    new_key_ref,
    new_value_ref,
    key_ref,
    value_ref,
    context_ref,
):
    del after_ref
    tokens = query_ref.shape[0]
    group = QHEADS // KVHEADS
    length = length_ref[0]
    scale = 1.0 / math.sqrt(HEAD)
    pieces = []
    for g in range(kv_local):
        columns = slice(g * HEAD, (g + 1) * HEAD)
        rows = jnp.concatenate(
            [
                query_ref[:, (g * group + i) * HEAD : (g * group + i + 1) * HEAD]
                for i in range(group)
            ],
            axis=0,
        )
        old = dot_t(rows, key_ref[:, columns]) * scale
        new = dot_t(rows, new_key_ref[:, columns]) * scale
        position = lax.broadcasted_iota(jnp.int32, old.shape, 1)
        old = jnp.where(position < length, old, -1e30)
        current = lax.broadcasted_iota(jnp.int32, new.shape, 0) % tokens
        position = lax.broadcasted_iota(jnp.int32, new.shape, 1)
        new = jnp.where(position <= current, new, -1e30)
        highest = jnp.maximum(
            jnp.max(old, axis=1, keepdims=True), jnp.max(new, axis=1, keepdims=True)
        )
        old = jnp.exp(old - highest)
        new = jnp.exp(new - highest)
        totals = jnp.sum(old, axis=1, keepdims=True) + jnp.sum(new, axis=1, keepdims=True)
        mixed = dot(old.astype(BF16), value_ref[:, columns]) + dot(
            new.astype(BF16), new_value_ref[:, columns]
        )
        mixed = (mixed / totals).astype(BF16)
        pieces += [mixed[i * tokens : (i + 1) * tokens] for i in range(group)]
    context_ref[...] = jnp.concatenate(pieces, axis=1)


def give_kernel(context_ref, weight_ref, give_ref):
    core = lax.axis_index("tp") % 2
    width = context_ref.shape[1]
    context = context_ref[...]
    for i in range(2):
        start = pl.multiple_of((2 * i + 1 - core) * width, width)
        part = dot(context, weight_ref[:, pl.ds(start, width)])
        give_ref[:, i * width : (i + 1) * width] = part.astype(BF16)


def keep_kernel(after_ref, context_ref, residual_ref, weight_ref, keep_ref):
    del after_ref
    tp = lax.axis_index("tp")
    half, core = tp // 2, tp % 2
    width = context_ref.shape[1]
    context = context_ref[...]
    for i in range(2):
        start = pl.multiple_of((2 * i + core) * width, width)
        part = dot(context, weight_ref[:, pl.ds(start, width)])
        keep_ref[:, i * width : (i + 1) * width] = part + jnp.where(
            half == i, residual_ref[...].astype(F32), 0.0
        )


def step(k, peers):
    near = peers // 2
    if isinstance(k, int):
        return near - 1 - k if k < near else k
    return jnp.where(k < near, near - 1 - k, k)


def peer_numbers(peers, tokens):
    number = lax.broadcasted_iota(jnp.int32, (peers, tokens), 0)
    near = peers // 2
    steps = jnp.where(number < near, near - 1 - number, number)
    return jnp.bitwise_xor(2 * steps + lax.axis_index("tp") % 2, lax.axis_index("ep"))


def earlier_tokens(tokens):
    earlier = lax.broadcasted_iota(jnp.int32, (tokens, tokens), 0) < lax.broadcasted_iota(
        jnp.int32, (tokens, tokens), 1
    )
    return jnp.where(earlier, 1.0, 0.0).astype(BF16)


def slot_numbers(named, tokens):
    rank = dot(named.astype(BF16), earlier_tokens(tokens))
    return jnp.where(named > 0.0, rank, -1.0)


def route_kernel(peers, after_ref, expert_ref, weight_ref, pick_ref, tags_ref):
    del after_ref
    top, tokens = expert_ref.shape
    rows_each = pick_ref.shape[0] // peers
    peer = peer_numbers(peers, tokens)
    weights = weight_ref[...]
    mixing = (weights / jnp.sum(weights, axis=0, keepdims=True)).astype(BF16).astype(F32)
    mix_of = jnp.zeros((peers, tokens), F32)
    named = jnp.zeros((peers, tokens), F32)
    for j in range(top):
        match = expert_ref[j : j + 1, :] == peer
        mix_of = mix_of + jnp.where(match, mixing[j : j + 1, :], 0.0)
        named = named + jnp.where(match, 1.0, 0.0)
    rank = slot_numbers(named, tokens)
    slot = lax.broadcasted_iota(jnp.int32, (rows_each, tokens), 0).astype(F32)
    line = lax.broadcasted_iota(jnp.int32, (TAGS, tokens), 0)
    names = jnp.zeros((TAGS, tokens), F32)
    for j in range(top):
        names = jnp.where(line == j + 1, expert_ref[j : j + 1, :].astype(F32), names)
    tags_ref[...] = jnp.zeros(tags_ref.shape, BF16)
    for k in range(peers):
        pick = jnp.where(rank[k : k + 1, :] == slot, 1.0, 0.0).astype(BF16)
        pick_ref[k * rows_each : (k + 1) * rows_each, :] = pick
        mix = jnp.where(line == 0, mix_of[k : k + 1, :], 0.0).astype(BF16)
        every = jnp.concatenate([pick, jnp.zeros((tokens - rows_each, tokens), BF16)], axis=0)
        tags_ref[k, :, :tokens] = (names + dot_t(mix, every)).astype(BF16)


def select_kernel(
    top,
    order_ref,
    side_ref,
    side_core_ref,
    chosen_ref,
    swap_ref,
    rows_ref,
    mix_ref,
    inverse_ref,
):
    me = lax.axis_index("ep")
    core = lax.axis_index("tp") % 2
    tokens = chosen_ref.shape[0]
    peers = side_ref.shape[0]
    rows_each = chosen_ref.shape[1] // peers
    names = jnp.zeros((TAGS, LANES), F32)
    for k in range(peers):
        for ref, parity in ((side_ref, core), (side_core_ref, 1 - core)):
            here = order_ref[jnp.bitwise_xor(me, 2 * step(k, peers) + parity)] == me
            tags = ref[k, ref.shape[1] - TAGS :, :].astype(F32)
            names = names + jnp.where(here, tags, 0.0)
    expert = peer_numbers(peers, tokens).astype(F32)
    named = jnp.zeros((peers, tokens), F32)
    for j in range(top):
        named = named + jnp.where(names[j + 1 : j + 2, :tokens] == expert, 1.0, 0.0)
    rank = slot_numbers(named, tokens)
    slot = lax.broadcasted_iota(jnp.int32, (rows_each, tokens), 0).astype(F32)
    pick = jnp.concatenate(
        [jnp.where(rank[k : k + 1, :] == slot, 1.0, 0.0) for k in range(peers)], axis=0
    )
    chosen_ref[...] = pick.T.astype(BF16)

    def place(s, carry):
        inverse_ref[order_ref[s]] = s
        return carry

    lax.fori_loop(0, order_ref.shape[0], place, 0)
    height = rows_ref.shape[1]
    diagonal = lax.broadcasted_iota(jnp.int32, (rows_each, LANES), 0) == lax.broadcasted_iota(
        jnp.int32, (rows_each, LANES), 1
    )
    row = lax.broadcasted_iota(jnp.int32, (rows_each, swap_ref.shape[1]), 0)
    column = lax.broadcasted_iota(jnp.int32, (rows_each, swap_ref.shape[1]), 1)
    for k in range(peers):
        offset = jnp.bitwise_xor(
            inverse_ref[jnp.bitwise_xor(me, 2 * step(k, peers) + core)], me
        )
        index = step(offset // 2, peers)
        mine = offset % 2 == core
        block = jnp.where(mine, side_ref[index], side_core_ref[index])
        rows_ref[k] = block[:height]
        tags = block[height:].astype(F32)[0:1, :]
        mix = jnp.sum(jnp.where(diagonal, tags, 0.0), axis=1, keepdims=True)
        span = slice(k * rows_each, (k + 1) * rows_each)
        mix_ref[span, :] = jnp.broadcast_to(mix, (rows_each, LANES))
        base = (index + jnp.where(mine, 0, peers)) * rows_each
        swap_ref[span, :] = jnp.where(column == base + row, 1.0, 0.0).astype(BF16)


def add_core_kernel(keep_ref, came_ref, sum_ref, send_ref):
    value = keep_ref[...] + came_ref[...].astype(F32)
    sum_ref[...] = value
    send_ref[...] = value.astype(BF16)


def add_half_kernel(sum_ref, came_ref, out_ref):
    out_ref[...] = (sum_ref[...] + came_ref[...].astype(F32)).astype(BF16)


def gather_kernel(members, split, after_ref, part_ref, other_ref, pick_ref, tags_ref, *send_refs):
    del after_ref
    tp = lax.axis_index("tp")
    mine, core = tp // 2, tp % 2
    count = len(members)
    rows_each = pick_ref.shape[0] // tags_ref.shape[0]
    pick = jnp.concatenate(
        [pick_ref[k * rows_each : (k + 1) * rows_each, :] for k in members], axis=0
    )
    width = part_ref.shape[1] // 2
    blocks = width // LANES
    tall = blocks * rows_each

    def put(ref, rows, base):
        for j in range(blocks):
            start = pl.multiple_of(base + j * rows_each, rows_each)
            ref[pl.ds(start, rows_each), :] = rows[:, j * LANES : (j + 1) * LANES]

    for source, parity in ((part_ref, core), (other_ref, 1 - core)):
        whole = [k for k in range(count) if not split[k]]
        for half in range(2) if whole else ():
            rows = dot(pick, source[:, half * width : (half + 1) * width]).astype(BF16)
            for k in whole:
                piece = rows[k * rows_each : (k + 1) * rows_each]
                put(send_refs[k], piece, (2 * half + parity) * tall)
        for k in range(count):
            if split[k]:
                columns = pl.ds(pl.multiple_of(mine * width, width), width)
                piece = pick[k * rows_each : (k + 1) * rows_each]
                put(send_refs[k], dot(piece, source[:, columns]).astype(BF16), parity * tall)
    for k in range(count):
        send_refs[k][send_refs[k].shape[0] - TAGS :, :] = tags_ref[members[k]]


def stage_kernel(after_ref, gate, up, gate_pair, up_pair, out_ref, held_ref, sems):
    del after_ref
    core = lax.axis_index("tp") % 2
    copies = [
        pltpu.make_async_copy(source, held_ref.at[place], sems.at[i])
        for i, (source, place) in enumerate(
            ((gate, core), (up, 2 + core), (gate_pair, 1 - core), (up_pair, 3 - core))
        )
    ]
    for copy in copies:
        copy.start()
    for copy in copies:
        copy.wait()
    units, width = held_ref.shape[1:]
    for j in range(width // LANES):
        columns = slice(j * LANES, (j + 1) * LANES)
        out_ref[columns, :] = held_ref[:, :, columns].reshape(4 * units, LANES).T


def hidden_units_kernel(order, split, rows_each, gain_ref, weight_ref, *refs):
    peers = len(split)
    got = [refs[order.index(k)] for k in range(peers)]
    halves, own_ref = list(refs[peers:-3]), refs[-3]
    nearest = peers // 2 - 1
    act_ref, side_ref = refs[-2:]
    tp = lax.axis_index("tp")
    half, core = tp // 2, tp % 2
    blocks = gain_ref.shape[0]
    tall = blocks // 4 * rows_each

    columns = []
    for ref, parted in zip(got, split):
        if parted:
            own, came = ref[: 2 * tall, :], halves.pop(0)[: 2 * tall, :]
            low = jnp.where(half == 0, own, came)
            high = jnp.where(half == 0, came, own)
            rows = jnp.concatenate([low, high], axis=0)
        else:
            rows = ref[: 4 * tall, :]
            if ref is got[nearest]:
                rows = jnp.where(core == 0, own_ref[: 4 * tall, :], rows)
        columns.append([rows[j * rows_each : (j + 1) * rows_each] for j in range(blocks)])
    parts = [
        jnp.concatenate([column[j] for column in columns], axis=0).astype(F32)
        for j in range(blocks)
    ]
    squares = parts[0] * parts[0]
    for part in parts[1:]:
        squares = squares + part * part
    mean = jnp.sum(squares, axis=1, keepdims=True) * (1.0 / (blocks * LANES))
    factor = lax.rsqrt(mean + 1e-06)
    normed = jnp.concatenate(
        [(parts[j] * factor * gain_ref[j : j + 1, :]).astype(BF16) for j in range(blocks)], axis=1
    )

    product = dot(normed, weight_ref[...])
    units = act_ref.shape[1]
    gate, up = product[:, :units], product[:, units:]
    act_ref[...] = (gate / (1.0 + jnp.exp(-gate)) * up).astype(BF16)
    for k in range(peers):
        start = 0 if split[k] else pl.multiple_of(2 * half * tall, 2 * tall)
        rows = got[k][pl.ds(start, 2 * tall), :]
        tags = got[k][got[k].shape[0] - TAGS :, :]
        if k == nearest:
            rows = jnp.where(core == 0, own_ref[pl.ds(start, 2 * tall), :], rows)
            tags = jnp.where(core == 0, own_ref[4 * tall :, :], tags)
        side_ref[k, : 2 * tall, :] = rows
        side_ref[k, 2 * tall :, :] = tags


def down_kernel(
    members,
    rows_each,
    after_ref,
    act_ref,
    act_half_ref,
    act_core_ref,
    act_both_ref,
    down_ref,
    down_pair_ref,
    swap_ref,
    rows_ref,
    mix_ref,
    *send_refs,
):
    del after_ref
    tp = lax.axis_index("tp")
    half, core = tp // 2, tp % 2
    units = act_ref.shape[1]
    blocks = down_ref.shape[1] // LANES
    tall = blocks * rows_each
    spans = [slice(k * rows_each, (k + 1) * rows_each) for k in members]
    swap = jnp.concatenate([swap_ref[span, :] for span in spans], axis=0)
    near = jnp.concatenate([act_ref[...], act_core_ref[...]], axis=0)
    far = jnp.concatenate([act_half_ref[...], act_both_ref[...]], axis=0)
    near, far = dot(swap, near).astype(BF16), dot(swap, far).astype(BF16)
    here = pl.ds(pl.multiple_of(half * units, units), units)
    there = pl.ds(pl.multiple_of((1 - half) * units, units), units)
    for ref, parity in ((down_ref, core), (down_pair_ref, 1 - core)):
        result = dot(near, ref[here, :]) + dot(far, ref[there, :])
        for i, k in enumerate(members):
            mix = mix_ref[spans[i], :]
            for j in range(blocks):
                piece = pl.ds(
                    pl.multiple_of(parity * tall + j * rows_each, rows_each), rows_each
                )
                value = rows_ref[k, piece, :].astype(F32) + result[
                    i * rows_each : (i + 1) * rows_each, j * LANES : (j + 1) * LANES
                ]
                send_refs[i][piece, :] = (mix * value).astype(BF16)


def combine_kernel(order, rows_each, chosen_ref, *refs):
    came = [refs[order.index(k)] for k in range(len(order))]
    own_ref = refs[len(order)]
    nearest = len(order) // 2 - 1
    keep_ref, give_ref = refs[-2:]
    core = lax.axis_index("tp") % 2
    chosen = chosen_ref[...]
    tall = came[0].shape[0] // 2
    for ref, parity in ((give_ref, 1 - core), (keep_ref, core)):
        for j in range(tall // rows_each):
            start = pl.multiple_of(parity * tall + j * rows_each, rows_each)
            pieces = [block[pl.ds(start, rows_each), :] for block in came]
            own = own_ref[pl.ds(start, rows_each), :]
            pieces[nearest] = jnp.where(core == 0, own, pieces[nearest])
            rows = jnp.concatenate(pieces, axis=0)
            ref[:, j * LANES : (j + 1) * LANES] = dot(chosen, rows).astype(ref.dtype)


def shards(
    queries,
    new_keys,
    new_values,
    key_cache,
    value_cache,
    cache_lengths,
    request_order,
    residual,
    out_weight,
    norm_gain,
    route_experts,
    route_weights,
    expert_gate,
    expert_up,
    expert_down,
):
    tp_count = lax.axis_size("tp")
    ep_count = lax.axis_size("ep")
    kv_local = KVHEADS // tp_count

    def swap_core(x):
        return lax.ppermute(x, "tp", [(i, i ^ 1) for i in range(tp_count)])

    def swap_half(x):
        return lax.ppermute(x, "tp", [(i, i ^ 2) for i in range(tp_count)])

    gate, up, down = expert_gate[0].T, expert_up[0].T, expert_down[0]
    tokens, top = route_experts.shape
    capacity = 2 * tokens * top // ep_count
    rows_each = -(-capacity // 16) * 16
    peers = ep_count // 2
    width = residual.shape[1]
    blocks = width // LANES
    tall = blocks * rows_each
    units = 2 * gate.shape[0]
    shape = jax.ShapeDtypeStruct

    begun = pl.pallas_call(
        begin_kernel,
        out_shape=shape((8, LANES), F32),
        out_specs=vmem(),
        compiler_params=params(1),
        cost_estimate=pl.CostEstimate(
            flops=20 * 10**9, bytes_accessed=64 * MIB, transcendentals=0
        ),
        name="begin",
    )()
    context = pl.pallas_call(
        functools.partial(attend_kernel, kv_local),
        out_shape=shape(queries.shape, BF16),
        in_specs=[pl.BlockSpec(memory_space=pl.ANY), pl.BlockSpec(memory_space=pltpu.SMEM)]
        + [vmem()] * 5,
        out_specs=vmem(),
        compiler_params=params(16),
        cost_estimate=pl.CostEstimate(
            flops=2 * 10**8, bytes_accessed=MIB // 2, transcendentals=0
        ),
        name="attend",
    )(begun, cache_lengths, queries, new_keys, new_values, key_cache[0], value_cache[0])
    give = pl.pallas_call(
        give_kernel,
        out_shape=shape((tokens, 2 * width), BF16),
        in_specs=[vmem()] * 2,
        out_specs=vmem(),
        compiler_params=params(16),
        name="project_given",
    )(context, out_weight)
    keep = pl.pallas_call(
        keep_kernel,
        out_shape=shape((tokens, 2 * width), F32),
        in_specs=[pl.BlockSpec(memory_space=pl.ANY)] + [vmem()] * 3,
        out_specs=vmem(),
        compiler_params=params(16),
        cost_estimate=pl.CostEstimate(flops=0, bytes_accessed=2 * MIB, transcendentals=0),
        name="project_kept",
    )(give, context, residual, out_weight)

    summed, send = pl.pallas_call(
        add_core_kernel,
        out_shape=(shape(keep.shape, F32), shape(keep.shape, BF16)),
        in_specs=[vmem()] * 2,
        out_specs=(vmem(), vmem()),
        compiler_params=params(4),
        name="add_core",
    )(keep, swap_core(give))

    part = pl.pallas_call(
        add_half_kernel,
        out_shape=shape(keep.shape, BF16),
        in_specs=[vmem()] * 2,
        out_specs=vmem(),
        compiler_params=params(4),
        name="add_half",
    )(summed, swap_half(send))
    pick, tags = pl.pallas_call(
        functools.partial(route_kernel, peers),
        out_shape=(
            shape((peers * rows_each, tokens), BF16),
            shape((peers, TAGS, LANES), BF16),
        ),
        in_specs=[pl.BlockSpec(memory_space=pl.ANY)] + [vmem()] * 2,
        out_specs=(vmem(), vmem()),
        compiler_params=params(4),
        cost_estimate=pl.CostEstimate(flops=0, bytes_accessed=MIB, transcendentals=0),
        name="route",
    )(part, route_experts.T, route_weights.T)
    other = swap_core(part)

    near = peers // 2
    split = [k >= near and (k - near) % 2 == 1 for k in range(peers)]

    def gather(members, after):
        sent = pl.pallas_call(
            functools.partial(gather_kernel, members, [split[k] for k in members]),
            out_shape=[
                shape(((2 if split[k] else 4) * tall + TAGS, LANES), BF16) for k in members
            ],
            in_specs=[pl.BlockSpec(memory_space=pl.ANY)] + [vmem()] * 4,
            out_specs=[vmem()] * len(members),
            compiler_params=params(8),
            cost_estimate=pl.CostEstimate(
                flops=(20 * 10**9 if members[0] >= near else 0),
                bytes_accessed=MIB,
                transcendentals=0,
            ),
            name="gather_rows",
        )(after, part, other, pick, tags)
        return dict(zip(members, sent))

    def route(k, own=True):
        return [
            (e * tp_count + t, (e ^ (2 * step(k, peers) + t % 2)) * tp_count + t)
            for e in range(ep_count)
            for t in range(tp_count)
            if own or step(k, peers) or t % 2
        ]

    send = gather(list(reversed(range(near, peers))), tags)
    gate, up, tags = lax.optimization_barrier((gate, up, tags))
    gate_pair, up_pair = swap_core(gate), swap_core(up)
    send.update(gather(list(range(near)), gate_pair))
    got = [lax.ppermute(send[k], ("ep", "tp"), route(k, False)) for k in range(peers)]
    halves = [swap_half(got[k]) for k in range(peers) if split[k]]

    weights = pl.pallas_call(
        stage_kernel,
        out_shape=shape((gate.shape[1], 2 * units), BF16),
        in_specs=[vmem()] + [hbm()] * 4,
        out_specs=vmem(),
        scratch_shapes=[
            pltpu.VMEM((4,) + gate.shape, BF16),
            pltpu.SemaphoreType.DMA((4,)),
        ],
        compiler_params=params(32),
        cost_estimate=pl.CostEstimate(
            flops=0, bytes_accessed=16 * gate.size, transcendentals=0
        ),
        name="stage",
    )(tags, gate, up, gate_pair, up_pair)

    down, weights = lax.optimization_barrier((down, weights))
    down_pair = swap_core(down)
    arrival = [*range(near, peers), *range(near)]
    act, side = pl.pallas_call(
        functools.partial(hidden_units_kernel, arrival, split, rows_each),
        out_shape=(
            shape((peers * rows_each, units), BF16),
            shape((peers, 2 * tall + TAGS, LANES), BF16),
        ),
        in_specs=[vmem()] * (3 + peers + len(halves)),
        out_specs=(vmem(), vmem()),
        compiler_params=params(16),
        cost_estimate=pl.CostEstimate(
            flops=20 * 10**9, bytes_accessed=MIB, transcendentals=0
        ),
        name="hidden_units",
    )(norm_gain.reshape(-1, LANES), weights, *[got[k] for k in arrival], *halves, send[near - 1])

    act_half = swap_half(act)
    act_core = swap_core(act)
    side_core = swap_core(side)
    act_both = swap_core(act_half)

    chosen, swap, rows, mixes = pl.pallas_call(
        functools.partial(select_kernel, top),
        out_shape=(
            shape((tokens, peers * rows_each), BF16),
            shape((peers * rows_each, 2 * peers * rows_each), BF16),
            shape((peers, 2 * tall, LANES), BF16),
            shape((peers * rows_each, LANES), F32),
        ),
        in_specs=[pl.BlockSpec(memory_space=pltpu.SMEM)] + [vmem()] * 2,
        out_specs=(vmem(),) * 4,
        scratch_shapes=[pltpu.SMEM(request_order.shape, jnp.int32)],
        compiler_params=params(8),
        cost_estimate=pl.CostEstimate(flops=10 * 10**9, bytes_accessed=MIB, transcendentals=0),
        name="select",
    )(request_order, side, side_core)

    def results(members, after):
        sent = pl.pallas_call(
            functools.partial(down_kernel, members, rows_each),
            out_shape=[shape((2 * tall, LANES), BF16)] * len(members),
            in_specs=[pl.BlockSpec(memory_space=pl.ANY)] + [vmem()] * 9,
            out_specs=[vmem()] * len(members),
            compiler_params=params(16),
            cost_estimate=pl.CostEstimate(
                flops=(20 * 10**9 if members[0] >= near else 0),
                bytes_accessed=MIB,
                transcendentals=0,
            ),
            name="down",
        )(
            after,
            act,
            act_half,
            act_core,
            act_both,
            down,
            down_pair,
            swap,
            rows,
            mixes,
        )
        return dict(zip(members, sent))

    order = [*range(near, peers), *range(near)]
    send = results(list(range(peers)), chosen)
    came = [lax.ppermute(send[k], ("ep", "tp"), route(k, False)) for k in order]

    keep, give = pl.pallas_call(
        functools.partial(combine_kernel, order, rows_each),
        out_shape=(shape((tokens, width), F32), shape((tokens, width), BF16)),
        in_specs=[vmem()] * (2 + peers),
        out_specs=(vmem(), vmem()),
        compiler_params=params(8),
        name="combine",
    )(chosen, *came, send[near - 1])
    return pl.pallas_call(
        add_half_kernel,
        out_shape=shape((tokens, width), BF16),
        in_specs=[vmem()] * 2,
        out_specs=vmem(),
        compiler_params=params(4),
        name="add_output",
    )(keep, swap_core(give))


def solution(mesh):
    return jax.shard_map(
        shards,
        mesh=mesh,
        in_specs=(
            P("ep", "tp"),
            P("ep", "tp"),
            P("ep", "tp"),
            P("ep", None, "tp"),
            P("ep", None, "tp"),
            P("ep"),
            P(),
            P("ep", "tp"),
            P("tp", None),
            P(),
            P("ep", None),
            P("ep", None),
            P("ep", None, "tp"),
            P("ep", None, "tp"),
            P("ep", None, "tp"),
        ),
        out_specs=P("ep", "tp"),
        check_vma=False,
    )
```
